256 devices in a mesh: segment: 2 (over core), row: 4 (over x), col: 32 (over y, z).
Axes of the slice: x: 4, y: 4, z: 8, core: 2. Of those that a mesh axis runs over, the one named last changes fastest.
Arguments:
- images: bfloat16 [6, 32, 4096, 512], P(None, 'row', 'col'), may hold values from -6 to 6
- tissue_list: int32 [6, 64], replicated, may hold values from 0 to 63, as said below
- tissue_count: int32 [6], replicated, may hold values from 1 to 64
- w_reduce: bfloat16 [2, 512, 128], P('segment'), may hold values from -0.25 to 0.25
- w_spatial: bfloat16 [2, 3, 3, 128, 128], P('segment'), may hold values from -0.1875 to 0.1875
- w_expand: bfloat16 [2, 128, 512], P('segment'), may hold values from -0.5 to 0.5
- inner_gain: bfloat16 [2, 2, 128], P('segment'), may hold values from 0.25 to 1.75
- inner_bias: bfloat16 [2, 2, 128], P('segment'), may hold values from -3 to 3
- outer_gain: bfloat16 [2, 512], P('segment'), may hold values from 0.25 to 1.75
- outer_bias: bfloat16 [2, 512], P('segment'), may hold values from -3 to 3
Outputs:
- features: bfloat16 [6, 32, 4096, 512], P('segment', 'row', 'col')
The draws below stay inside these ranges and needn't reach their ends.
Inputs may be any that keep to these rules, and one draw needn't show every extreme that they name: `tissue_list`: the first tissue_count[m] entries of row m are distinct tile indices in ascending order; the entries after them are arbitrary tile indices.
All inputs are finite; a program needn't handle non-finite values.
Results may differ from the reference program's by a relative error of at most 0.0065.
Values may be sent and summed in bfloat16 or wider, within the bound.
A program may use at most 64 MiB of HBM per device.

```python
import jax
import jax.numpy as jnp
from jax import lax

C = 512
CI = 128
TW = 64
SLIDES = 6
ROWS = 32
TILES = 64
COLS = 4096


def tissue_tables(key):
    kl, ks, kd, kf = jax.random.split(key, 4)
    idx = jnp.arange(TILES, dtype=jnp.int32)[None, :]
    slide = jnp.arange(SLIDES, dtype=jnp.int32)[:, None]
    length = jax.random.randint(kl, (SLIDES,), TILES // 4, TILES + 1)
    length = jnp.where(jnp.arange(SLIDES) == 0, TILES, length)
    start = jax.random.randint(ks, (SLIDES,), 0, TILES - length + 1)
    inside = (idx >= start[:, None]) & (idx < (start + length)[:, None])
    dropped = jax.random.randint(kd, (SLIDES, TILES), 0, 4) == 0
    keep = inside & (~dropped | (idx == start[:, None]))
    keep = keep | (slide == 0)
    count = jnp.sum(keep.astype(jnp.int32), axis=1).astype(jnp.int32)
    order = jnp.argsort(jnp.where(keep, idx, TILES + idx), axis=1, stable=True).astype(jnp.int32)
    filler = jax.random.randint(kf, (SLIDES, TILES), 0, TILES)
    listed = jnp.where(idx < count[:, None], order, filler).astype(jnp.int32)
    return (listed, count)


def draw_tissue_list(key, part):
    listed, count = tissue_tables(jax.random.fold_in(key, 7))
    return listed


def draw_tissue_count(key, part):
    listed, count = tissue_tables(jax.random.fold_in(key, 7))
    return count


def steps_of(stream_key, shape, cuts, least, high):
    def one(axis_at, blocks):
        heights = jax.random.uniform(jax.random.fold_in(jax.random.fold_in(stream_key, 6), axis_at), (blocks,), jnp.float32, least / len(cuts), high / len(cuts))
        return jnp.repeat(jnp.exp(heights), shape[axis_at] // blocks).reshape((-1,) + (1,) * (len(shape) - axis_at - 1))

    level = one(*cuts[0])
    for cut in cuts[1:]:
        level = level * one(*cut)
    return level


def gaussian(rng, dims, deviation, reach, pieces=(), kind=jnp.bfloat16):
    array = jax.random.normal(rng, dims, jnp.float32) * deviation
    if len(pieces) > 0:
        array = steps_of(rng, dims, pieces, -0.22, 0.18) * array
    return jnp.clip(array, min=-reach, max=reach).astype(kind)


def setup_inputs(seed: int = 0) -> dict:
    splits = jax.random.split(jax.random.key(seed), 11)
    return {
        "images": gaussian(splits[0], (SLIDES, ROWS, COLS, C), 1.0, 6.0, ((1, 4), (2, 32))),
        "tissue_list": draw_tissue_list(jax.random.fold_in(splits[10], 71), 0),
        "tissue_count": draw_tissue_count(jax.random.fold_in(splits[10], 71), 0),
        "w_reduce": gaussian(splits[3], (2, C, CI), C ** -0.5, 0.25, ((0, 2),)),
        "w_spatial": gaussian(splits[4], (2, 3, 3, CI, CI), (9 * CI) ** -0.5, 0.1875, ((0, 2),)),
        "w_expand": gaussian(splits[5], (2, CI, C), CI ** -0.5, 0.5, ((0, 2),)),
        "inner_gain": jnp.clip(1.0 + 0.15 * jax.random.normal(splits[6], (2, 2, CI), jnp.float32), 0.25, 1.75).astype(jnp.bfloat16),
        "inner_bias": gaussian(splits[7], (2, 2, CI), 0.5, 3.0, ((0, 2),)),
        "outer_gain": jnp.clip(1.0 + 0.15 * jax.random.normal(splits[8], (2, C), jnp.float32), 0.25, 1.75).astype(jnp.bfloat16),
        "outer_bias": gaussian(splits[9], (2, C), 0.5, 3.0, ((0, 2),)),
    }


def run_block(x, mask_cols, wr, ws, we, ig, ib, og, ob):
    rows, cols, chans = x.shape
    inner = wr.shape[1]
    v = jnp.dot(x.reshape(-1, chans), wr, preferred_element_type=jnp.float32)
    v = jax.nn.relu(v * ig[0].astype(jnp.float32) + ib[0].astype(jnp.float32))
    reduced = (v.reshape(rows, cols, inner) * mask_cols[None, :, None]).astype(jnp.bfloat16)
    padded = jnp.pad(reduced, ((1, 1), (1, 1), (0, 0)))
    total = jnp.zeros((rows * cols, inner), jnp.float32)
    for dy in range(3):
        for dx in range(3):
            window = padded[dy:dy + rows, dx:dx + cols].reshape(-1, inner)
            total = total + jnp.dot(window, ws[dy, dx], preferred_element_type=jnp.float32)
    spatial = jax.nn.relu(total * ig[1].astype(jnp.float32) + ib[1].astype(jnp.float32)).astype(jnp.bfloat16)
    z = jnp.dot(spatial, we, preferred_element_type=jnp.float32)
    z = z * og.astype(jnp.float32) + ob.astype(jnp.float32) + x.reshape(-1, chans).astype(jnp.float32)
    z = jax.nn.relu(z).reshape(rows, cols, chans) * mask_cols[None, :, None]
    return z.astype(jnp.bfloat16)


def reference(images, tissue_list, tissue_count, w_reduce, w_spatial, w_expand, inner_gain, inner_bias, outer_gain, outer_bias):
    tiles = jnp.arange(TILES, dtype=jnp.int32)

    def one_slide(packed):
        image, listed, count = packed
        valid = tiles < count
        hit = (listed[:, None] == tiles[None, :]) & valid[:, None]
        tissue = jnp.any(hit, axis=0).astype(jnp.float32)
        mask_cols = jnp.repeat(tissue, TW)
        h = image
        for b in range(2):
            h = run_block(h, mask_cols, w_reduce[b], w_spatial[b], w_expand[b], inner_gain[b], inner_bias[b], outer_gain[b], outer_bias[b])
        return h

    return lax.map(one_slide, (images, tissue_list, tissue_count))
```

```python
import functools

import jax
import jax.numpy as jnp
from jax import lax
from jax.experimental import pallas as pl
from jax.experimental.pallas import tpu as pltpu
from jax.sharding import PartitionSpec as P

MESH = pl.DeviceIdType.MESH
TW = 64
F32 = jnp.float32
BF16 = jnp.bfloat16


def widen(row, times):
    return jnp.concatenate([row] * times, axis=1)


def blocks_kernel(
    grid,
    images,
    tissue_list,
    tissue_count,
    w_reduce,
    w_spatial,
    w_expand,
    inner_gain,
    inner_bias,
    outer_gain,
    outer_bias,
    h_out,
    spat_out,
    we_out,
    epi_out,
    img,
    wr,
    ws,
    wa,
    wb,
    we,
    gb,
    mk,
    rb,
    row_send,
    row_recv,
    edge_send,
    edge_recv,
    img_sem,
    w_sem,
    w_send_sem,
    w_recv_sem,
    row_send_sem,
    row_recv_sem,
    edge_send_sem,
    edge_recv_sem,
):
    n_row, n_col = grid
    slides, pairs, _, cols, chans = img.shape
    inner = wr.shape[2]
    last = cols - 1
    seg = lax.axis_index("segment")
    row = lax.axis_index("row")
    col = lax.axis_index("col")
    peer = {"segment": 1 - seg}
    up = lax.rem(row + n_row - 1, n_row)
    down = lax.rem(row + 1, n_row)
    left = lax.rem(col + n_col - 1, n_col)
    right = lax.rem(col + 1, n_col)
    beside = [
        {"row": r, "col": c} for c in (left, right) for r in (row, up, down)
    ]

    barrier = pltpu.get_barrier_semaphore()
    for other in [peer, {"row": up}, {"row": down}] + beside:
        pl.semaphore_signal(barrier, inc=1, device_id=other, device_id_type=MESH)

    loads = []
    for s in range(slides):
        load = pltpu.make_async_copy(
            images.at[seg * slides + s], img.at[s], img_sem.at[s]
        )
        if s == 0:
            load.start()
        loads.append(load)
    own = [
        pltpu.make_async_copy(w_reduce.at[0], wr.at[seg], w_sem.at[0]),
        pltpu.make_async_copy(w_spatial.at[0], ws.at[seg], w_sem.at[1]),
        pltpu.make_async_copy(w_expand.at[0], we.at[seg], w_sem.at[2]),
    ]
    for load in own:
        load.start()
    for load in loads[1:]:
        load.start()

    lines = [inner_gain[0].astype(F32), inner_bias[0].astype(F32)]
    for whole in (outer_gain[...].astype(F32), outer_bias[...].astype(F32)):
        lines += [whole[:, i * inner : (i + 1) * inner] for i in range(chans // inner)]
    lines.append(jnp.zeros((4, inner), F32))
    gb[seg] = jnp.concatenate(lines, axis=0)

    position = lax.broadcasted_iota(jnp.int32, (1, tissue_list.shape[1]), 1)
    for s in range(slides):
        slide = seg * slides + s
        listed = tissue_list[pl.ds(slide, 1), :]
        for t in range(cols // TW):
            tile = col * (cols // TW) + t
            hit = (listed == tile) & (position < tissue_count[slide])
            one = jnp.max(jnp.where(hit, 1.0, 0.0), axis=1, keepdims=True)
            mk[s, t] = jnp.broadcast_to(one, mk.shape[2:])

    pl.semaphore_wait(barrier, 9)

    def swap(src, dst, i):
        return pltpu.make_async_remote_copy(
            src_ref=src,
            dst_ref=dst.at[seg],
            send_sem=w_send_sem.at[i],
            recv_sem=w_recv_sem.at[i],
            device_id=peer,
            device_id_type=MESH,
        )

    swaps = [
        swap(w_reduce.at[0], wr, 0),
        swap(gb.at[seg], gb, 1),
        swap(w_spatial.at[0], ws, 2),
        swap(w_expand.at[0], we, 3),
    ]
    for copy in swaps:
        copy.start()

    def row_copies(e, s):
        for way, there in ((0, up), (1, down)):
            yield pltpu.make_async_remote_copy(
                src_ref=row_send.at[e, s, way],
                dst_ref=row_recv.at[e, s, 1 - way],
                send_sem=row_send_sem.at[e, s, way],
                recv_sem=row_recv_sem.at[e, s, 1 - way],
                device_id={"row": there},
                device_id_type=MESH,
            )

    def edge_copies(e, s):
        for i, there in enumerate(beside):
            side = i // 3
            slot = (1 - side) * 3 + (0, 2, 1)[i % 3]
            yield pltpu.make_async_remote_copy(
                src_ref=edge_send.at[e, s, side],
                dst_ref=edge_recv.at[e, s, slot],
                send_sem=edge_send_sem.at[e, s, i],
                recv_sem=edge_recv_sem.at[e, s, slot],
                device_id=there,
                device_id_type=MESH,
            )

    def store_shifted(e, s, half, red):
        place = rb.at[e, s, pl.ds(half, pairs), :, pl.ds((1 - half) * 3 * inner, 3 * inner)]
        place[...] = jnp.concatenate(
            [
                pltpu.roll(red, 1, 1).astype(BF16),
                red.astype(BF16),
                pltpu.roll(red, last, 1).astype(BF16),
            ],
            axis=2,
        )

    def reduce_half(e, s, half, x):
        v = jnp.dot(
            x.reshape(pairs * cols, chans), wr[e], preferred_element_type=F32
        ).reshape(pairs, cols // TW, TW, inner)
        mask = mk[s][:, 0:1]
        gain = (gb[e, 0:1] * mask)[None]
        bias = (gb[e, 2:3] * mask)[None]
        red = jnp.maximum(v * gain + bias, 0.0).reshape(pairs, cols, inner)
        if half == 0:
            row_send[e, s, 0] = red[0].astype(BF16)
        else:
            row_send[e, s, 1] = red[pairs - 1].astype(BF16)
        edge_send[e, s, 0, pl.ds(half * pairs, pairs)] = red[:, 0]
        edge_send[e, s, 1, pl.ds(half * pairs, pairs)] = red[:, last]
        return red

    def send(e, s):
        for copy in row_copies(e, s):
            copy.start()
        for copy in edge_copies(e, s):
            copy.start()

    def halo(e, s):
        for copy in row_copies(e, s):
            copy.wait_recv()
        for copy in edge_copies(e, s):
            copy.wait_recv()
        above, below = row > 0, row < n_row - 1
        at_left, at_right = col > 0, col < n_col - 1
        place = lax.broadcasted_iota(jnp.int32, (cols, inner), 0)
        spot = lax.broadcasted_iota(jnp.int32, (16, inner), 0)
        zero = jnp.zeros((1, inner), F32)

        def beyond(side, slot, line, there):
            pixel = edge_recv[e, s, 3 * side + slot, line : line + 1]
            return jnp.where(there & (at_right if side else at_left), pixel, zero)

        for way, there, slot, line, q, lane in (
            (0, above, 1, 2 * pairs - 1, 0, 0),
            (1, below, 2, 0, pairs, 3 * inner),
        ):
            got = jnp.where(there, row_recv[e, s, way].astype(F32), 0.0)
            before = jnp.where(place == 0, beyond(0, slot, line, there), pltpu.roll(got, 1, 0))
            after = jnp.where(place == last, beyond(1, slot, line, there), pltpu.roll(got, last, 0))
            rb[e, s, q, :, lane : lane + 3 * inner] = jnp.concatenate(
                [before.astype(BF16), got.astype(BF16), after.astype(BF16)], axis=1
            )
        for half in range(2):
            for p in range(pairs):
                line, lane = half * pairs + p, (1 - half) * 3 * inner
                here = rb.at[e, s, p + half, 0:16, lane : lane + inner]
                here[...] = jnp.where(
                    spot == 0, beyond(0, 0, line, True), here[...].astype(F32)
                ).astype(BF16)
                here = rb.at[e, s, p + half, cols - 16 : cols, lane + 2 * inner : lane + 3 * inner]
                here[...] = jnp.where(
                    spot == 15, beyond(1, 0, line, True), here[...].astype(F32)
                ).astype(BF16)

    def spatial(e, s):
        total = jnp.dot(
            rb[e, s, 0:pairs].reshape(pairs * cols, 6 * inner), wa[e], preferred_element_type=F32
        ) + jnp.dot(
            rb[e, s, 1 : pairs + 1].reshape(pairs * cols, 6 * inner),
            wb[e],
            preferred_element_type=F32,
        )
        gain, bias = widen(gb[e, 1:2], 2), widen(gb[e, 3:4], 2)
        return jnp.maximum(total * gain + bias, 0.0).astype(BF16)

    def spread(b):
        depth = 3 * inner
        zero = jnp.zeros((depth, inner), BF16)
        w = [ws[b, dy].reshape(depth, inner) for dy in range(3)]
        wa[b] = jnp.concatenate(
            [jnp.concatenate([w[0], zero], axis=1), jnp.concatenate([w[1], w[0]], axis=1)], axis=0
        )
        wb[b] = jnp.concatenate(
            [jnp.concatenate([w[2], w[1]], axis=1), jnp.concatenate([zero, w[2]], axis=1)], axis=0
        )

    def outer(b):
        n = chans // inner
        gain = jnp.concatenate([gb[b, 4 + i : 5 + i] for i in range(n)], axis=1)
        bias = jnp.concatenate([gb[b, 4 + n + i : 5 + n + i] for i in range(n)], axis=1)
        return gain, bias

    own[0].wait()
    for copy in swaps[:2]:
        copy.wait()

    def first_reduce(s, carry):
        pltpu.make_async_copy(images.at[seg * slides + s], img.at[s], img_sem.at[s]).wait()
        reds = [reduce_half(0, s, half, img[s, :, half]) for half in range(2)]
        send(0, s)
        for half in range(2):
            store_shifted(0, s, half, reds[half])
        return carry

    lax.fori_loop(0, slides, first_reduce, 0)

    for load in own[1:]:
        load.wait()
    for copy in swaps[2:]:
        copy.wait()
    spread(0)
    spread(1)

    def middle(s, carry):
        halo(0, s)
        sp = spatial(0, s)
        gain, bias = outer(0)
        mask = widen(mk[s][:, 0:1].reshape(cols // TW, inner), chans // inner)[:, None]
        reds = []
        for half in range(2):
            z = jnp.dot(
                sp[:, half * inner : (half + 1) * inner], we[0], preferred_element_type=F32
            ).reshape(pairs, cols, chans)
            z = z * gain + bias + img[s, :, half].astype(F32)
            z = jnp.maximum(z, 0.0).reshape(pairs, cols // TW, TW, chans) * mask[None]
            z = z.astype(BF16).reshape(pairs, cols, chans)
            h_out[s, :, half] = z
            reds.append(reduce_half(1, s, half, z))
        send(1, s)
        for half in range(2):
            store_shifted(1, s, half, reds[half])
        return carry

    lax.fori_loop(0, slides, middle, 0)

    def final(s, carry):
        halo(1, s)
        spat_out[s] = spatial(1, s).reshape(pairs, cols, 2 * inner)
        return carry

    we_out[...] = we[1]
    gain, bias = outer(1)
    for s in range(slides):
        for t in range(cols // TW):
            mask = widen(mk[s, t, 0:1], chans // inner)
            epi_out[s, t : t + 1] = gain * mask
            epi_out[s, 2 + t : 3 + t] = bias * mask
    lax.fori_loop(0, slides, final, 0)

    def drain(s, carry):
        for e in range(2):
            for copy in row_copies(e, s):
                copy.wait_send()
            for copy in edge_copies(e, s):
                copy.wait_send()
        return carry

    lax.fori_loop(0, slides, drain, 0)


def expand_kernel(h, spat, we, epi, out, held, sem):
    slides, pairs, _, cols, chans = h.shape
    inner = we.shape[0]
    tiles = cols // TW

    def one(s, carry):
        for half in range(2):
            z = jnp.dot(
                spat[s].reshape(pairs * cols, 2 * inner)[:, half * inner : (half + 1) * inner],
                we[...],
                preferred_element_type=F32,
            ).reshape(pairs, tiles, TW, chans)
            gain = epi[s, 0:tiles][None, :, None]
            bias = epi[s, 2 : 2 + tiles][None, :, None]
            z = z * gain + bias + h[s, :, half].astype(F32).reshape(pairs, tiles, TW, chans)
            held[s, :, half] = jnp.maximum(z, 0.0).astype(BF16).reshape(pairs, cols, chans)
        pltpu.make_async_copy(held.at[s], out.at[s], sem.at[s]).start()
        return carry

    lax.fori_loop(0, slides, one, 0)
    for s in range(slides):
        pltpu.make_async_copy(held.at[s], out.at[s], sem.at[s]).wait()


def shards(grid, images, tissue_list, tissue_count, *weights):
    total, rows, cols, chans = images.shape
    slides, pairs = total // 2, rows // 2
    inner = weights[0].shape[2]
    w_reduce, w_spatial, w_expand, inner_gain, inner_bias, outer_gain, outer_bias = weights
    w_spatial = w_spatial.reshape(1, 3, 3, inner, inner)
    hbm = pl.BlockSpec(memory_space=pltpu.HBM)
    vmem = pl.BlockSpec(memory_space=pltpu.VMEM)
    smem = pl.BlockSpec(memory_space=pltpu.SMEM)
    dma = pltpu.SemaphoreType.DMA
    h, spat, we, epi = pl.pallas_call(
        functools.partial(blocks_kernel, grid),
        out_shape=(
            pltpu.VMEM((slides, pairs, 2, cols, chans), BF16),
            pltpu.VMEM((slides, pairs, cols, 2 * inner), BF16),
            pltpu.VMEM((inner, chans), BF16),
            pltpu.VMEM((slides, 4, chans), F32),
        ),
        in_specs=[hbm, vmem, smem, hbm, hbm, hbm] + [vmem] * 4,
        out_specs=(vmem,) * 4,
        scratch_shapes=[
            pltpu.VMEM((slides, pairs, 2, cols, chans), BF16),
            pltpu.VMEM((2, chans, inner), BF16),
            pltpu.VMEM((2, 3, 3, inner, inner), BF16),
            pltpu.VMEM((2, 6 * inner, 2 * inner), BF16),
            pltpu.VMEM((2, 6 * inner, 2 * inner), BF16),
            pltpu.VMEM((2, inner, chans), BF16),
            pltpu.VMEM((2, 16, inner), F32),
            pltpu.VMEM((slides, cols // TW, 8, inner), F32),
            pltpu.VMEM((2, slides, pairs + 1, cols, 6 * inner), BF16),
            pltpu.VMEM((2, slides, 2, cols, inner), BF16),
            pltpu.VMEM((2, slides, 2, cols, inner), BF16),
            pltpu.VMEM((2, slides, 2, rows, inner), F32),
            pltpu.VMEM((2, slides, 6, rows, inner), F32),
            dma((slides,)),
            dma((3,)),
            dma((4,)),
            dma((4,)),
            dma((2, slides, 2)),
            dma((2, slides, 2)),
            dma((2, slides, 6)),
            dma((2, slides, 6)),
        ],
        compiler_params=pltpu.CompilerParams(
            collective_id=0, has_side_effects=True, vmem_limit_bytes=40 * 2**20
        ),
        name="blocks",
    )(
        images.reshape(total, pairs, 2, cols, chans),
        tissue_list,
        tissue_count,
        w_reduce,
        w_spatial,
        w_expand,
        inner_gain,
        inner_bias,
        outer_gain,
        outer_bias,
    )
    out = pl.pallas_call(
        expand_kernel,
        out_shape=jax.ShapeDtypeStruct((slides, pairs, 2, cols, chans), BF16),
        in_specs=[vmem] * 4,
        out_specs=hbm,
        scratch_shapes=[
            pltpu.VMEM((slides, pairs, 2, cols, chans), BF16),
            dma((slides,)),
        ],
        compiler_params=pltpu.CompilerParams(vmem_limit_bytes=24 * 2**20),
        name="expand",
    )(h, spat, we, epi)
    return out.reshape(slides, rows, cols, chans)


def solution(mesh):
    placed = (
        P(None, "row", "col", None),
        P(),
        P(),
        P("segment", None, None),
        P("segment", None, None, None, None),
        P("segment", None, None),
        P("segment", None, None),
        P("segment", None, None),
        P("segment", None),
        P("segment", None),
    )
    return jax.shard_map(
        functools.partial(shards, (mesh.shape["row"], mesh.shape["col"])),
        mesh=mesh,
        in_specs=placed,
        out_specs=P("segment", "row", "col", None),
        check_vma=False,
    )
```

```python
import functools

import jax
import jax.numpy as jnp
from jax import lax
from jax.experimental import pallas as pl
from jax.experimental.pallas import tpu as pltpu
from jax.sharding import PartitionSpec as P

MESH = pl.DeviceIdType.MESH
TW = 64
F32 = jnp.float32
BF16 = jnp.bfloat16
remote = pltpu.make_async_remote_copy


def widen(row, times):
    return jnp.concatenate([row] * times, axis=1)


def inside(i, n):
    return (i >= 0) & (i < n)


def blocks_kernel(
    grid,
    images,
    tissue_list,
    tissue_count,
    w_reduce,
    w_spatial,
    w_expand,
    inner_gain,
    inner_bias,
    outer_gain,
    outer_bias,
    h_out,
    spat_out,
    we_out,
    epi_out,
    img,
    listed,
    counts,
    ig,
    ib,
    og,
    ob,
    wr,
    ws,
    wa,
    wb,
    we,
    gb,
    mk,
    rb,
    row_send,
    row_recv,
    edge_send,
    edge_recv,
    img_sem,
    w_sem,
    w_send_sem,
    w_recv_sem,
    send_sem,
    recv_sem,
):
    n_row, n_col = grid
    slides, pairs, _, cols, chans = img.shape
    inner = wr.shape[2]
    last = cols - 1
    seg = lax.axis_index("segment")
    row = lax.axis_index("row")
    col = lax.axis_index("col")
    peer = {"segment": 1 - seg}
    around = [
        (i, j, inside(row + i, n_row) & inside(col + j, n_col))
        for j in (0, -1, 1)
        for i in (-1, 1, 0)
        if i or j
    ]

    def at(i, j):
        return {"row": row + i, "col": col + j}

    barrier = pltpu.get_barrier_semaphore()

    def greet(other):
        pl.semaphore_signal(barrier, inc=1, device_id=other, device_id_type=MESH)

    greet(peer)
    for i, j, there in around:
        pl.when(there)(functools.partial(greet, at(i, j)))

    def image_load(s):
        return pltpu.make_async_copy(images.at[seg * slides + s], img.at[s], img_sem.at[s])

    own = [
        pltpu.make_async_copy(src, dst, w_sem.at[i])
        for i, (src, dst) in enumerate(
            (
                (w_reduce.at[0], wr.at[seg]),
                (w_spatial.at[0], ws.at[seg]),
                (w_expand.at[0], we.at[seg]),
                (inner_gain, ig),
                (inner_bias, ib),
                (outer_gain, og),
                (outer_bias, ob),
                (tissue_count, counts),
                (tissue_list, listed),
            )
        )
    ]
    for load in own[3:] + own[:1]:
        load.start()
    for s in range(slides):
        image_load(s).start()
    for load in own[1:3]:
        load.start()
    for load in own[3:]:
        load.wait()

    lines = [ig[0].astype(F32), ib[0].astype(F32)]
    for whole in (og[...].astype(F32), ob[...].astype(F32)):
        lines += [whole[:, i * inner : (i + 1) * inner] for i in range(chans // inner)]
    lines.append(jnp.zeros((4, inner), F32))
    gb[seg] = jnp.concatenate(lines, axis=0)

    position = lax.broadcasted_iota(jnp.int32, (1, listed.shape[1]), 1)
    for s in range(slides):
        slide = seg * slides + s
        here = listed[pl.ds(slide, 1), :]
        for t in range(cols // TW):
            tile = col * (cols // TW) + t
            hit = (here == tile) & (position < counts[slide])
            one = jnp.max(jnp.where(hit, 1.0, 0.0), axis=1, keepdims=True)
            mk[s, t] = jnp.broadcast_to(one, mk.shape[2:])

    partners = 1
    for _, _, there in around:
        partners = partners + there.astype(jnp.int32)
    pl.semaphore_wait(barrier, partners)

    def swap(src, dst, i):
        return remote(
            src_ref=src,
            dst_ref=dst.at[seg],
            send_sem=w_send_sem.at[i],
            recv_sem=w_recv_sem.at[i],
            device_id=peer,
            device_id_type=MESH,
        )

    swaps = [
        swap(w_reduce.at[0], wr, 0),
        swap(gb.at[seg], gb, 1),
        swap(w_spatial.at[0], ws, 2),
        swap(w_expand.at[0], we, 3),
    ]
    for copy in swaps:
        copy.start()

    def sends(e, s):
        for n, (i, j, there) in enumerate(around):
            if j == 0:
                src, dst = row_send.at[e, s, n], row_recv.at[e, s, 1 - n]
            else:
                src = edge_send.at[e, s, (1 + j) // 2]
                dst = edge_recv.at[e, s, (1 - j) // 2 * 3 + (i + 2 if i == 0 else (1 - i) // 2)]
            yield there, remote(
                src_ref=src,
                dst_ref=dst,
                send_sem=send_sem.at[e, s, n],
                recv_sem=recv_sem.at[e, s, mirror(n)],
                device_id=at(i, j),
                device_id_type=MESH,
            )

    def mirror(n):
        i, j, _ = around[n]
        return [(a, b) for a, b, _ in around].index((-i, -j))

    def store_shifted(e, s, half, red):
        place = rb.at[e, s, pl.ds(half, pairs), :, pl.ds((1 - half) * 3 * inner, 3 * inner)]
        place[...] = jnp.concatenate(
            [
                pltpu.roll(red, 1, 1).astype(BF16),
                red.astype(BF16),
                pltpu.roll(red, last, 1).astype(BF16),
            ],
            axis=2,
        )

    def reduce_half(e, s, half, x):
        v = jnp.dot(
            x.reshape(pairs * cols, chans), wr[e], preferred_element_type=F32
        ).reshape(pairs, cols // TW, TW, inner)
        mask = mk[s][:, 0:1]
        gain = (gb[e, 0:1] * mask)[None]
        bias = (gb[e, 2:3] * mask)[None]
        red = jnp.maximum(v * gain + bias, 0.0).reshape(pairs, cols, inner)
        if half == 0:
            row_send[e, s, 0] = red[0].astype(BF16)
        else:
            row_send[e, s, 1] = red[pairs - 1].astype(BF16)
        edge_send[e, s, 0, pl.ds(half * pairs, pairs)] = red[:, 0]
        edge_send[e, s, 1, pl.ds(half * pairs, pairs)] = red[:, last]
        return red

    def send(e, s):
        for there, copy in sends(e, s):
            pl.when(there)(copy.start)

    def halo(e, s):
        copies = list(sends(e, s))
        for n, (there, _) in enumerate(copies):
            pl.when(there)(copies[mirror(n)][1].wait_recv)
        above, below = row > 0, row < n_row - 1
        at_left, at_right = col > 0, col < n_col - 1
        place = lax.broadcasted_iota(jnp.int32, (cols, inner), 0)
        spot = lax.broadcasted_iota(jnp.int32, (16, inner), 0)
        zero = jnp.zeros((1, inner), F32)

        def beyond(side, slot, line, there):
            pixel = edge_recv[e, s, 3 * side + slot, line : line + 1]
            return jnp.where(there & (at_right if side else at_left), pixel, zero)

        for way, there, slot, line, q, lane in (
            (0, above, 0, 2 * pairs - 1, 0, 0),
            (1, below, 1, 0, pairs, 3 * inner),
        ):
            got = jnp.where(there, row_recv[e, s, way].astype(F32), 0.0)
            before = jnp.where(place == 0, beyond(0, slot, line, there), pltpu.roll(got, 1, 0))
            after = jnp.where(place == last, beyond(1, slot, line, there), pltpu.roll(got, last, 0))
            rb[e, s, q, :, lane : lane + 3 * inner] = jnp.concatenate(
                [before.astype(BF16), got.astype(BF16), after.astype(BF16)], axis=1
            )
        for half in range(2):
            for p in range(pairs):
                line, lane = half * pairs + p, (1 - half) * 3 * inner
                here = rb.at[e, s, p + half, 0:16, lane : lane + inner]
                here[...] = jnp.where(
                    spot == 0, beyond(0, 2, line, True), here[...].astype(F32)
                ).astype(BF16)
                here = rb.at[e, s, p + half, cols - 16 : cols, lane + 2 * inner : lane + 3 * inner]
                here[...] = jnp.where(
                    spot == 15, beyond(1, 2, line, True), here[...].astype(F32)
                ).astype(BF16)

    def spatial(e, s):
        total = jnp.dot(
            rb[e, s, 0:pairs].reshape(pairs * cols, 6 * inner), wa[e], preferred_element_type=F32
        ) + jnp.dot(
            rb[e, s, 1 : pairs + 1].reshape(pairs * cols, 6 * inner),
            wb[e],
            preferred_element_type=F32,
        )
        gain, bias = widen(gb[e, 1:2], 2), widen(gb[e, 3:4], 2)
        return jnp.maximum(total * gain + bias, 0.0).astype(BF16)

    def spread(b):
        depth = 3 * inner
        zero = jnp.zeros((depth, inner), BF16)
        w = [ws[b, dy].reshape(depth, inner) for dy in range(3)]
        wa[b] = jnp.concatenate(
            [jnp.concatenate([w[0], zero], axis=1), jnp.concatenate([w[1], w[0]], axis=1)], axis=0
        )
        wb[b] = jnp.concatenate(
            [jnp.concatenate([w[2], w[1]], axis=1), jnp.concatenate([zero, w[2]], axis=1)], axis=0
        )

    def outer(b):
        n = chans // inner
        gain = jnp.concatenate([gb[b, 4 + i : 5 + i] for i in range(n)], axis=1)
        bias = jnp.concatenate([gb[b, 4 + n + i : 5 + n + i] for i in range(n)], axis=1)
        return gain, bias

    own[0].wait()
    for copy in swaps[:2]:
        copy.wait()

    def first_reduce(s, carry):
        image_load(s).wait()
        reds = [reduce_half(0, s, half, img[s, :, half]) for half in range(2)]
        send(0, s)
        for half in range(2):
            store_shifted(0, s, half, reds[half])
        return carry

    lax.fori_loop(0, slides, first_reduce, 0)

    for load in own[1:3]:
        load.wait()
    for copy in swaps[2:]:
        copy.wait()
    spread(0)
    spread(1)

    def middle(s, carry):
        halo(0, s)
        sp = spatial(0, s)
        gain, bias = outer(0)
        mask = widen(mk[s][:, 0:1].reshape(cols // TW, inner), chans // inner)[:, None]
        reds = []
        for half in range(2):
            z = jnp.dot(
                sp[:, half * inner : (half + 1) * inner], we[0], preferred_element_type=F32
            ).reshape(pairs, cols, chans)
            z = z * gain + bias + img[s, :, half].astype(F32)
            z = jnp.maximum(z, 0.0).reshape(pairs, cols // TW, TW, chans) * mask[None]
            z = z.astype(BF16).reshape(pairs, cols, chans)
            h_out[s, :, half] = z
            reds.append(reduce_half(1, s, half, z))
        send(1, s)
        for half in range(2):
            store_shifted(1, s, half, reds[half])
        return carry

    lax.fori_loop(0, slides, middle, 0)

    def final(s, carry):
        halo(1, s)
        spat_out[s] = spatial(1, s).reshape(pairs, cols, 2 * inner)
        return carry

    we_out[...] = we[1]
    gain, bias = outer(1)
    for s in range(slides):
        for t in range(cols // TW):
            mask = widen(mk[s, t, 0:1], chans // inner)
            epi_out[s, t : t + 1] = gain * mask
            epi_out[s, 2 + t : 3 + t] = bias * mask
    lax.fori_loop(0, slides, final, 0)

    def drain(s, carry):
        for e in range(2):
            for there, copy in sends(e, s):
                pl.when(there)(copy.wait_send)
        return carry

    lax.fori_loop(0, slides, drain, 0)


def expand_kernel(h, spat, we, epi, out, held, sem):
    slides, pairs, _, cols, chans = h.shape
    inner = we.shape[0]
    tiles = cols // TW

    def one(s, carry):
        for half in range(2):
            z = jnp.dot(
                spat[s].reshape(pairs * cols, 2 * inner)[:, half * inner : (half + 1) * inner],
                we[...],
                preferred_element_type=F32,
            ).reshape(pairs, tiles, TW, chans)
            gain = epi[s, 0:tiles][None, :, None]
            bias = epi[s, 2 : 2 + tiles][None, :, None]
            z = z * gain + bias + h[s, :, half].astype(F32).reshape(pairs, tiles, TW, chans)
            held[s, :, half] = jnp.maximum(z, 0.0).astype(BF16).reshape(pairs, cols, chans)
        pltpu.make_async_copy(held.at[s], out.at[s], sem.at[s]).start()
        return carry

    lax.fori_loop(0, slides, one, 0)
    for s in range(slides):
        pltpu.make_async_copy(held.at[s], out.at[s], sem.at[s]).wait()


def shards(grid, images, tissue_list, tissue_count, *weights):
    total, rows, cols, chans = images.shape
    slides, pairs = total // 2, rows // 2
    inner = weights[0].shape[2]
    w_reduce, w_spatial, w_expand, inner_gain, inner_bias, outer_gain, outer_bias = weights
    w_spatial = w_spatial.reshape(1, 3, 3, inner, inner)
    hbm = pl.BlockSpec(memory_space=pltpu.HBM)
    vmem = pl.BlockSpec(memory_space=pltpu.VMEM)
    dma = pltpu.SemaphoreType.DMA
    h, spat, we, epi = pl.pallas_call(
        functools.partial(blocks_kernel, grid),
        out_shape=(
            pltpu.VMEM((slides, pairs, 2, cols, chans), BF16),
            pltpu.VMEM((slides, pairs, cols, 2 * inner), BF16),
            pltpu.VMEM((inner, chans), BF16),
            pltpu.VMEM((slides, 4, chans), F32),
        ),
        in_specs=[hbm] * 10,
        out_specs=(vmem,) * 4,
        scratch_shapes=[
            pltpu.VMEM((slides, pairs, 2, cols, chans), BF16),
            pltpu.VMEM(tissue_list.shape, jnp.int32),
            pltpu.SMEM(tissue_count.shape, jnp.int32),
            pltpu.VMEM(inner_gain.shape, BF16),
            pltpu.VMEM(inner_bias.shape, BF16),
            pltpu.VMEM(outer_gain.shape, BF16),
            pltpu.VMEM(outer_bias.shape, BF16),
            pltpu.VMEM((2, chans, inner), BF16),
            pltpu.VMEM((2, 3, 3, inner, inner), BF16),
            pltpu.VMEM((2, 6 * inner, 2 * inner), BF16),
            pltpu.VMEM((2, 6 * inner, 2 * inner), BF16),
            pltpu.VMEM((2, inner, chans), BF16),
            pltpu.VMEM((2, 16, inner), F32),
            pltpu.VMEM((slides, cols // TW, 8, inner), F32),
            pltpu.VMEM((2, slides, pairs + 1, cols, 6 * inner), BF16),
            pltpu.VMEM((2, slides, 2, cols, inner), BF16),
            pltpu.VMEM((2, slides, 2, cols, inner), BF16),
            pltpu.VMEM((2, slides, 2, rows, inner), F32),
            pltpu.VMEM((2, slides, 6, rows, inner), F32),
            dma((slides,)),
            dma((9,)),
            dma((4,)),
            dma((4,)),
            dma((2, slides, 8)),
            dma((2, slides, 8)),
        ],
        compiler_params=pltpu.CompilerParams(
            collective_id=0, has_side_effects=True, vmem_limit_bytes=40 * 2**20
        ),
        name="blocks",
    )(
        *(
            pltpu.with_memory_space_constraint(x, pltpu.HBM)
            for x in (
                images.reshape(total, pairs, 2, cols, chans),
                tissue_list,
                tissue_count,
                w_reduce,
                w_spatial,
                w_expand,
                inner_gain,
                inner_bias,
                outer_gain,
                outer_bias,
            )
        )
    )
    out = pl.pallas_call(
        expand_kernel,
        out_shape=jax.ShapeDtypeStruct((slides, pairs, 2, cols, chans), BF16),
        in_specs=[vmem] * 4,
        out_specs=hbm,
        scratch_shapes=[
            pltpu.VMEM((slides, pairs, 2, cols, chans), BF16),
            dma((slides,)),
        ],
        compiler_params=pltpu.CompilerParams(vmem_limit_bytes=24 * 2**20),
        name="expand",
    )(h, spat, we, epi)
    return out.reshape(slides, rows, cols, chans)


def solution(mesh):
    placed = (
        P(None, "row", "col", None),
        P(),
        P(),
        P("segment", None, None),
        P("segment", None, None, None, None),
        P("segment", None, None),
        P("segment", None, None),
        P("segment", None, None),
        P("segment", None),
        P("segment", None),
    )
    return jax.shard_map(
        functools.partial(shards, (mesh.shape["row"], mesh.shape["col"])),
        mesh=mesh,
        in_specs=placed,
        out_specs=P("segment", "row", "col", None),
        check_vma=False,
    )
```

```python
import functools

import jax
import jax.numpy as jnp
import ml_dtypes
import numpy as np
from jax import lax
from jax.experimental import pallas as pl
from jax.experimental.pallas import tpu as pltpu
from jax.sharding import PartitionSpec as P

MESH = pl.DeviceIdType.MESH
TW = 64
F32 = jnp.float32
BF16 = jnp.bfloat16
remote = pltpu.make_async_remote_copy


RUN = 8


def selections(rows):
    gather = np.zeros((2, 48, 128), np.float32)
    window = np.zeros((2, 2, 96, 256), np.float32)
    scatter = np.zeros((6, 128, 128), np.float32)
    for side in range(2):
        own = [12 * side + q for q in range(4)]
        outer = own[2:] if side else own[:2]
        for q in range(2):
            for r in range(rows):
                gather[side, q * 8 + r, r * 16 + outer[q]] = 1
            for t in range(2):
                gather[side, 32 + q * 2 + t, t * 16 + outer[q]] = 1
                gather[side, 40 + q * 2 + t, (rows - 2 + t) * 16 + outer[q]] = 1
        for q in range(4):
            for t in range(2):
                gather[side, 16 + q * 2 + t, t * 16 + own[q]] = 1
                gather[side, 24 + q * 2 + t, (rows - 2 + t) * 16 + own[q]] = 1
        for half in range(2):
            to = window[side, half]
            for q in range(4):
                w = (q if side else q + 2) * 16
                for r in range(rows):
                    to[w + r, r * 16 + own[q]] = 1
                for t in range(2):
                    to[w + 8 + t, 160 + side * 8 + q * 2 + t] = 1
                    to[w + 14 + t, 144 + side * 8 + q * 2 + t] = 1
            for q in range(2):
                w = (q + 4 if side else q) * 16
                for r in range(rows):
                    to[w + r, 128 + q * 8 + r] = 1
                for t in range(2):
                    to[w + 8 + t, 192 + half * 8 + q * 2 + t] = 1
                    to[w + 14 + t, 176 + half * 8 + q * 2 + t] = 1
        for s in range(3):
            strip = s * 2 + side
            for q in range(2):
                for r in range(rows):
                    scatter[strip, r * 16 + 14 * side + q, strip * 16 + q * 8 + r] = 1
    window = window.reshape(4, 96, 256)
    return [x.astype(ml_dtypes.bfloat16) for x in (gather, window, scatter)]


def widen(row, times):
    return jnp.concatenate([row] * times, axis=1)


def inside(i, n):
    return (i >= 0) & (i < n)


def blocks_kernel(
    grid,
    images,
    tissue_list,
    tissue_count,
    w_reduce,
    w_spatial,
    w_expand,
    inner_gain,
    inner_bias,
    outer_gain,
    outer_bias,
    gather_in,
    window_in,
    scatter_in,
    h_out,
    spat_out,
    we_out,
    epi_out,
    edge_out,
    img,
    listed,
    counts,
    ig,
    ib,
    og,
    ob,
    wr,
    ws,
    wa,
    wb,
    wat,
    wbt,
    we,
    gb,
    mk,
    rb,
    row_send,
    row_recv,
    gather,
    window,
    scatter,
    col_send,
    col_recv,
    lines_send,
    lines_recv,
    diag_send,
    diag_recv,
    rows_ready,
    cols_ready,
    img_sem,
    w_sem,
    edge_send_sem,
    edge_recv_sem,
    w_send_sem,
    w_recv_sem,
    send_sem,
    recv_sem,
):
    n_row, n_col = grid
    slides, pairs, _, cols, chans = img.shape
    inner = wr.shape[2]
    last = cols - 1
    seg = lax.axis_index("segment")
    row = lax.axis_index("row")
    col = lax.axis_index("col")
    peer = {"segment": 1 - seg}
    around = [
        (i, j, inside(row + i, n_row) & inside(col + j, n_col))
        for j in (0, -1, 1)
        for i in (-1, 1, 0)
        if i or j
    ]

    def at(i, j):
        return {"row": row + i, "col": col + j}

    barrier = pltpu.get_barrier_semaphore()

    def greet(other):
        pl.semaphore_signal(barrier, inc=1, device_id=other, device_id_type=MESH)

    pl.when(seg == 0)(functools.partial(greet, peer))
    for i, j, there in around:
        core = 1 if j == 0 else 0
        pl.when(there)(functools.partial(greet, {"segment": core, **at(i, j)}))

    def meet(core, count, ready):
        @pl.when(seg == core)
        def _():
            pl.semaphore_wait(barrier, count)
            pl.semaphore_signal(ready, inc=1, device_id=peer, device_id_type=MESH)

        @pl.when(seg != core)
        def _():
            pl.semaphore_wait(ready, 1)

    def number(pick):
        return sum((there.astype(jnp.int32) for _, j, there in around if pick(j)), 0)

    def image_load(s):
        return pltpu.make_async_copy(images.at[seg * slides + s], img.at[s], img_sem.at[s])

    own = [
        pltpu.make_async_copy(src, dst, w_sem.at[i])
        for i, (src, dst) in enumerate(
            (
                (w_reduce.at[0], wr.at[seg]),
                (w_spatial.at[0], ws.at[seg]),
                (w_expand.at[0], we.at[seg]),
                (inner_gain, ig),
                (inner_bias, ib),
                (outer_gain, og),
                (outer_bias, ob),
                (tissue_count, counts),
                (tissue_list, listed),
                (gather_in, gather),
                (window_in, window),
                (scatter_in, scatter),
            )
        )
    ]
    for load in own[3:9] + own[:1]:
        load.start()
    for s in range(slides):
        image_load(s).start()
    for load in own[1:3] + own[9:]:
        load.start()
    for load in own[3:9]:
        load.wait()

    lines = [ig[0].astype(F32), ib[0].astype(F32)]
    for whole in (og[...].astype(F32), ob[...].astype(F32)):
        lines += [whole[:, i * inner : (i + 1) * inner] for i in range(chans // inner)]
    lines.append(jnp.zeros((4, inner), F32))
    gb[seg] = jnp.concatenate(lines, axis=0)

    position = lax.broadcasted_iota(jnp.int32, (1, listed.shape[1]), 1)
    for s in range(slides):
        slide = seg * slides + s
        here = listed[pl.ds(slide, 1), :]
        for t in range(cols // TW + 2):
            tile = col * (cols // TW) + t - 1
            hit = (here == tile) & (position < counts[slide])
            one = jnp.max(jnp.where(hit, 1.0, 0.0), axis=1, keepdims=True)
            mk[s, t] = jnp.broadcast_to(one, mk.shape[2:])

    meet(1, 1 + 2 * number(lambda j: j == 0), rows_ready)

    def swap(src, dst, i):
        return remote(
            src_ref=src,
            dst_ref=dst.at[seg],
            send_sem=w_send_sem.at[i],
            recv_sem=w_recv_sem.at[i],
            device_id=peer,
            device_id_type=MESH,
        )

    swaps = [
        swap(w_reduce.at[0], wr, 0),
        swap(gb.at[seg], gb, 1),
        swap(w_spatial.at[0], ws, 2),
        swap(w_expand.at[0], we, 3),
    ]
    for copy in swaps:
        copy.start()

    def sends(e, s):
        for n, (i, j, there) in enumerate(around[:2]):
            yield there, remote(
                src_ref=row_send.at[e, s, n],
                dst_ref=row_recv.at[e, s, 1 - n],
                send_sem=send_sem.at[e, s, n],
                recv_sem=recv_sem.at[e, s, 1 - n],
                device_id=at(i, j),
                device_id_type=MESH,
            )

    def edge_sends():
        for n, (i, j, there) in enumerate(around):
            a, b = (1 + i) // 2, (1 + j) // 2
            if j == 0:
                src, dst, here = lines_send.at[a], lines_recv.at[1 - a], lines_recv.at[a]
            elif i == 0:
                src, dst, here = col_send.at[b], col_recv.at[1 - b], col_recv.at[b]
            else:
                src, dst = diag_send.at[a, b], diag_recv.at[1 - a, 1 - b]
                here = diag_recv.at[a, b]
            copy = remote(
                src_ref=src,
                dst_ref=dst,
                send_sem=edge_send_sem.at[n],
                recv_sem=edge_recv_sem.at[mirror(n)],
                device_id=at(i, j),
                device_id_type=MESH,
            )
            yield there, copy, here

    def mirror(n):
        i, j, _ = around[n]
        return [(a, b) for a, b, _ in around].index((-i, -j))

    def store_shifted(e, s, half, red):
        place = rb.at[e, s, pl.ds(half, pairs), :, pl.ds((1 - half) * 3 * inner, 3 * inner)]
        place[...] = jnp.concatenate(
            [
                pltpu.roll(red, 1, 1).astype(BF16),
                red.astype(BF16),
                pltpu.roll(red, last, 1).astype(BF16),
            ],
            axis=2,
        )

    def reduce_half(e, s, half, x):
        v = jnp.dot(
            x.reshape(pairs * cols, chans), wr[e], preferred_element_type=F32
        ).reshape(pairs, cols // TW, TW, inner)
        mask = mk[s, 1 : 1 + cols // TW][:, 0:1]
        gain = (gb[e, 0:1] * mask)[None]
        bias = (gb[e, 2:3] * mask)[None]
        red = jnp.maximum(v * gain + bias, 0.0).reshape(pairs, cols, inner)
        if half == 0:
            row_send[e, s, 0] = red[0].astype(BF16)
        else:
            row_send[e, s, 1] = red[pairs - 1].astype(BF16)
        return red

    def send(e, s):
        for there, copy in sends(e, s):
            pl.when(there)(copy.start)

    def halo(e, s):
        copies = list(sends(e, s))
        for n, (there, _) in enumerate(copies):
            pl.when(there)(copies[1 - n][1].wait_recv)
        for way, there, q, lane in ((0, row > 0, 0, 0), (1, row < n_row - 1, pairs, 3 * inner)):
            got = jnp.where(there, row_recv[e, s, way].astype(F32), 0.0)
            rb[e, s, q, :, lane : lane + 3 * inner] = jnp.concatenate(
                [
                    pltpu.roll(got, 1, 0).astype(BF16),
                    got.astype(BF16),
                    pltpu.roll(got, last, 0).astype(BF16),
                ],
                axis=1,
            )

    def spatial(e, s):
        total = jnp.dot(
            rb[e, s, 0:pairs].reshape(pairs * cols, 6 * inner), wa[e], preferred_element_type=F32
        ) + jnp.dot(
            rb[e, s, 1 : pairs + 1].reshape(pairs * cols, 6 * inner),
            wb[e],
            preferred_element_type=F32,
        )
        gain, bias = widen(gb[e, 1:2], 2), widen(gb[e, 3:4], 2)
        return jnp.maximum(total * gain + bias, 0.0).astype(BF16)

    def spread(b):
        depth = 3 * inner
        zero = jnp.zeros((depth, inner), BF16)
        for w, first, second in (
            ([ws[b, i].reshape(depth, inner) for i in range(3)], wa, wb),
            ([ws[b, :, i].reshape(depth, inner) for i in range(3)], wat, wbt),
        ):
            first[b] = jnp.concatenate(
                [jnp.concatenate([w[0], zero], axis=1), jnp.concatenate([w[1], w[0]], axis=1)],
                axis=0,
            )
            second[b] = jnp.concatenate(
                [jnp.concatenate([w[2], w[1]], axis=1), jnp.concatenate([zero, w[2]], axis=1)],
                axis=0,
            )

    def outer(b):
        n = chans // inner
        gain = jnp.concatenate([gb[b, 4 + i : 5 + i] for i in range(n)], axis=1)
        bias = jnp.concatenate([gb[b, 4 + n + i : 5 + n + i] for i in range(n)], axis=1)
        return gain, bias

    def edge_pixels(s, side):
        cells = img[s, :, :, side * (cols - 16) : side * (cols - 16) + 16]
        return cells.reshape(2 * pairs * 16, chans)

    def send_edges():
        meet(0, 2 * number(lambda j: j != 0), cols_ready)
        parts = []
        for s in range(slides):
            parts.append(
                [
                    jnp.dot(gather[side], edge_pixels(s, side), preferred_element_type=F32)
                    for side in range(2)
                ]
            )
            for side in range(2):
                col_send[side, s] = parts[s][side][0:16].astype(BF16)
            for way in range(2):
                cut = slice(16 + 8 * way, 24 + 8 * way)
                lines_send[way, s] = jnp.concatenate(
                    [parts[s][0][cut], parts[s][1][cut]], axis=0
                ).astype(BF16)
        for way in range(2):
            cut = slice(32 + 8 * way, 40 + 8 * way)
            for side in range(2):
                for t in range(2):
                    two = [parts[min(2 * t + i, slides - 1)][side][cut] for i in range(2)]
                    diag_send[way, side, t] = jnp.concatenate(two, axis=0).astype(BF16)
        for there, copy, _ in edge_sends():
            pl.when(there)(copy.start)

    def edge_strips():
        copies = list(edge_sends())
        for n, (there, _, here) in enumerate(copies):
            pl.when(there)(copies[mirror(n)][1].wait_recv)

            @pl.when(jnp.logical_not(there))
            def _():
                here[...] = jnp.zeros_like(here)

        strips = 2 * slides
        own_row = lax.broadcasted_iota(jnp.int32, (16, inner), 0)
        valid = jnp.where(
            own_row < 8,
            1.0,
            jnp.where(
                own_row < 14,
                jnp.where(row < n_row - 1, 1.0, 0.0),
                jnp.where(row > 0, 1.0, 0.0),
            ),
        )
        cells, masks = [], []
        for s in range(slides):
            for side in range(2):
                mine = edge_pixels(s, side)
                source = jnp.concatenate(
                    [
                        mine,
                        col_recv[side, s],
                        lines_recv[0, s],
                        lines_recv[1, s],
                        diag_recv[0, side, s // 2],
                        diag_recv[1, side, s // 2],
                        mine[0:48],
                    ],
                    axis=0,
                )
                got = jnp.dot(window[2 * side + s % 2], source, preferred_element_type=F32)
                cells.append(got.astype(BF16).reshape(1, 6, 16, chans))
                tiles = (2, 2, 2, 2, 3, 3) if side else (0, 0, 1, 1, 1, 1)
                masks.append([mk[s, t, 0:1] for t in tiles])
        x = jnp.concatenate(cells, axis=0)

        def mask_of(columns):
            return jnp.concatenate(
                [jnp.stack([m[w] * valid for w in columns])[None] for m in masks], axis=0
            )

        def reduced(e, x, columns):
            n = len(columns)
            v = jnp.dot(x.reshape(-1, chans), wr[e], preferred_element_type=F32)
            v = jnp.maximum(v * gb[e, 0:1] + gb[e, 2:3], 0.0)
            v = v.reshape(strips, n, 16, inner) * mask_of(columns)
            flat = v.reshape(strips * n, 16, inner)
            return jnp.concatenate(
                [
                    pltpu.roll(flat, 1, 1).astype(BF16),
                    flat.astype(BF16),
                    pltpu.roll(flat, 15, 1).astype(BF16),
                ],
                axis=2,
            ).reshape(strips, n, 16, 3 * inner)

        def conv(e, first, second):
            total = jnp.dot(first, wat[e], preferred_element_type=F32)
            total += jnp.dot(second, wbt[e], preferred_element_type=F32)
            gain, bias = widen(gb[e, 1:2], 2), widen(gb[e, 3:4], 2)
            return jnp.maximum(total * gain + bias, 0.0)

        def expanded(e, sp, h, mask):
            gain, bias = outer(e)
            z = jnp.dot(sp, we[e], preferred_element_type=F32).reshape(h.shape)
            z = jnp.maximum(z * gain + bias + h.astype(F32), 0.0)
            return z * mask

        r = reduced(0, x, range(6))
        two = [jnp.concatenate([r[:, 2 * i], r[:, 2 * i + 1]], axis=2)[:, None] for i in range(3)]
        sp = conv(
            0,
            jnp.concatenate(two[0:2], axis=1).reshape(-1, 6 * inner),
            jnp.concatenate(two[1:3], axis=1).reshape(-1, 6 * inner),
        ).astype(BF16)
        h, red = [], []
        for half in range(2):
            columns = (1 + half, 3 + half)
            before = jnp.concatenate([x[:, w][:, None] for w in columns], axis=1)
            mask = jnp.concatenate(
                [
                    jnp.stack([jnp.broadcast_to(widen(m[w], chans // inner), (16, chans)) for w in columns])[None]
                    for m in masks
                ],
                axis=0,
            )
            now = expanded(0, sp[:, half * inner : (half + 1) * inner], before, mask)
            h.append(now)
            red.append(reduced(1, now.astype(BF16), columns))
        first, second = (
            jnp.concatenate([red[0][:, i], red[1][:, i]], axis=2).reshape(-1, 6 * inner)
            for i in range(2)
        )
        sp = conv(1, first, second).reshape(strips, 16, 2 * inner)[:, 0:8]
        done = []
        for half in range(2):
            now = h[1 - half][:, half, 0:8].astype(BF16)
            mask = jnp.concatenate([widen(m[2 + half], chans // inner)[None] for m in masks], axis=0)
            z = sp[:, :, half * inner : (half + 1) * inner].reshape(strips * 8, inner)
            done.append(expanded(1, z.astype(BF16), now, mask)[:, None])
        done = jnp.concatenate(done, axis=1).reshape(strips * 16, chans).astype(BF16)
        done = jnp.concatenate([done, jnp.zeros((128 - strips * 16, chans), BF16)], axis=0)
        for i in range(strips):
            put = jnp.dot(scatter[i], done, preferred_element_type=F32).astype(BF16)
            edge_out[i] = put.reshape(pairs, 2, 16, chans)

    late = lax.rem(col, RUN) == 0
    for load in own[9:]:
        load.wait()
    for s in range(slides):
        image_load(s).wait()
    pl.when(jnp.logical_not(late))(send_edges)

    own[0].wait()
    for copy in swaps[:2]:
        copy.wait()

    def first_reduce(s, carry):
        reds = [reduce_half(0, s, half, img[s, :, half]) for half in range(2)]
        send(0, s)
        for half in range(2):
            store_shifted(0, s, half, reds[half])
        return carry

    lax.fori_loop(0, slides, first_reduce, 0)

    for load in own[1:3]:
        load.wait()
    for copy in swaps[2:]:
        copy.wait()
    spread(0)
    spread(1)

    def middle(s, carry):
        halo(0, s)
        sp = spatial(0, s)
        gain, bias = outer(0)
        mask = widen(mk[s, 1 : 1 + cols // TW][:, 0:1].reshape(cols // TW, inner), chans // inner)[:, None]
        reds = []
        for half in range(2):
            z = jnp.dot(
                sp[:, half * inner : (half + 1) * inner], we[0], preferred_element_type=F32
            ).reshape(pairs, cols, chans)
            z = z * gain + bias + img[s, :, half].astype(F32)
            z = jnp.maximum(z, 0.0).reshape(pairs, cols // TW, TW, chans) * mask[None]
            z = z.astype(BF16).reshape(pairs, cols, chans)
            h_out[s, :, half] = z
            reds.append(reduce_half(1, s, half, z))
        send(1, s)
        for half in range(2):
            store_shifted(1, s, half, reds[half])
        return carry

    lax.fori_loop(0, slides, middle, 0)

    def final(s, carry):
        halo(1, s)
        spat_out[s] = spatial(1, s).reshape(pairs, cols, 2 * inner)
        return carry

    we_out[...] = we[1]
    gain, bias = outer(1)
    for s in range(slides):
        for t in range(cols // TW):
            mask = widen(mk[s, t + 1, 0:1], chans // inner)
            epi_out[s, t : t + 1] = gain * mask
            epi_out[s, 2 + t : 3 + t] = bias * mask
    lax.fori_loop(0, slides, final, 0)

    pl.when(late)(send_edges)
    edge_strips()
    for there, copy, _ in edge_sends():
        pl.when(there)(copy.wait_send)

    def drain(s, carry):
        for e in range(2):
            for there, copy in sends(e, s):
                pl.when(there)(copy.wait_send)
        return carry

    lax.fori_loop(0, slides, drain, 0)


def expand_kernel(h, spat, we, epi, edge, out, held, sem):
    slides, pairs, _, cols, chans = h.shape
    inner = we.shape[0]
    tiles = cols // TW

    def one(s, carry):
        for half in range(2):
            z = jnp.dot(
                spat[s].reshape(pairs * cols, 2 * inner)[:, half * inner : (half + 1) * inner],
                we[...],
                preferred_element_type=F32,
            ).reshape(pairs, tiles, TW, chans)
            gain = epi[s, 0:tiles][None, :, None]
            bias = epi[s, 2 : 2 + tiles][None, :, None]
            z = z * gain + bias + h[s, :, half].astype(F32).reshape(pairs, tiles, TW, chans)
            held[s, :, half] = jnp.maximum(z, 0.0).astype(BF16).reshape(pairs, cols, chans)
        place = lax.broadcasted_iota(jnp.int32, (pairs, 2, 16, chans), 2)
        for side in range(2):
            here = held.at[s, :, :, side * (cols - 16) : side * (cols - 16) + 16]
            edges = place >= 14 if side else place < 2
            here[...] = jnp.where(edges, edge[2 * s + side].astype(F32), here[...].astype(F32)).astype(BF16)
        pltpu.make_async_copy(held.at[s], out.at[s], sem.at[s]).start()
        return carry

    lax.fori_loop(0, slides, one, 0)
    for s in range(slides):
        pltpu.make_async_copy(held.at[s], out.at[s], sem.at[s]).wait()


def shards(grid, images, tissue_list, tissue_count, *weights):
    total, rows, cols, chans = images.shape
    slides, pairs = total // 2, rows // 2
    inner = weights[0].shape[2]
    w_reduce, w_spatial, w_expand, inner_gain, inner_bias, outer_gain, outer_bias = weights
    w_spatial = w_spatial.reshape(1, 3, 3, inner, inner)
    picks = [jnp.asarray(x) for x in selections(rows)]
    hbm = pl.BlockSpec(memory_space=pltpu.HBM)
    vmem = pl.BlockSpec(memory_space=pltpu.VMEM)
    dma = pltpu.SemaphoreType.DMA
    h, spat, we, epi, edge = pl.pallas_call(
        functools.partial(blocks_kernel, grid),
        out_shape=(
            pltpu.VMEM((slides, pairs, 2, cols, chans), BF16),
            pltpu.VMEM((slides, pairs, cols, 2 * inner), BF16),
            pltpu.VMEM((inner, chans), BF16),
            pltpu.VMEM((slides, 4, chans), F32),
            pltpu.VMEM((2 * slides, pairs, 2, 16, chans), BF16),
        ),
        in_specs=[hbm] * 13,
        out_specs=(vmem,) * 5,
        scratch_shapes=[
            pltpu.VMEM((slides, pairs, 2, cols, chans), BF16),
            pltpu.VMEM(tissue_list.shape, jnp.int32),
            pltpu.SMEM(tissue_count.shape, jnp.int32),
            pltpu.VMEM(inner_gain.shape, BF16),
            pltpu.VMEM(inner_bias.shape, BF16),
            pltpu.VMEM(outer_gain.shape, BF16),
            pltpu.VMEM(outer_bias.shape, BF16),
            pltpu.VMEM((2, chans, inner), BF16),
            pltpu.VMEM((2, 3, 3, inner, inner), BF16),
            *[pltpu.VMEM((2, 6 * inner, 2 * inner), BF16)] * 4,
            pltpu.VMEM((2, inner, chans), BF16),
            pltpu.VMEM((2, 16, inner), F32),
            pltpu.VMEM((slides, cols // TW + 2, 8, inner), F32),
            pltpu.VMEM((2, slides, pairs + 1, cols, 6 * inner), BF16),
            pltpu.VMEM((2, slides, 2, cols, inner), BF16),
            pltpu.VMEM((2, slides, 2, cols, inner), BF16),
            *[pltpu.VMEM(x.shape, BF16) for x in picks],
            *[pltpu.VMEM((2, slides, 16, chans), BF16)] * 4,
            *[pltpu.VMEM((2, 2, 2, 16, chans), BF16)] * 2,
            pltpu.SemaphoreType.REGULAR,
            pltpu.SemaphoreType.REGULAR,
            dma((slides,)),
            dma((12,)),
            dma((8,)),
            dma((8,)),
            dma((4,)),
            dma((4,)),
            dma((2, slides, 2)),
            dma((2, slides, 2)),
        ],
        compiler_params=pltpu.CompilerParams(
            collective_id=0, has_side_effects=True, vmem_limit_bytes=40 * 2**20
        ),
        name="blocks",
    )(
        *(
            pltpu.with_memory_space_constraint(x, pltpu.HBM)
            for x in (
                images.reshape(total, pairs, 2, cols, chans),
                tissue_list,
                tissue_count,
                w_reduce,
                w_spatial,
                w_expand,
                inner_gain,
                inner_bias,
                outer_gain,
                outer_bias,
                *picks,
            )
        )
    )
    out = pl.pallas_call(
        expand_kernel,
        out_shape=jax.ShapeDtypeStruct((slides, pairs, 2, cols, chans), BF16),
        in_specs=[vmem] * 5,
        out_specs=hbm,
        scratch_shapes=[
            pltpu.VMEM((slides, pairs, 2, cols, chans), BF16),
            dma((slides,)),
        ],
        compiler_params=pltpu.CompilerParams(vmem_limit_bytes=24 * 2**20),
        name="expand",
    )(h, spat, we, epi, edge)
    return out.reshape(slides, rows, cols, chans)


def solution(mesh):
    placed = (
        P(None, "row", "col", None),
        P(),
        P(),
        P("segment", None, None),
        P("segment", None, None, None, None),
        P("segment", None, None),
        P("segment", None, None),
        P("segment", None, None),
        P("segment", None),
        P("segment", None),
    )
    return jax.shard_map(
        functools.partial(shards, (mesh.shape["row"], mesh.shape["col"])),
        mesh=mesh,
        in_specs=placed,
        out_specs=P("segment", "row", "col", None),
        check_vma=False,
    )
```

```python
import functools

import jax
import jax.numpy as jnp
import ml_dtypes
import numpy as np
from jax import lax
from jax.experimental import pallas as pl
from jax.experimental.pallas import tpu as pltpu
from jax.sharding import PartitionSpec as P

MESH = pl.DeviceIdType.MESH
TW = 64
F32 = jnp.float32
BF16 = jnp.bfloat16
remote = pltpu.make_async_remote_copy


RUN = 8


def selections(rows):
    gather = np.zeros((2, 48, 128), np.float32)
    window = np.zeros((2, 2, 96, 256), np.float32)
    scatter = np.zeros((6, 128, 128), np.float32)
    for side in range(2):
        own = [12 * side + q for q in range(4)]
        outer = own[2:] if side else own[:2]
        for q in range(2):
            for r in range(rows):
                gather[side, q * 8 + r, r * 16 + outer[q]] = 1
            for t in range(2):
                gather[side, 32 + q * 2 + t, t * 16 + outer[q]] = 1
                gather[side, 40 + q * 2 + t, (rows - 2 + t) * 16 + outer[q]] = 1
        for q in range(4):
            for t in range(2):
                gather[side, 16 + q * 2 + t, t * 16 + own[q]] = 1
                gather[side, 24 + q * 2 + t, (rows - 2 + t) * 16 + own[q]] = 1
        for half in range(2):
            to = window[side, half]
            for q in range(4):
                w = (q if side else q + 2) * 16
                for r in range(rows):
                    to[w + r, r * 16 + own[q]] = 1
                for t in range(2):
                    to[w + 8 + t, 160 + side * 8 + q * 2 + t] = 1
                    to[w + 14 + t, 144 + side * 8 + q * 2 + t] = 1
            for q in range(2):
                w = (q + 4 if side else q) * 16
                for r in range(rows):
                    to[w + r, 128 + q * 8 + r] = 1
                for t in range(2):
                    to[w + 8 + t, 192 + half * 8 + q * 2 + t] = 1
                    to[w + 14 + t, 176 + half * 8 + q * 2 + t] = 1
        for s in range(3):
            strip = s * 2 + side
            for q in range(2):
                for r in range(rows):
                    scatter[strip, r * 16 + 14 * side + q, strip * 16 + q * 8 + r] = 1
    window = window.reshape(4, 96, 2, 128).swapaxes(1, 2)
    window = window.reshape(8, 96, 128)
    return [x.astype(ml_dtypes.bfloat16) for x in (gather, window, scatter)]


def widen(row, times):
    return jnp.concatenate([row] * times, axis=1)


def inside(i, n):
    return (i >= 0) & (i < n)


def blocks_kernel(
    grid,
    images,
    tissue_list,
    tissue_count,
    w_reduce,
    w_spatial,
    w_expand,
    inner_gain,
    inner_bias,
    outer_gain,
    outer_bias,
    gather_in,
    window_in,
    scatter_in,
    out,
    img,
    mid,
    listed,
    counts,
    ig,
    ib,
    og,
    ob,
    wr,
    ws,
    wa,
    wb,
    wat,
    wbt,
    we,
    gb,
    mk,
    rb,
    row_send,
    row_recv,
    gather,
    window,
    scatter,
    col_send,
    col_recv,
    lines_send,
    lines_recv,
    diag_send,
    diag_recv,
    rows_ready,
    cols_ready,
    img_sem,
    w_sem,
    edge_send_sem,
    edge_recv_sem,
    w_send_sem,
    w_recv_sem,
    send_sem,
    recv_sem,
):
    n_row, n_col = grid
    slides, pairs, _, cols, chans = img.shape
    inner = wr.shape[2]
    last = cols - 1
    seg = lax.axis_index("segment")
    row = lax.axis_index("row")
    col = lax.axis_index("col")
    peer = {"segment": 1 - seg}
    around = [
        (i, j, inside(row + i, n_row) & inside(col + j, n_col))
        for j in (0, -1, 1)
        for i in (-1, 1, 0)
        if i or j
    ]

    def at(i, j):
        return {"row": row + i, "col": col + j}

    barrier = pltpu.get_barrier_semaphore()

    def greet(other):
        pl.semaphore_signal(barrier, inc=1, device_id=other, device_id_type=MESH)

    pl.when(seg == 0)(functools.partial(greet, peer))
    for i, j, there in around:
        core = 1 if j == 0 else 0
        pl.when(there)(functools.partial(greet, {"segment": core, **at(i, j)}))

    def meet(core, count, ready):
        @pl.when(seg == core)
        def _():
            pl.semaphore_wait(barrier, count)
            pl.semaphore_signal(ready, inc=1, device_id=peer, device_id_type=MESH)

        @pl.when(seg != core)
        def _():
            pl.semaphore_wait(ready, 1)

    def number(pick):
        return sum((there.astype(jnp.int32) for _, j, there in around if pick(j)), 0)

    def image_load(s):
        return pltpu.make_async_copy(images.at[seg * slides + s], img.at[s], img_sem.at[s])

    own = [
        pltpu.make_async_copy(src, dst, w_sem.at[i])
        for i, (src, dst) in enumerate(
            (
                (w_reduce.at[0], wr.at[seg]),
                (w_spatial.at[0], ws.at[seg]),
                (w_expand.at[0], we.at[seg]),
                (inner_gain, ig),
                (inner_bias, ib),
                (outer_gain, og),
                (outer_bias, ob),
                (tissue_count, counts),
                (tissue_list, listed),
                (gather_in, gather),
                (window_in, window),
                (scatter_in, scatter),
            )
        )
    ]
    for load in own[3:9] + own[:1]:
        load.start()
    for s in range(slides):
        image_load(s).start()
    for load in own[1:3] + own[9:]:
        load.start()
    for load in own[3:9]:
        load.wait()

    lines = [ig[0].astype(F32), ib[0].astype(F32)]
    for whole in (og[...].astype(F32), ob[...].astype(F32)):
        lines += [whole[:, i * inner : (i + 1) * inner] for i in range(chans // inner)]
    lines.append(jnp.zeros((4, inner), F32))
    gb[seg] = jnp.concatenate(lines, axis=0)

    position = lax.broadcasted_iota(jnp.int32, (1, listed.shape[1]), 1)
    for s in range(slides):
        slide = seg * slides + s
        here = listed[pl.ds(slide, 1), :]
        for t in range(cols // TW + 2):
            tile = col * (cols // TW) + t - 1
            hit = (here == tile) & (position < counts[slide])
            one = jnp.max(jnp.where(hit, 1.0, 0.0), axis=1, keepdims=True)
            mk[s, t] = jnp.broadcast_to(one, mk.shape[2:])

    meet(1, 1 + 2 * number(lambda j: j == 0), rows_ready)

    def swap(src, dst, i):
        return remote(
            src_ref=src,
            dst_ref=dst.at[seg],
            send_sem=w_send_sem.at[i],
            recv_sem=w_recv_sem.at[i],
            device_id=peer,
            device_id_type=MESH,
        )

    swaps = [
        swap(w_reduce.at[0], wr, 0),
        swap(gb.at[seg], gb, 1),
        swap(w_spatial.at[0], ws, 2),
        swap(w_expand.at[0], we, 3),
    ]
    for copy in swaps:
        copy.start()

    def row_sends(e):
        for n, (i, j, there) in enumerate(around[:2]):
            yield there, remote(
                src_ref=row_send.at[e, n],
                dst_ref=row_recv.at[e, 1 - n],
                send_sem=send_sem.at[e, n],
                recv_sem=recv_sem.at[e, 1 - n],
                device_id=at(i, j),
                device_id_type=MESH,
            )

    def edge_sends():
        for n, (i, j, there) in enumerate(around):
            a, b = (1 + i) // 2, (1 + j) // 2
            if j == 0:
                src, dst, here = lines_send.at[a], lines_recv.at[1 - a], lines_recv.at[a]
            elif i == 0:
                src, dst, here = col_send.at[b], col_recv.at[1 - b], col_recv.at[b]
            else:
                src, dst = diag_send.at[a, b], diag_recv.at[1 - a, 1 - b]
                here = diag_recv.at[a, b]
            copy = remote(
                src_ref=src,
                dst_ref=dst,
                send_sem=edge_send_sem.at[n],
                recv_sem=edge_recv_sem.at[mirror(n)],
                device_id=at(i, j),
                device_id_type=MESH,
            )
            yield there, copy, here

    def mirror(n):
        i, j, _ = around[n]
        return [(a, b) for a, b, _ in around].index((-i, -j))

    def place_row(e, r, red):
        lane = (r + 1) % 2 * 3 * inner
        rb[e, :, (r + 1) // 2, :, lane : lane + 3 * inner] = jnp.concatenate(
            [
                pltpu.roll(red, 1, 1).astype(BF16),
                red.astype(BF16),
                pltpu.roll(red, last, 1).astype(BF16),
            ],
            axis=2,
        )

    def reduce_pair(e, x, p):
        v = jnp.dot(x.reshape(-1, chans), wr[e], preferred_element_type=F32)
        v = v.reshape(slides, 2, cols // TW, TW, inner)
        mask = mk[:, 1 : 1 + cols // TW, 0:1][:, None]
        red = jnp.maximum(v * (gb[e, 0:1] * mask) + gb[e, 2:3] * mask, 0.0)
        return red.reshape(slides, 2, cols, inner)

    def send_row(e, way, red):
        row_send[e, way] = red[:, way].astype(BF16)
        there, copy = list(row_sends(e))[way]
        pl.when(there)(copy.start)

    def halo(e):
        copies = list(row_sends(e))
        for n, (there, _) in enumerate(copies):
            pl.when(there)(copies[1 - n][1].wait_recv)
        for way, there, r in ((0, row > 0, -1), (1, row < n_row - 1, 2 * pairs)):
            place_row(e, r, jnp.where(there, row_recv[e, way].astype(F32), 0.0))

    def spatial(e, p):
        total = jnp.dot(rb[e, :, p].reshape(-1, 6 * inner), wa[e], preferred_element_type=F32)
        total += jnp.dot(rb[e, :, p + 1].reshape(-1, 6 * inner), wb[e], preferred_element_type=F32)
        gain, bias = widen(gb[e, 1:2], 2), widen(gb[e, 3:4], 2)
        return jnp.maximum(total * gain + bias, 0.0).astype(BF16)

    def expand(e, sp, p, before, after):
        gain, bias = outer(e)
        mask = mk[:, 1 : 1 + cols // TW, 0:1]
        mask = jnp.concatenate([mask] * (chans // inner), axis=3)
        for half in range(2):
            z = jnp.dot(
                sp[:, half * inner : (half + 1) * inner], we[e], preferred_element_type=F32
            ).reshape(slides, cols, chans)
            y = jnp.maximum(z * gain + bias + before[:, p, half].astype(F32), 0.0)
            y = y.reshape(slides, cols // TW, TW, chans) * mask
            after[:, p, half] = y.reshape(slides, cols, chans).astype(BF16)

    def spread(b):
        depth = 3 * inner
        zero = jnp.zeros((depth, inner), BF16)
        for w, first, second in (
            ([ws[b, i].reshape(depth, inner) for i in range(3)], wa, wb),
            ([ws[b, :, i].reshape(depth, inner) for i in range(3)], wat, wbt),
        ):
            first[b] = jnp.concatenate(
                [jnp.concatenate([w[0], zero], axis=1), jnp.concatenate([w[1], w[0]], axis=1)],
                axis=0,
            )
            second[b] = jnp.concatenate(
                [jnp.concatenate([w[2], w[1]], axis=1), jnp.concatenate([zero, w[2]], axis=1)],
                axis=0,
            )

    def outer(b):
        n = chans // inner
        gain = jnp.concatenate([gb[b, 4 + i : 5 + i] for i in range(n)], axis=1)
        bias = jnp.concatenate([gb[b, 4 + n + i : 5 + n + i] for i in range(n)], axis=1)
        return gain, bias

    def edge_pixels(s, side):
        cells = img[s, :, :, side * (cols - 16) : side * (cols - 16) + 16]
        return cells.reshape(2 * pairs * 16, chans)

    def send_edges():
        meet(0, 2 * number(lambda j: j != 0), cols_ready)
        parts = []
        for s in range(slides):
            parts.append(
                [
                    jnp.dot(gather[side], edge_pixels(s, side), preferred_element_type=F32)
                    for side in range(2)
                ]
            )
            for side in range(2):
                col_send[side, s] = parts[s][side][0:16].astype(BF16)
            for way in range(2):
                cut = slice(16 + 8 * way, 24 + 8 * way)
                lines_send[way, s] = jnp.concatenate(
                    [parts[s][0][cut], parts[s][1][cut]], axis=0
                ).astype(BF16)
        for way in range(2):
            cut = slice(32 + 8 * way, 40 + 8 * way)
            for side in range(2):
                for t in range(2):
                    two = [parts[min(2 * t + i, slides - 1)][side][cut] for i in range(2)]
                    diag_send[way, side, t] = jnp.concatenate(two, axis=0).astype(BF16)
        for there, copy, _ in edge_sends():
            pl.when(there)(copy.start)

    def edge_strips():
        copies = list(edge_sends())
        for n, (there, _, here) in enumerate(copies):
            pl.when(there)(copies[mirror(n)][1].wait_recv)

            @pl.when(jnp.logical_not(there))
            def _():
                here[...] = jnp.zeros_like(here)

        strips = 2 * slides
        own_row = lax.broadcasted_iota(jnp.int32, (16, inner), 0)
        valid = jnp.where(
            own_row < 8,
            1.0,
            jnp.where(
                own_row < 14,
                jnp.where(row < n_row - 1, 1.0, 0.0),
                jnp.where(row > 0, 1.0, 0.0),
            ),
        )
        cells, masks = [], []
        for s in range(slides):
            for side in range(2):
                mine = edge_pixels(s, side)
                source = jnp.concatenate(
                    [
                        mine,
                        col_recv[side, s],
                        lines_recv[0, s],
                        lines_recv[1, s],
                        diag_recv[0, side, s // 2],
                        diag_recv[1, side, s // 2],
                        mine[0:48],
                    ],
                    axis=0,
                )
                k = 4 * side + 2 * (s % 2)
                pick = jnp.concatenate([window[k], window[k + 1]], axis=1)
                got = jnp.dot(pick, source, preferred_element_type=F32)
                cells.append(got.astype(BF16).reshape(1, 6, 16, chans))
                tiles = (2, 2, 2, 2, 3, 3) if side else (0, 0, 1, 1, 1, 1)
                masks.append([mk[s, t, 0:1] for t in tiles])
        x = jnp.concatenate(cells, axis=0)

        def mask_of(columns):
            return jnp.concatenate(
                [jnp.stack([m[w] * valid for w in columns])[None] for m in masks], axis=0
            )

        def reduced(e, x, columns):
            n = len(columns)
            v = jnp.dot(x.reshape(-1, chans), wr[e], preferred_element_type=F32)
            v = jnp.maximum(v * gb[e, 0:1] + gb[e, 2:3], 0.0)
            v = v.reshape(strips, n, 16, inner) * mask_of(columns)
            flat = v.reshape(strips * n, 16, inner)
            return jnp.concatenate(
                [
                    pltpu.roll(flat, 1, 1).astype(BF16),
                    flat.astype(BF16),
                    pltpu.roll(flat, 15, 1).astype(BF16),
                ],
                axis=2,
            ).reshape(strips, n, 16, 3 * inner)

        def conv(e, first, second):
            total = jnp.dot(first, wat[e], preferred_element_type=F32)
            total += jnp.dot(second, wbt[e], preferred_element_type=F32)
            gain, bias = widen(gb[e, 1:2], 2), widen(gb[e, 3:4], 2)
            return jnp.maximum(total * gain + bias, 0.0)

        def expanded(e, sp, h, mask):
            gain, bias = outer(e)
            z = jnp.dot(sp, we[e], preferred_element_type=F32).reshape(h.shape)
            z = jnp.maximum(z * gain + bias + h.astype(F32), 0.0)
            return z * mask

        r = reduced(0, x, range(6))
        two = [jnp.concatenate([r[:, 2 * i], r[:, 2 * i + 1]], axis=2)[:, None] for i in range(3)]
        sp = conv(
            0,
            jnp.concatenate(two[0:2], axis=1).reshape(-1, 6 * inner),
            jnp.concatenate(two[1:3], axis=1).reshape(-1, 6 * inner),
        ).astype(BF16)
        h, red = [], []
        for half in range(2):
            columns = (1 + half, 3 + half)
            before = jnp.concatenate([x[:, w][:, None] for w in columns], axis=1)
            mask = jnp.concatenate(
                [
                    jnp.stack([jnp.broadcast_to(widen(m[w], chans // inner), (16, chans)) for w in columns])[None]
                    for m in masks
                ],
                axis=0,
            )
            now = expanded(0, sp[:, half * inner : (half + 1) * inner], before, mask)
            h.append(now)
            red.append(reduced(1, now.astype(BF16), columns))
        first, second = (
            jnp.concatenate([red[0][:, i], red[1][:, i]], axis=2).reshape(-1, 6 * inner)
            for i in range(2)
        )
        sp = conv(1, first, second).reshape(strips, 16, 2 * inner)[:, 0:8]
        done = []
        for half in range(2):
            now = h[1 - half][:, half, 0:8].astype(BF16)
            mask = jnp.concatenate([widen(m[2 + half], chans // inner)[None] for m in masks], axis=0)
            z = sp[:, :, half * inner : (half + 1) * inner].reshape(strips * 8, inner)
            done.append(expanded(1, z.astype(BF16), now, mask)[:, None])
        done = jnp.concatenate(done, axis=1).reshape(strips * 16, chans).astype(BF16)
        done = jnp.concatenate([done, jnp.zeros((128 - strips * 16, chans), BF16)], axis=0)
        for i in range(strips):
            put = jnp.dot(scatter[i], done, preferred_element_type=F32).reshape(pairs, 2, 16, chans)
            spot = lax.broadcasted_iota(jnp.int32, put.shape, 2)
            here = out.at[i // 2, :, :, i % 2 * (cols - 16) : i % 2 * (cols - 16) + 16]
            edges = spot >= 14 if i % 2 else spot < 2
            here[...] = jnp.where(edges, put, here[...].astype(F32)).astype(BF16)

    late = lax.rem(col, RUN) == 0
    for load in own[9:]:
        load.wait()
    for s in range(slides):
        image_load(s).wait()
    pl.when(jnp.logical_not(late))(send_edges)

    own[0].wait()
    for copy in swaps[:2]:
        copy.wait()
    ends = (0, pairs - 1)
    between = tuple(range(1, pairs - 1))

    def place_pairs(e, group, reds):
        for p, red in zip(group, reds):
            for half in range(2):
                place_row(e, 2 * p + half, red[:, half])

    def reduce_ends(e, x):
        reds = [reduce_pair(e, x[:, p], p) for p in ends]
        for way in range(2):
            send_row(e, way, reds[way])
        place_pairs(e, ends, reds)

    def reduce_between(e, x):
        place_pairs(e, between, [reduce_pair(e, x[:, p], p) for p in between])

    reduce_ends(0, img)
    reduce_between(0, img)

    for load in own[1:3]:
        load.wait()
    for copy in swaps[2:]:
        copy.wait()
    spread(0)
    spread(1)

    def expand_pairs(e, group, before, after):
        parts = [spatial(e, p) for p in group]
        for p, sp in zip(group, parts):
            expand(e, sp, p, before, after)

    expand_pairs(0, between, img, mid)
    reduce_between(1, mid)
    halo(0)
    expand_pairs(0, ends, img, mid)
    reduce_ends(1, mid)
    expand_pairs(1, between, mid, out)
    halo(1)
    expand_pairs(1, ends, mid, out)

    pl.when(late)(send_edges)
    edge_strips()
    for there, copy, _ in edge_sends():
        pl.when(there)(copy.wait_send)

    for e in range(2):
        for there, copy in row_sends(e):
            pl.when(there)(copy.wait_send)


def write_kernel(held, out, sem):
    copies = [pltpu.make_async_copy(held.at[s], out.at[s], sem.at[s]) for s in range(held.shape[0])]
    for copy in copies:
        copy.start()
    for copy in copies:
        copy.wait()


def shards(grid, images, tissue_list, tissue_count, *weights):
    total, rows, cols, chans = images.shape
    slides, pairs = total // 2, rows // 2
    inner = weights[0].shape[2]
    w_reduce, w_spatial, w_expand, inner_gain, inner_bias, outer_gain, outer_bias = weights
    w_spatial = w_spatial.reshape(1, 3, 3, inner, inner)
    picks = [jnp.asarray(x) for x in selections(rows)]
    hbm = pl.BlockSpec(memory_space=pltpu.HBM)
    vmem = pl.BlockSpec(memory_space=pltpu.VMEM)
    dma = pltpu.SemaphoreType.DMA
    held = pl.pallas_call(
        functools.partial(blocks_kernel, grid),
        out_shape=pltpu.VMEM((slides, pairs, 2, cols, chans), BF16),
        in_specs=[hbm] * 13,
        out_specs=vmem,
        scratch_shapes=[
            *[pltpu.VMEM((slides, pairs, 2, cols, chans), BF16)] * 2,
            pltpu.VMEM(tissue_list.shape, jnp.int32),
            pltpu.SMEM(tissue_count.shape, jnp.int32),
            pltpu.VMEM(inner_gain.shape, BF16),
            pltpu.VMEM(inner_bias.shape, BF16),
            pltpu.VMEM(outer_gain.shape, BF16),
            pltpu.VMEM(outer_bias.shape, BF16),
            pltpu.VMEM((2, chans, inner), BF16),
            pltpu.VMEM((2, 3, 3, inner, inner), BF16),
            *[pltpu.VMEM((2, 6 * inner, 2 * inner), BF16)] * 4,
            pltpu.VMEM((2, inner, chans), BF16),
            pltpu.VMEM((2, 16, inner), F32),
            pltpu.VMEM((slides, cols // TW + 2, 8, inner), F32),
            pltpu.VMEM((2, slides, pairs + 1, cols, 6 * inner), BF16),
            *[pltpu.VMEM((2, 2, slides, cols, inner), BF16)] * 2,
            *[pltpu.VMEM(x.shape, BF16) for x in picks],
            *[pltpu.VMEM((2, slides, 16, chans), BF16)] * 4,
            *[pltpu.VMEM((2, 2, 2, 16, chans), BF16)] * 2,
            pltpu.SemaphoreType.REGULAR,
            pltpu.SemaphoreType.REGULAR,
            dma((slides,)),
            dma((12,)),
            dma((8,)),
            dma((8,)),
            dma((4,)),
            dma((4,)),
            dma((2, 2)),
            dma((2, 2)),
        ],
        compiler_params=pltpu.CompilerParams(
            collective_id=0, has_side_effects=True, vmem_limit_bytes=40 * 2**20
        ),
        name="blocks",
    )(
        *(
            pltpu.with_memory_space_constraint(x, pltpu.HBM)
            for x in (
                images.reshape(total, pairs, 2, cols, chans),
                tissue_list,
                tissue_count,
                w_reduce,
                w_spatial,
                w_expand,
                inner_gain,
                inner_bias,
                outer_gain,
                outer_bias,
                *picks,
            )
        )
    )
    out = pl.pallas_call(
        write_kernel,
        out_shape=jax.ShapeDtypeStruct((slides, pairs, 2, cols, chans), BF16),
        in_specs=[vmem],
        out_specs=hbm,
        scratch_shapes=[dma((slides,))],
        compiler_params=pltpu.CompilerParams(vmem_limit_bytes=16 * 2**20),
        name="write",
    )(held)
    return out.reshape(slides, rows, cols, chans)


def solution(mesh):
    placed = (
        P(None, "row", "col", None),
        P(),
        P(),
        P("segment", None, None),
        P("segment", None, None, None, None),
        P("segment", None, None),
        P("segment", None, None),
        P("segment", None, None),
        P("segment", None),
        P("segment", None),
    )
    return jax.shard_map(
        functools.partial(shards, (mesh.shape["row"], mesh.shape["col"])),
        mesh=mesh,
        in_specs=placed,
        out_specs=P("segment", "row", "col", None),
        check_vma=False,
    )
```

```python
import functools

import jax
import jax.numpy as jnp
import ml_dtypes
import numpy as np
from jax import lax
from jax.experimental import pallas as pl
from jax.experimental.pallas import tpu as pltpu
from jax.sharding import PartitionSpec as P

MESH = pl.DeviceIdType.MESH
TW = 64
F32 = jnp.float32
BF16 = jnp.bfloat16
remote = pltpu.make_async_remote_copy


RUN = 8


def selections(rows):
    gather = np.zeros((2, 48, 128), np.float32)
    window = np.zeros((2, 2, 96, 256), np.float32)
    scatter = np.zeros((6, 128, 128), np.float32)
    for side in range(2):
        own = [12 * side + q for q in range(4)]
        outer = own[2:] if side else own[:2]
        for q in range(2):
            for r in range(rows):
                gather[side, q * 8 + r, r * 16 + outer[q]] = 1
            for t in range(2):
                gather[side, 32 + q * 2 + t, t * 16 + outer[q]] = 1
                gather[side, 40 + q * 2 + t, (rows - 2 + t) * 16 + outer[q]] = 1
        for q in range(4):
            for t in range(2):
                gather[side, 16 + q * 2 + t, t * 16 + own[q]] = 1
                gather[side, 24 + q * 2 + t, (rows - 2 + t) * 16 + own[q]] = 1
        for half in range(2):
            to = window[side, half]
            for q in range(4):
                w = (q if side else q + 2) * 16
                for r in range(rows):
                    to[w + r, r * 16 + own[q]] = 1
                for t in range(2):
                    to[w + 8 + t, 160 + side * 8 + q * 2 + t] = 1
                    to[w + 14 + t, 144 + side * 8 + q * 2 + t] = 1
            for q in range(2):
                w = (q + 4 if side else q) * 16
                for r in range(rows):
                    to[w + r, 128 + q * 8 + r] = 1
                for t in range(2):
                    to[w + 8 + t, 192 + half * 8 + q * 2 + t] = 1
                    to[w + 14 + t, 176 + half * 8 + q * 2 + t] = 1
        for s in range(3):
            strip = s * 2 + side
            for q in range(2):
                for r in range(rows):
                    scatter[strip, r * 16 + 14 * side + q, strip * 16 + q * 8 + r] = 1
    window = window.reshape(4, 96, 2, 128).swapaxes(1, 2)
    window = window.reshape(8, 96, 128)
    return [x.astype(ml_dtypes.bfloat16) for x in (gather, window, scatter)]


def widen(row, times):
    return jnp.concatenate([row] * times, axis=1)


def inside(i, n):
    return (i >= 0) & (i < n)


def blocks_kernel(
    grid,
    images,
    tissue_list,
    tissue_count,
    w_reduce,
    w_spatial,
    w_expand,
    inner_gain,
    inner_bias,
    outer_gain,
    outer_bias,
    gather_in,
    window_in,
    scatter_in,
    out,
    img,
    mid,
    listed,
    counts,
    ig,
    ib,
    og,
    ob,
    wr,
    ws,
    wa,
    wb,
    wat,
    wbt,
    we,
    gb,
    mk,
    rb,
    row_send,
    row_recv,
    gather,
    window,
    scatter,
    col_send,
    col_recv,
    lines_send,
    lines_recv,
    diag_send,
    diag_recv,
    fixed,
    rows_ready,
    cols_ready,
    img_sem,
    w_sem,
    edge_send_sem,
    edge_recv_sem,
    w_send_sem,
    w_recv_sem,
    send_sem,
    recv_sem,
):
    n_row, n_col = grid
    slides, pairs, _, cols, chans = img.shape
    inner = wr.shape[2]
    last = cols - 1
    seg = lax.axis_index("segment")
    row = lax.axis_index("row")
    col = lax.axis_index("col")
    peer = {"segment": 1 - seg}
    around = [
        (i, j, inside(row + i, n_row) & inside(col + j, n_col))
        for j in (0, -1, 1)
        for i in (-1, 1, 0)
        if i or j
    ]

    def at(i, j):
        return {"row": row + i, "col": col + j}

    barrier = pltpu.get_barrier_semaphore()

    def greet(other):
        pl.semaphore_signal(barrier, inc=1, device_id=other, device_id_type=MESH)

    pl.when(seg == 0)(functools.partial(greet, peer))
    for i, j, there in around:
        core = 1 if j == 0 else 0
        pl.when(there)(functools.partial(greet, {"segment": core, **at(i, j)}))

    def meet(core, count, ready):
        @pl.when(seg == core)
        def _():
            pl.semaphore_wait(barrier, count)
            pl.semaphore_signal(ready, inc=1, device_id=peer, device_id_type=MESH)

        @pl.when(seg != core)
        def _():
            pl.semaphore_wait(ready, 1)

    def number(pick):
        return sum((there.astype(jnp.int32) for _, j, there in around if pick(j)), 0)

    def image_load(s):
        return pltpu.make_async_copy(images.at[seg * slides + s], img.at[s], img_sem.at[s])

    own = [
        pltpu.make_async_copy(src, dst, w_sem.at[i])
        for i, (src, dst) in enumerate(
            (
                (w_reduce.at[0], wr.at[seg]),
                (w_spatial.at[0], ws.at[seg]),
                (w_expand.at[0], we.at[seg]),
                (inner_gain, ig),
                (inner_bias, ib),
                (outer_gain, og),
                (outer_bias, ob),
                (tissue_count, counts),
                (tissue_list, listed),
                (gather_in, gather),
                (window_in, window),
                (scatter_in, scatter),
            )
        )
    ]
    for load in own[3:9] + own[:1]:
        load.start()
    for s in range(slides):
        image_load(s).start()
    for load in own[1:3] + own[9:]:
        load.start()
    for load in own[3:9]:
        load.wait()

    lines = [ig[0].astype(F32), ib[0].astype(F32)]
    for whole in (og[...].astype(F32), ob[...].astype(F32)):
        lines += [whole[:, i * inner : (i + 1) * inner] for i in range(chans // inner)]
    lines.append(jnp.zeros((4, inner), F32))
    gb[seg] = jnp.concatenate(lines, axis=0)

    position = lax.broadcasted_iota(jnp.int32, (1, listed.shape[1]), 1)
    for s in range(slides):
        slide = seg * slides + s
        here = listed[pl.ds(slide, 1), :]
        for t in range(cols // TW + 2):
            tile = col * (cols // TW) + t - 1
            hit = (here == tile) & (position < counts[slide])
            one = jnp.max(jnp.where(hit, 1.0, 0.0), axis=1, keepdims=True)
            mk[s, t] = jnp.broadcast_to(one, mk.shape[2:])

    meet(1, 1 + 2 * number(lambda j: j == 0), rows_ready)

    def swap(src, dst, i):
        return remote(
            src_ref=src,
            dst_ref=dst.at[seg],
            send_sem=w_send_sem.at[i],
            recv_sem=w_recv_sem.at[i],
            device_id=peer,
            device_id_type=MESH,
        )

    swaps = [
        swap(w_reduce.at[0], wr, 0),
        swap(gb.at[seg], gb, 1),
        swap(w_spatial.at[0], ws, 2),
        swap(w_expand.at[0], we, 3),
    ]
    for copy in swaps:
        copy.start()

    def row_sends(e):
        for n, (i, j, there) in enumerate(around[:2]):
            yield there, remote(
                src_ref=row_send.at[e, n],
                dst_ref=row_recv.at[e, 1 - n],
                send_sem=send_sem.at[e, n],
                recv_sem=recv_sem.at[e, 1 - n],
                device_id=at(i, j),
                device_id_type=MESH,
            )

    def edge_sends():
        for n, (i, j, there) in enumerate(around):
            a, b = (1 + i) // 2, (1 + j) // 2
            if j == 0:
                src, dst, here = lines_send.at[a], lines_recv.at[1 - a], lines_recv.at[a]
            elif i == 0:
                src, dst, here = col_send.at[b], col_recv.at[1 - b], col_recv.at[b]
            else:
                src, dst = diag_send.at[a, b], diag_recv.at[1 - a, 1 - b]
                here = diag_recv.at[a, b]
            copy = remote(
                src_ref=src,
                dst_ref=dst,
                send_sem=edge_send_sem.at[n],
                recv_sem=edge_recv_sem.at[mirror(n)],
                device_id=at(i, j),
                device_id_type=MESH,
            )
            yield there, copy, here

    def mirror(n):
        i, j, _ = around[n]
        return [(a, b) for a, b, _ in around].index((-i, -j))

    def place_row(e, r, red):
        lane = (r + 1) % 2 * 3 * inner
        rb[e, :, (r + 1) // 2, :, lane : lane + 3 * inner] = jnp.concatenate(
            [
                pltpu.roll(red, 1, 1).astype(BF16),
                red.astype(BF16),
                pltpu.roll(red, last, 1).astype(BF16),
            ],
            axis=2,
        )

    def reduce_pair(e, x, p):
        v = jnp.dot(x.reshape(-1, chans), wr[e], preferred_element_type=F32)
        v = v.reshape(slides, 2, cols // TW, TW, inner)
        mask = mk[:, 1 : 1 + cols // TW, 0:1][:, None]
        red = jnp.maximum(v * (gb[e, 0:1] * mask) + gb[e, 2:3] * mask, 0.0)
        return red.reshape(slides, 2, cols, inner)

    def send_row(e, way, red):
        row_send[e, way] = red[:, way].astype(BF16)
        there, copy = list(row_sends(e))[way]
        pl.when(there)(copy.start)

    def halo(e):
        copies = list(row_sends(e))
        for n, (there, _) in enumerate(copies):
            pl.when(there)(copies[1 - n][1].wait_recv)
        for way, there, r in ((0, row > 0, -1), (1, row < n_row - 1, 2 * pairs)):
            place_row(e, r, jnp.where(there, row_recv[e, way].astype(F32), 0.0))

    def spatial(e, p):
        total = jnp.dot(rb[e, :, p].reshape(-1, 6 * inner), wa[e], preferred_element_type=F32)
        total += jnp.dot(rb[e, :, p + 1].reshape(-1, 6 * inner), wb[e], preferred_element_type=F32)
        gain, bias = widen(gb[e, 1:2], 2), widen(gb[e, 3:4], 2)
        return jnp.maximum(total * gain + bias, 0.0).astype(BF16)

    def expand(e, sp, p, before, after):
        gain, bias = outer(e)
        mask = mk[:, 1 : 1 + cols // TW, 0:1]
        mask = jnp.concatenate([mask] * (chans // inner), axis=3)
        for half in range(2):
            z = jnp.dot(
                sp[:, half * inner : (half + 1) * inner], we[e], preferred_element_type=F32
            ).reshape(slides, cols, chans)
            y = jnp.maximum(z * gain + bias + before[:, p, half].astype(F32), 0.0)
            y = y.reshape(slides, cols // TW, TW, chans) * mask
            after[:, p, half] = y.reshape(slides, cols, chans).astype(BF16)

    def spread(b):
        depth = 3 * inner
        zero = jnp.zeros((depth, inner), BF16)
        for w, first, second in (
            ([ws[b, i].reshape(depth, inner) for i in range(3)], wa, wb),
            ([ws[b, :, i].reshape(depth, inner) for i in range(3)], wat, wbt),
        ):
            first[b] = jnp.concatenate(
                [jnp.concatenate([w[0], zero], axis=1), jnp.concatenate([w[1], w[0]], axis=1)],
                axis=0,
            )
            second[b] = jnp.concatenate(
                [jnp.concatenate([w[2], w[1]], axis=1), jnp.concatenate([zero, w[2]], axis=1)],
                axis=0,
            )

    def outer(b):
        n = chans // inner
        gain = jnp.concatenate([gb[b, 4 + i : 5 + i] for i in range(n)], axis=1)
        bias = jnp.concatenate([gb[b, 4 + n + i : 5 + n + i] for i in range(n)], axis=1)
        return gain, bias

    def edge_pixels(s, side):
        cells = img[s, :, :, side * (cols - 16) : side * (cols - 16) + 16]
        return cells.reshape(2 * pairs * 16, chans)

    def send_edges():
        meet(0, 2 * number(lambda j: j != 0), cols_ready)
        parts = []
        for s in range(slides):
            parts.append(
                [
                    jnp.dot(gather[side], edge_pixels(s, side), preferred_element_type=F32)
                    for side in range(2)
                ]
            )
            for side in range(2):
                col_send[side, s] = parts[s][side][0:16].astype(BF16)
            for way in range(2):
                cut = slice(16 + 8 * way, 24 + 8 * way)
                lines_send[way, s] = jnp.concatenate(
                    [parts[s][0][cut], parts[s][1][cut]], axis=0
                ).astype(BF16)
        for way in range(2):
            cut = slice(32 + 8 * way, 40 + 8 * way)
            for side in range(2):
                for t in range(2):
                    two = [parts[min(2 * t + i, slides - 1)][side][cut] for i in range(2)]
                    diag_send[way, side, t] = jnp.concatenate(two, axis=0).astype(BF16)
        for there, copy, _ in edge_sends():
            pl.when(there)(copy.start)

    def edge_strips():
        copies = list(edge_sends())
        for n, (there, _, here) in enumerate(copies):
            pl.when(there)(copies[mirror(n)][1].wait_recv)

            @pl.when(jnp.logical_not(there))
            def _():
                here[...] = jnp.zeros_like(here)

        strips = 2 * slides
        own_row = lax.broadcasted_iota(jnp.int32, (16, inner), 0)
        valid = jnp.where(
            own_row < 8,
            1.0,
            jnp.where(
                own_row < 14,
                jnp.where(row < n_row - 1, 1.0, 0.0),
                jnp.where(row > 0, 1.0, 0.0),
            ),
        )
        cells, masks = [], []
        for s in range(slides):
            for side in range(2):
                mine = edge_pixels(s, side)
                source = jnp.concatenate(
                    [
                        mine,
                        col_recv[side, s],
                        lines_recv[0, s],
                        lines_recv[1, s],
                        diag_recv[0, side, s // 2],
                        diag_recv[1, side, s // 2],
                        mine[0:48],
                    ],
                    axis=0,
                )
                k = 4 * side + 2 * (s % 2)
                pick = jnp.concatenate([window[k], window[k + 1]], axis=1)
                got = jnp.dot(pick, source, preferred_element_type=F32)
                cells.append(got.astype(BF16).reshape(1, 6, 16, chans))
                tiles = (2, 2, 2, 2, 3, 3) if side else (0, 0, 1, 1, 1, 1)
                masks.append([mk[s, t, 0:1] for t in tiles])
        x = jnp.concatenate(cells, axis=0)

        def mask_of(columns):
            return jnp.concatenate(
                [jnp.stack([m[w] * valid for w in columns])[None] for m in masks], axis=0
            )

        def reduced(e, x, columns):
            n = len(columns)
            v = jnp.dot(x.reshape(-1, chans), wr[e], preferred_element_type=F32)
            v = jnp.maximum(v * gb[e, 0:1] + gb[e, 2:3], 0.0)
            v = v.reshape(strips, n, 16, inner) * mask_of(columns)
            flat = v.reshape(strips * n, 16, inner)
            return jnp.concatenate(
                [
                    pltpu.roll(flat, 1, 1).astype(BF16),
                    flat.astype(BF16),
                    pltpu.roll(flat, 15, 1).astype(BF16),
                ],
                axis=2,
            ).reshape(strips, n, 16, 3 * inner)

        def conv(e, first, second):
            total = jnp.dot(first, wat[e], preferred_element_type=F32)
            total += jnp.dot(second, wbt[e], preferred_element_type=F32)
            gain, bias = widen(gb[e, 1:2], 2), widen(gb[e, 3:4], 2)
            return jnp.maximum(total * gain + bias, 0.0)

        def expanded(e, sp, h, mask):
            gain, bias = outer(e)
            z = jnp.dot(sp, we[e], preferred_element_type=F32).reshape(h.shape)
            z = jnp.maximum(z * gain + bias + h.astype(F32), 0.0)
            return z * mask

        r = reduced(0, x, range(6))
        two = [jnp.concatenate([r[:, 2 * i], r[:, 2 * i + 1]], axis=2)[:, None] for i in range(3)]
        sp = conv(
            0,
            jnp.concatenate(two[0:2], axis=1).reshape(-1, 6 * inner),
            jnp.concatenate(two[1:3], axis=1).reshape(-1, 6 * inner),
        ).astype(BF16)
        h, red = [], []
        for half in range(2):
            columns = (1 + half, 3 + half)
            before = jnp.concatenate([x[:, w][:, None] for w in columns], axis=1)
            mask = jnp.concatenate(
                [
                    jnp.stack([jnp.broadcast_to(widen(m[w], chans // inner), (16, chans)) for w in columns])[None]
                    for m in masks
                ],
                axis=0,
            )
            now = expanded(0, sp[:, half * inner : (half + 1) * inner], before, mask)
            h.append(now)
            red.append(reduced(1, now.astype(BF16), columns))
        first, second = (
            jnp.concatenate([red[0][:, i], red[1][:, i]], axis=2).reshape(-1, 6 * inner)
            for i in range(2)
        )
        sp = conv(1, first, second).reshape(strips, 16, 2 * inner)[:, 0:8]
        done = []
        for half in range(2):
            now = h[1 - half][:, half, 0:8].astype(BF16)
            mask = jnp.concatenate([widen(m[2 + half], chans // inner)[None] for m in masks], axis=0)
            z = sp[:, :, half * inner : (half + 1) * inner].reshape(strips * 8, inner)
            done.append(expanded(1, z.astype(BF16), now, mask)[:, None])
        done = jnp.concatenate(done, axis=1).reshape(strips * 16, chans).astype(BF16)
        done = jnp.concatenate([done, jnp.zeros((128 - strips * 16, chans), BF16)], axis=0)
        for i in range(strips):
            put = jnp.dot(scatter[i], done, preferred_element_type=F32).reshape(pairs, 2, 16, chans)
            fixed[i] = put.astype(BF16)

    turn = lax.rem(col, RUN)
    late, soon = turn == 0, turn == RUN - 1
    for load in own[9:]:
        load.wait()
    for s in range(slides):
        image_load(s).wait()
    pl.when(soon)(send_edges)

    own[0].wait()
    for copy in swaps[:2]:
        copy.wait()
    ends = (0, pairs - 1)
    between = tuple(range(1, pairs - 1))

    def place_pairs(e, group, reds):
        for p, red in zip(group, reds):
            for half in range(2):
                place_row(e, 2 * p + half, red[:, half])

    def reduce_ends(e, x):
        reds = [reduce_pair(e, x[:, p], p) for p in ends]
        for way in range(2):
            send_row(e, way, reds[way])
        place_pairs(e, ends, reds)

    def reduce_between(e, x):
        place_pairs(e, between, [reduce_pair(e, x[:, p], p) for p in between])

    reduce_ends(0, img)
    reduce_between(0, img)
    pl.when((turn > 0) & (turn < RUN - 1))(send_edges)

    for load in own[1:3]:
        load.wait()
    for copy in swaps[2:]:
        copy.wait()
    spread(0)
    spread(1)

    def expand_pairs(e, group, before, after):
        parts = [spatial(e, p) for p in group]
        for p, sp in zip(group, parts):
            expand(e, sp, p, before, after)

    expand_pairs(0, between, img, mid)
    reduce_between(1, mid)
    halo(0)
    expand_pairs(0, ends, img, mid)
    reduce_ends(1, mid)
    pl.when(late)(send_edges)
    expand_pairs(1, between, mid, out)
    edge_strips()
    halo(1)
    expand_pairs(1, ends, mid, out)
    for i in range(2 * slides):
        place = lax.broadcasted_iota(jnp.int32, (pairs, 2, 16, chans), 2)
        here = out.at[i // 2, :, :, i % 2 * (cols - 16) : i % 2 * (cols - 16) + 16]
        edges = place >= 14 if i % 2 else place < 2
        here[...] = jnp.where(edges, fixed[i].astype(F32), here[...].astype(F32)).astype(BF16)
    for there, copy, _ in edge_sends():
        pl.when(there)(copy.wait_send)

    for e in range(2):
        for there, copy in row_sends(e):
            pl.when(there)(copy.wait_send)


def write_kernel(held, out, sem):
    copies = [pltpu.make_async_copy(held.at[s], out.at[s], sem.at[s]) for s in range(held.shape[0])]
    for copy in copies:
        copy.start()
    for copy in copies:
        copy.wait()


def shards(grid, images, tissue_list, tissue_count, *weights):
    total, rows, cols, chans = images.shape
    slides, pairs = total // 2, rows // 2
    inner = weights[0].shape[2]
    w_reduce, w_spatial, w_expand, inner_gain, inner_bias, outer_gain, outer_bias = weights
    w_spatial = w_spatial.reshape(1, 3, 3, inner, inner)
    picks = [jnp.asarray(x) for x in selections(rows)]
    hbm = pl.BlockSpec(memory_space=pltpu.HBM)
    vmem = pl.BlockSpec(memory_space=pltpu.VMEM)
    dma = pltpu.SemaphoreType.DMA
    held = pl.pallas_call(
        functools.partial(blocks_kernel, grid),
        out_shape=pltpu.VMEM((slides, pairs, 2, cols, chans), BF16),
        in_specs=[hbm] * 13,
        out_specs=vmem,
        scratch_shapes=[
            *[pltpu.VMEM((slides, pairs, 2, cols, chans), BF16)] * 2,
            pltpu.VMEM(tissue_list.shape, jnp.int32),
            pltpu.SMEM(tissue_count.shape, jnp.int32),
            pltpu.VMEM(inner_gain.shape, BF16),
            pltpu.VMEM(inner_bias.shape, BF16),
            pltpu.VMEM(outer_gain.shape, BF16),
            pltpu.VMEM(outer_bias.shape, BF16),
            pltpu.VMEM((2, chans, inner), BF16),
            pltpu.VMEM((2, 3, 3, inner, inner), BF16),
            *[pltpu.VMEM((2, 6 * inner, 2 * inner), BF16)] * 4,
            pltpu.VMEM((2, inner, chans), BF16),
            pltpu.VMEM((2, 16, inner), F32),
            pltpu.VMEM((slides, cols // TW + 2, 8, inner), F32),
            pltpu.VMEM((2, slides, pairs + 1, cols, 6 * inner), BF16),
            *[pltpu.VMEM((2, 2, slides, cols, inner), BF16)] * 2,
            *[pltpu.VMEM(x.shape, BF16) for x in picks],
            *[pltpu.VMEM((2, slides, 16, chans), BF16)] * 4,
            *[pltpu.VMEM((2, 2, 2, 16, chans), BF16)] * 2,
            pltpu.VMEM((2 * slides, pairs, 2, 16, chans), BF16),
            pltpu.SemaphoreType.REGULAR,
            pltpu.SemaphoreType.REGULAR,
            dma((slides,)),
            dma((12,)),
            dma((8,)),
            dma((8,)),
            dma((4,)),
            dma((4,)),
            dma((2, 2)),
            dma((2, 2)),
        ],
        compiler_params=pltpu.CompilerParams(
            collective_id=0, has_side_effects=True, vmem_limit_bytes=40 * 2**20
        ),
        name="blocks",
    )(
        *(
            pltpu.with_memory_space_constraint(x, pltpu.HBM)
            for x in (
                images.reshape(total, pairs, 2, cols, chans),
                tissue_list,
                tissue_count,
                w_reduce,
                w_spatial,
                w_expand,
                inner_gain,
                inner_bias,
                outer_gain,
                outer_bias,
                *picks,
            )
        )
    )
    out = pl.pallas_call(
        write_kernel,
        out_shape=jax.ShapeDtypeStruct((slides, pairs, 2, cols, chans), BF16),
        in_specs=[vmem],
        out_specs=hbm,
        scratch_shapes=[dma((slides,))],
        compiler_params=pltpu.CompilerParams(vmem_limit_bytes=16 * 2**20),
        name="write",
    )(held)
    return out.reshape(slides, rows, cols, chans)


def solution(mesh):
    placed = (
        P(None, "row", "col", None),
        P(),
        P(),
        P("segment", None, None),
        P("segment", None, None, None, None),
        P("segment", None, None),
        P("segment", None, None),
        P("segment", None, None),
        P("segment", None),
        P("segment", None),
    )
    return jax.shard_map(
        functools.partial(shards, (mesh.shape["row"], mesh.shape["col"])),
        mesh=mesh,
        in_specs=placed,
        out_specs=P("segment", "row", "col", None),
        check_vma=False,
    )
```

```python
import functools

import jax
import jax.numpy as jnp
import ml_dtypes
import numpy as np
from jax import lax
from jax.experimental import pallas as pl
from jax.experimental.pallas import tpu as pltpu
from jax.sharding import PartitionSpec as P

MESH = pl.DeviceIdType.MESH
TW = 64
F32 = jnp.float32
BF16 = jnp.bfloat16
remote = pltpu.make_async_remote_copy


RUN = 8


def selections(rows):
    gather = np.zeros((2, 48, 128), np.float32)
    window = np.zeros((2, 2, 96, 256), np.float32)
    scatter = np.zeros((6, 128, 128), np.float32)
    for side in range(2):
        own = [12 * side + q for q in range(4)]
        outer = own[2:] if side else own[:2]
        for q in range(2):
            for r in range(rows):
                gather[side, q * 8 + r, r * 16 + outer[q]] = 1
            for t in range(2):
                gather[side, 32 + q * 2 + t, t * 16 + outer[q]] = 1
                gather[side, 40 + q * 2 + t, (rows - 2 + t) * 16 + outer[q]] = 1
        for q in range(4):
            for t in range(2):
                gather[side, 16 + q * 2 + t, t * 16 + own[q]] = 1
                gather[side, 24 + q * 2 + t, (rows - 2 + t) * 16 + own[q]] = 1
        for half in range(2):
            to = window[side, half]
            for q in range(4):
                w = (q if side else q + 2) * 16
                for r in range(rows):
                    to[w + r, r * 16 + own[q]] = 1
                for t in range(2):
                    to[w + 8 + t, 160 + side * 8 + q * 2 + t] = 1
                    to[w + 14 + t, 144 + side * 8 + q * 2 + t] = 1
            for q in range(2):
                w = (q + 4 if side else q) * 16
                for r in range(rows):
                    to[w + r, 128 + q * 8 + r] = 1
                for t in range(2):
                    to[w + 8 + t, 192 + half * 8 + q * 2 + t] = 1
                    to[w + 14 + t, 176 + half * 8 + q * 2 + t] = 1
        for s in range(3):
            strip = s * 2 + side
            for q in range(2):
                for r in range(rows):
                    scatter[strip, r * 16 + 14 * side + q, strip * 16 + q * 8 + r] = 1
    window = window.reshape(4, 96, 2, 128).swapaxes(1, 2)
    window = window.reshape(8, 96, 128)
    return [x.astype(ml_dtypes.bfloat16) for x in (gather, window, scatter)]


def widen(row, times):
    return jnp.concatenate([row] * times, axis=1)


def inside(i, n):
    return (i >= 0) & (i < n)


def blocks_kernel(
    grid,
    images,
    tissue_list,
    tissue_count,
    w_reduce,
    w_spatial,
    w_expand,
    inner_gain,
    inner_bias,
    outer_gain,
    outer_bias,
    gather_in,
    window_in,
    scatter_in,
    out,
    img,
    mid,
    listed,
    counts,
    ig,
    ib,
    og,
    ob,
    wr,
    ws,
    wa,
    wb,
    wat,
    wbt,
    we,
    gb,
    mk,
    rb,
    row_send,
    row_recv,
    gather,
    window,
    scatter,
    col_send,
    col_recv,
    lines_send,
    lines_recv,
    diag_send,
    diag_recv,
    fixed,
    rows_ready,
    cols_ready,
    img_sem,
    w_sem,
    edge_send_sem,
    edge_recv_sem,
    w_send_sem,
    w_recv_sem,
    send_sem,
    recv_sem,
):
    n_row, n_col = grid
    slides, pairs, _, cols, chans = img.shape
    inner = wr.shape[2]
    last = cols - 1
    seg = lax.axis_index("segment")
    row = lax.axis_index("row")
    col = lax.axis_index("col")
    peer = {"segment": 1 - seg}
    around = [
        (i, j, inside(row + i, n_row) & inside(col + j, n_col))
        for j in (0, -1, 1)
        for i in (-1, 1, 0)
        if i or j
    ]

    def at(i, j):
        return {"row": row + i, "col": col + j}

    barrier = pltpu.get_barrier_semaphore()

    def greet(other):
        pl.semaphore_signal(barrier, inc=1, device_id=other, device_id_type=MESH)

    pl.when(seg == 0)(functools.partial(greet, peer))
    for i, j, there in around:
        core = 1 if j == 0 else 0
        pl.when(there)(functools.partial(greet, {"segment": core, **at(i, j)}))

    def meet(core, count, ready):
        @pl.when(seg == core)
        def _():
            pl.semaphore_wait(barrier, count)
            pl.semaphore_signal(ready, inc=1, device_id=peer, device_id_type=MESH)

        @pl.when(seg != core)
        def _():
            pl.semaphore_wait(ready, 1)

    def number(pick):
        return sum((there.astype(jnp.int32) for _, j, there in around if pick(j)), 0)

    def image_load(s):
        return pltpu.make_async_copy(images.at[seg * slides + s], img.at[s], img_sem.at[s])

    own = [
        pltpu.make_async_copy(src, dst, w_sem.at[i])
        for i, (src, dst) in enumerate(
            (
                (w_reduce.at[0], wr.at[seg]),
                (w_spatial.at[0], ws.at[seg]),
                (w_expand.at[0], we.at[seg]),
                (inner_gain, ig),
                (inner_bias, ib),
                (outer_gain, og),
                (outer_bias, ob),
                (tissue_count, counts),
                (tissue_list, listed),
                (gather_in, gather),
                (window_in, window),
                (scatter_in, scatter),
            )
        )
    ]
    for load in own[3:9] + own[:1]:
        load.start()
    for s in range(slides):
        image_load(s).start()
    for load in own[1:3] + own[9:]:
        load.start()
    for load in own[3:9]:
        load.wait()

    lines = [ig[0].astype(F32), ib[0].astype(F32)]
    for whole in (og[...].astype(F32), ob[...].astype(F32)):
        lines += [whole[:, i * inner : (i + 1) * inner] for i in range(chans // inner)]
    lines.append(jnp.zeros((4, inner), F32))
    gb[seg] = jnp.concatenate(lines, axis=0)

    position = lax.broadcasted_iota(jnp.int32, (1, listed.shape[1]), 1)
    for s in range(slides):
        slide = seg * slides + s
        here = listed[pl.ds(slide, 1), :]
        for t in range(cols // TW + 2):
            tile = col * (cols // TW) + t - 1
            hit = (here == tile) & (position < counts[slide])
            one = jnp.max(jnp.where(hit, 1.0, 0.0), axis=1, keepdims=True)
            mk[s, t] = jnp.broadcast_to(one, mk.shape[2:])

    meet(1, 1 + 2 * number(lambda j: j == 0), rows_ready)

    def swap(src, dst, i):
        return remote(
            src_ref=src,
            dst_ref=dst.at[seg],
            send_sem=w_send_sem.at[i],
            recv_sem=w_recv_sem.at[i],
            device_id=peer,
            device_id_type=MESH,
        )

    swaps = [
        swap(w_reduce.at[0], wr, 0),
        swap(gb.at[seg], gb, 1),
        swap(w_spatial.at[0], ws, 2),
        swap(w_expand.at[0], we, 3),
    ]
    for copy in swaps:
        copy.start()

    def row_sends(e):
        for n, (i, j, there) in enumerate(around[:2]):
            yield there, remote(
                src_ref=row_send.at[e, n],
                dst_ref=row_recv.at[e, 1 - n],
                send_sem=send_sem.at[e, n],
                recv_sem=recv_sem.at[e, 1 - n],
                device_id=at(i, j),
                device_id_type=MESH,
            )

    def edge_sends():
        for n, (i, j, there) in enumerate(around):
            a, b = (1 + i) // 2, (1 + j) // 2
            if j == 0:
                src, dst, here = lines_send.at[a], lines_recv.at[1 - a], lines_recv.at[a]
            elif i == 0:
                src, dst, here = col_send.at[b], col_recv.at[1 - b], col_recv.at[b]
            else:
                src, dst = diag_send.at[a, b], diag_recv.at[1 - a, 1 - b]
                here = diag_recv.at[a, b]
            copy = remote(
                src_ref=src,
                dst_ref=dst,
                send_sem=edge_send_sem.at[n],
                recv_sem=edge_recv_sem.at[mirror(n)],
                device_id=at(i, j),
                device_id_type=MESH,
            )
            yield there, copy, here

    def mirror(n):
        i, j, _ = around[n]
        return [(a, b) for a, b, _ in around].index((-i, -j))

    def place_row(e, r, red):
        lane = (r + 1) % 2 * 3 * inner
        rb[e, :, (r + 1) // 2, :, lane : lane + 3 * inner] = jnp.concatenate(
            [
                pltpu.roll(red, 1, 1).astype(BF16),
                red.astype(BF16),
                pltpu.roll(red, last, 1).astype(BF16),
            ],
            axis=2,
        )

    def reduce_pair(e, x, p):
        v = jnp.dot(x.reshape(-1, chans), wr[e], preferred_element_type=F32)
        v = v.reshape(slides, 2, cols // TW, TW, inner)
        mask = mk[:, 1 : 1 + cols // TW, 0:1][:, None]
        red = jnp.maximum(v * (gb[e, 0:1] * mask) + gb[e, 2:3] * mask, 0.0)
        return red.reshape(slides, 2, cols, inner)

    def send_row(e, way, red):
        row_send[e, way] = red[:, way].astype(BF16)
        there, copy = list(row_sends(e))[way]
        pl.when(there)(copy.start)

    def halo(e):
        copies = list(row_sends(e))
        for n, (there, _) in enumerate(copies):
            pl.when(there)(copies[1 - n][1].wait_recv)
        for way, there, r in ((0, row > 0, -1), (1, row < n_row - 1, 2 * pairs)):
            place_row(e, r, jnp.where(there, row_recv[e, way].astype(F32), 0.0))

    def spatial(e, p):
        total = jnp.dot(rb[e, :, p].reshape(-1, 6 * inner), wa[e], preferred_element_type=F32)
        total += jnp.dot(rb[e, :, p + 1].reshape(-1, 6 * inner), wb[e], preferred_element_type=F32)
        gain, bias = widen(gb[e, 1:2], 2), widen(gb[e, 3:4], 2)
        return jnp.maximum(total * gain + bias, 0.0).astype(BF16)

    def expand(e, sp, p, before, after):
        gain, bias = outer(e)
        mask = mk[:, 1 : 1 + cols // TW, 0:1]
        mask = jnp.concatenate([mask] * (chans // inner), axis=3)
        for half in range(2):
            z = jnp.dot(
                sp[:, half * inner : (half + 1) * inner], we[e], preferred_element_type=F32
            ).reshape(slides, cols, chans)
            y = jnp.maximum(z * gain + bias + before[:, p, half].astype(F32), 0.0)
            y = y.reshape(slides, cols // TW, TW, chans) * mask
            after[:, p, half] = y.reshape(slides, cols, chans).astype(BF16)

    def spread(b):
        depth = 3 * inner
        zero = jnp.zeros((depth, inner), BF16)
        for w, first, second in (
            ([ws[b, i].reshape(depth, inner) for i in range(3)], wa, wb),
            ([ws[b, :, i].reshape(depth, inner) for i in range(3)], wat, wbt),
        ):
            first[b] = jnp.concatenate(
                [jnp.concatenate([w[0], zero], axis=1), jnp.concatenate([w[1], w[0]], axis=1)],
                axis=0,
            )
            second[b] = jnp.concatenate(
                [jnp.concatenate([w[2], w[1]], axis=1), jnp.concatenate([zero, w[2]], axis=1)],
                axis=0,
            )

    def outer(b):
        n = chans // inner
        gain = jnp.concatenate([gb[b, 4 + i : 5 + i] for i in range(n)], axis=1)
        bias = jnp.concatenate([gb[b, 4 + n + i : 5 + n + i] for i in range(n)], axis=1)
        return gain, bias

    def edge_pixels(s, side):
        cells = img[s, :, :, side * (cols - 16) : side * (cols - 16) + 16]
        return cells.reshape(2 * pairs * 16, chans)

    def send_edges():
        meet(0, 2 * number(lambda j: j != 0), cols_ready)
        parts = []
        for s in range(slides):
            parts.append(
                [
                    jnp.dot(gather[side], edge_pixels(s, side), preferred_element_type=F32)
                    for side in range(2)
                ]
            )
            for side in range(2):
                col_send[side, s] = parts[s][side][0:16].astype(BF16)
            for way in range(2):
                cut = slice(16 + 8 * way, 24 + 8 * way)
                lines_send[way, s] = jnp.concatenate(
                    [parts[s][0][cut], parts[s][1][cut]], axis=0
                ).astype(BF16)
        for way in range(2):
            cut = slice(32 + 8 * way, 40 + 8 * way)
            for side in range(2):
                for t in range(2):
                    two = [parts[min(2 * t + i, slides - 1)][side][cut] for i in range(2)]
                    diag_send[way, side, t] = jnp.concatenate(two, axis=0).astype(BF16)
        for there, copy, _ in edge_sends():
            pl.when(there)(copy.start)

    def edge_wait():
        copies = list(edge_sends())
        for n, (there, _, here) in enumerate(copies):
            pl.when(there)(copies[mirror(n)][1].wait_recv)

            @pl.when(jnp.logical_not(there))
            def _():
                here[...] = jnp.zeros_like(here)

    def edge_strips():
        strips = 2 * slides
        own_row = lax.broadcasted_iota(jnp.int32, (16, inner), 0)
        valid = jnp.where(
            own_row < 8,
            1.0,
            jnp.where(
                own_row < 14,
                jnp.where(row < n_row - 1, 1.0, 0.0),
                jnp.where(row > 0, 1.0, 0.0),
            ),
        )
        cells, masks = [], []
        for s in range(slides):
            for side in range(2):
                mine = edge_pixels(s, side)
                source = jnp.concatenate(
                    [
                        mine,
                        col_recv[side, s],
                        lines_recv[0, s],
                        lines_recv[1, s],
                        diag_recv[0, side, s // 2],
                        diag_recv[1, side, s // 2],
                        mine[0:48],
                    ],
                    axis=0,
                )
                k = 4 * side + 2 * (s % 2)
                pick = jnp.concatenate([window[k], window[k + 1]], axis=1)
                got = jnp.dot(pick, source, preferred_element_type=F32)
                cells.append(got.astype(BF16).reshape(1, 6, 16, chans))
                tiles = (2, 2, 2, 2, 3, 3) if side else (0, 0, 1, 1, 1, 1)
                masks.append([mk[s, t, 0:1] for t in tiles])
        x = jnp.concatenate(cells, axis=0)

        def mask_of(columns):
            return jnp.concatenate(
                [jnp.stack([m[w] * valid for w in columns])[None] for m in masks], axis=0
            )

        def reduced(e, x, columns):
            n = len(columns)
            v = jnp.dot(x.reshape(-1, chans), wr[e], preferred_element_type=F32)
            v = jnp.maximum(v * gb[e, 0:1] + gb[e, 2:3], 0.0)
            v = v.reshape(strips, n, 16, inner) * mask_of(columns)
            flat = v.reshape(strips * n, 16, inner)
            return jnp.concatenate(
                [
                    pltpu.roll(flat, 1, 1).astype(BF16),
                    flat.astype(BF16),
                    pltpu.roll(flat, 15, 1).astype(BF16),
                ],
                axis=2,
            ).reshape(strips, n, 16, 3 * inner)

        def conv(e, first, second):
            total = jnp.dot(first, wat[e], preferred_element_type=F32)
            total += jnp.dot(second, wbt[e], preferred_element_type=F32)
            gain, bias = widen(gb[e, 1:2], 2), widen(gb[e, 3:4], 2)
            return jnp.maximum(total * gain + bias, 0.0)

        def expanded(e, sp, h, mask):
            gain, bias = outer(e)
            z = jnp.dot(sp, we[e], preferred_element_type=F32).reshape(h.shape)
            z = jnp.maximum(z * gain + bias + h.astype(F32), 0.0)
            return z * mask

        r = reduced(0, x, range(6))
        two = [jnp.concatenate([r[:, 2 * i], r[:, 2 * i + 1]], axis=2)[:, None] for i in range(3)]
        sp = conv(
            0,
            jnp.concatenate(two[0:2], axis=1).reshape(-1, 6 * inner),
            jnp.concatenate(two[1:3], axis=1).reshape(-1, 6 * inner),
        ).astype(BF16)
        h, red = [], []
        for half in range(2):
            columns = (1 + half, 3 + half)
            before = jnp.concatenate([x[:, w][:, None] for w in columns], axis=1)
            mask = jnp.concatenate(
                [
                    jnp.stack([jnp.broadcast_to(widen(m[w], chans // inner), (16, chans)) for w in columns])[None]
                    for m in masks
                ],
                axis=0,
            )
            now = expanded(0, sp[:, half * inner : (half + 1) * inner], before, mask)
            h.append(now)
            red.append(reduced(1, now.astype(BF16), columns))
        first, second = (
            jnp.concatenate([red[0][:, i], red[1][:, i]], axis=2).reshape(-1, 6 * inner)
            for i in range(2)
        )
        sp = conv(1, first, second).reshape(strips, 16, 2 * inner)[:, 0:8]
        done = []
        for half in range(2):
            now = h[1 - half][:, half, 0:8].astype(BF16)
            mask = jnp.concatenate([widen(m[2 + half], chans // inner)[None] for m in masks], axis=0)
            z = sp[:, :, half * inner : (half + 1) * inner].reshape(strips * 8, inner)
            done.append(expanded(1, z.astype(BF16), now, mask)[:, None])
        done = jnp.concatenate(done, axis=1).reshape(strips * 16, chans).astype(BF16)
        done = jnp.concatenate([done, jnp.zeros((128 - strips * 16, chans), BF16)], axis=0)
        for i in range(strips):
            put = jnp.dot(scatter[i], done, preferred_element_type=F32).reshape(pairs, 2, 16, chans)
            fixed[i] = put.astype(BF16)

    turn = lax.rem(col, RUN)
    late, soon = turn == 0, turn == RUN - 1
    for load in own[9:]:
        load.wait()
    for s in range(slides):
        image_load(s).wait()
    pl.when(soon)(send_edges)

    own[0].wait()
    for copy in swaps[:2]:
        copy.wait()
    ends = (0, pairs - 1)
    between = tuple(range(1, pairs - 1))

    def place_pairs(e, group, reds):
        for p, red in zip(group, reds):
            for half in range(2):
                place_row(e, 2 * p + half, red[:, half])

    def reduce_ends(e, x):
        reds = [reduce_pair(e, x[:, p], p) for p in ends]
        for way in range(2):
            send_row(e, way, reds[way])
        place_pairs(e, ends, reds)

    def reduce_between(e, x):
        place_pairs(e, between, [reduce_pair(e, x[:, p], p) for p in between])

    reduce_ends(0, img)
    reduce_between(0, img)
    pl.when((turn > 0) & (turn < RUN - 1))(send_edges)

    for load in own[1:3]:
        load.wait()
    for copy in swaps[2:]:
        copy.wait()
    spread(0)
    spread(1)

    def expand_pairs(e, group, before, after):
        parts = [spatial(e, p) for p in group]
        for p, sp in zip(group, parts):
            expand(e, sp, p, before, after)

    expand_pairs(0, between, img, mid)
    reduce_between(1, mid)
    halo(0)
    expand_pairs(0, ends, img, mid)
    reduce_ends(1, mid)
    pl.when(late)(send_edges)
    expand_pairs(1, between, mid, out)

    @pl.when(jnp.logical_not(late))
    def _():
        edge_wait()
        edge_strips()

    halo(1)
    expand_pairs(1, ends, mid, out)

    @pl.when(late)
    def _():
        edge_wait()
        edge_strips()

    for i in range(2 * slides):
        place = lax.broadcasted_iota(jnp.int32, (pairs, 2, 16, chans), 2)
        here = out.at[i // 2, :, :, i % 2 * (cols - 16) : i % 2 * (cols - 16) + 16]
        edges = place >= 14 if i % 2 else place < 2
        here[...] = jnp.where(edges, fixed[i].astype(F32), here[...].astype(F32)).astype(BF16)
    for there, copy, _ in edge_sends():
        pl.when(there)(copy.wait_send)

    for e in range(2):
        for there, copy in row_sends(e):
            pl.when(there)(copy.wait_send)


def write_kernel(held, out, sem):
    copies = [pltpu.make_async_copy(held.at[s], out.at[s], sem.at[s]) for s in range(held.shape[0])]
    for copy in copies:
        copy.start()
    for copy in copies:
        copy.wait()


def shards(grid, images, tissue_list, tissue_count, *weights):
    total, rows, cols, chans = images.shape
    slides, pairs = total // 2, rows // 2
    inner = weights[0].shape[2]
    w_reduce, w_spatial, w_expand, inner_gain, inner_bias, outer_gain, outer_bias = weights
    w_spatial = w_spatial.reshape(1, 3, 3, inner, inner)
    picks = [jnp.asarray(x) for x in selections(rows)]
    hbm = pl.BlockSpec(memory_space=pltpu.HBM)
    vmem = pl.BlockSpec(memory_space=pltpu.VMEM)
    dma = pltpu.SemaphoreType.DMA
    held = pl.pallas_call(
        functools.partial(blocks_kernel, grid),
        out_shape=pltpu.VMEM((slides, pairs, 2, cols, chans), BF16),
        in_specs=[hbm] * 13,
        out_specs=vmem,
        scratch_shapes=[
            *[pltpu.VMEM((slides, pairs, 2, cols, chans), BF16)] * 2,
            pltpu.VMEM(tissue_list.shape, jnp.int32),
            pltpu.SMEM(tissue_count.shape, jnp.int32),
            pltpu.VMEM(inner_gain.shape, BF16),
            pltpu.VMEM(inner_bias.shape, BF16),
            pltpu.VMEM(outer_gain.shape, BF16),
            pltpu.VMEM(outer_bias.shape, BF16),
            pltpu.VMEM((2, chans, inner), BF16),
            pltpu.VMEM((2, 3, 3, inner, inner), BF16),
            *[pltpu.VMEM((2, 6 * inner, 2 * inner), BF16)] * 4,
            pltpu.VMEM((2, inner, chans), BF16),
            pltpu.VMEM((2, 16, inner), F32),
            pltpu.VMEM((slides, cols // TW + 2, 8, inner), F32),
            pltpu.VMEM((2, slides, pairs + 1, cols, 6 * inner), BF16),
            *[pltpu.VMEM((2, 2, slides, cols, inner), BF16)] * 2,
            *[pltpu.VMEM(x.shape, BF16) for x in picks],
            *[pltpu.VMEM((2, slides, 16, chans), BF16)] * 4,
            *[pltpu.VMEM((2, 2, 2, 16, chans), BF16)] * 2,
            pltpu.VMEM((2 * slides, pairs, 2, 16, chans), BF16),
            pltpu.SemaphoreType.REGULAR,
            pltpu.SemaphoreType.REGULAR,
            dma((slides,)),
            dma((12,)),
            dma((8,)),
            dma((8,)),
            dma((4,)),
            dma((4,)),
            dma((2, 2)),
            dma((2, 2)),
        ],
        compiler_params=pltpu.CompilerParams(
            collective_id=0, has_side_effects=True, vmem_limit_bytes=40 * 2**20
        ),
        name="blocks",
    )(
        *(
            pltpu.with_memory_space_constraint(x, pltpu.HBM)
            for x in (
                images.reshape(total, pairs, 2, cols, chans),
                tissue_list,
                tissue_count,
                w_reduce,
                w_spatial,
                w_expand,
                inner_gain,
                inner_bias,
                outer_gain,
                outer_bias,
                *picks,
            )
        )
    )
    out = pl.pallas_call(
        write_kernel,
        out_shape=jax.ShapeDtypeStruct((slides, pairs, 2, cols, chans), BF16),
        in_specs=[vmem],
        out_specs=hbm,
        scratch_shapes=[dma((slides,))],
        compiler_params=pltpu.CompilerParams(vmem_limit_bytes=16 * 2**20),
        name="write",
    )(held)
    return out.reshape(slides, rows, cols, chans)


def solution(mesh):
    placed = (
        P(None, "row", "col", None),
        P(),
        P(),
        P("segment", None, None),
        P("segment", None, None, None, None),
        P("segment", None, None),
        P("segment", None, None),
        P("segment", None, None),
        P("segment", None),
        P("segment", None),
    )
    return jax.shard_map(
        functools.partial(shards, (mesh.shape["row"], mesh.shape["col"])),
        mesh=mesh,
        in_specs=placed,
        out_specs=P("segment", "row", "col", None),
        check_vma=False,
    )
```

```python
import functools

import jax
import jax.numpy as jnp
import ml_dtypes
import numpy as np
from jax import lax
from jax.experimental import pallas as pl
from jax.experimental.pallas import tpu as pltpu
from jax.sharding import PartitionSpec as P

MESH = pl.DeviceIdType.MESH
TW = 64
F32 = jnp.float32
BF16 = jnp.bfloat16
remote = pltpu.make_async_remote_copy


RUN = 8


def selections(rows):
    gather = np.zeros((2, 48, 128), np.float32)
    window = np.zeros((2, 2, 96, 256), np.float32)
    scatter = np.zeros((6, 128, 128), np.float32)
    for side in range(2):
        own = [12 * side + q for q in range(4)]
        outer = own[2:] if side else own[:2]
        for q in range(2):
            for r in range(rows):
                gather[side, q * 8 + r, r * 16 + outer[q]] = 1
            for t in range(2):
                gather[side, 32 + q * 2 + t, t * 16 + outer[q]] = 1
                gather[side, 40 + q * 2 + t, (rows - 2 + t) * 16 + outer[q]] = 1
        for q in range(4):
            for t in range(2):
                gather[side, 16 + q * 2 + t, t * 16 + own[q]] = 1
                gather[side, 24 + q * 2 + t, (rows - 2 + t) * 16 + own[q]] = 1
        for half in range(2):
            to = window[side, half]
            for q in range(4):
                w = (q if side else q + 2) * 16
                for r in range(rows):
                    to[w + r, r * 16 + own[q]] = 1
                for t in range(2):
                    to[w + 8 + t, 160 + side * 8 + q * 2 + t] = 1
                    to[w + 14 + t, 144 + side * 8 + q * 2 + t] = 1
            for q in range(2):
                w = (q + 4 if side else q) * 16
                for r in range(rows):
                    to[w + r, 128 + q * 8 + r] = 1
                for t in range(2):
                    to[w + 8 + t, 192 + half * 8 + q * 2 + t] = 1
                    to[w + 14 + t, 176 + half * 8 + q * 2 + t] = 1
        for s in range(3):
            strip = s * 2 + side
            for q in range(2):
                for r in range(rows):
                    scatter[strip, r * 16 + 14 * side + q, strip * 16 + q * 8 + r] = 1
    window = window.reshape(4, 96, 2, 128).swapaxes(1, 2)
    window = window.reshape(8, 96, 128)
    return [x.astype(ml_dtypes.bfloat16) for x in (gather, window, scatter)]


def widen(row, times):
    return jnp.concatenate([row] * times, axis=1)


def inside(i, n):
    return (i >= 0) & (i < n)


def blocks_kernel(
    grid,
    images,
    tissue_list,
    tissue_count,
    w_reduce,
    w_spatial,
    w_expand,
    inner_gain,
    inner_bias,
    outer_gain,
    outer_bias,
    gather_in,
    window_in,
    scatter_in,
    out,
    img,
    mid,
    listed,
    counts,
    ig,
    ib,
    og,
    ob,
    wr,
    ws,
    wa,
    wb,
    wat,
    wbt,
    we,
    gb,
    mk,
    rb,
    row_send,
    row_recv,
    gather,
    window,
    scatter,
    col_send,
    col_recv,
    lines_send,
    lines_recv,
    diag_send,
    diag_recv,
    fixed,
    rows_ready,
    cols_ready,
    img_sem,
    w_sem,
    edge_send_sem,
    edge_recv_sem,
    w_send_sem,
    w_recv_sem,
    send_sem,
    recv_sem,
):
    n_row, n_col = grid
    slides, pairs, _, cols, chans = img.shape
    inner = wr.shape[2]
    last = cols - 1
    seg = lax.axis_index("segment")
    row = lax.axis_index("row")
    col = lax.axis_index("col")
    peer = {"segment": 1 - seg}
    around = [
        (i, j, inside(row + i, n_row) & inside(col + j, n_col))
        for j in (0, -1, 1)
        for i in (-1, 1, 0)
        if i or j
    ]

    def at(i, j):
        return {"row": row + i, "col": col + j}

    barrier = pltpu.get_barrier_semaphore()

    def greet(other):
        pl.semaphore_signal(barrier, inc=1, device_id=other, device_id_type=MESH)

    pl.when(seg == 0)(functools.partial(greet, peer))
    for i, j, there in around:
        core = 1 if j == 0 else 0
        pl.when(there)(functools.partial(greet, {"segment": core, **at(i, j)}))

    def meet(core, count, ready):
        @pl.when(seg == core)
        def _():
            pl.semaphore_wait(barrier, count)
            pl.semaphore_signal(ready, inc=1, device_id=peer, device_id_type=MESH)

        @pl.when(seg != core)
        def _():
            pl.semaphore_wait(ready, 1)

    def number(pick):
        return sum((there.astype(jnp.int32) for _, j, there in around if pick(j)), 0)

    def image_load(s):
        return pltpu.make_async_copy(images.at[seg * slides + s], img.at[s], img_sem.at[s])

    own = [
        pltpu.make_async_copy(src, dst, w_sem.at[i])
        for i, (src, dst) in enumerate(
            (
                (w_reduce.at[0], wr.at[seg]),
                (w_spatial.at[0], ws.at[seg]),
                (w_expand.at[0], we.at[seg]),
                (inner_gain, ig),
                (inner_bias, ib),
                (outer_gain, og),
                (outer_bias, ob),
                (tissue_count, counts),
                (tissue_list, listed),
                (gather_in, gather),
                (window_in, window),
                (scatter_in, scatter),
            )
        )
    ]
    for load in own[3:9] + own[:1]:
        load.start()
    for s in range(slides):
        image_load(s).start()
    for load in own[1:3] + own[9:]:
        load.start()
    for load in own[3:9]:
        load.wait()

    lines = [ig[0].astype(F32), ib[0].astype(F32)]
    for whole in (og[...].astype(F32), ob[...].astype(F32)):
        lines += [whole[:, i * inner : (i + 1) * inner] for i in range(chans // inner)]
    lines.append(jnp.zeros((4, inner), F32))
    gb[seg] = jnp.concatenate(lines, axis=0)

    position = lax.broadcasted_iota(jnp.int32, (1, listed.shape[1]), 1)
    for s in range(slides):
        slide = seg * slides + s
        here = listed[pl.ds(slide, 1), :]
        for t in range(cols // TW + 2):
            tile = col * (cols // TW) + t - 1
            hit = (here == tile) & (position < counts[slide])
            one = jnp.max(jnp.where(hit, 1.0, 0.0), axis=1, keepdims=True)
            mk[s, t] = jnp.broadcast_to(one, mk.shape[2:])

    meet(1, 1 + 2 * number(lambda j: j == 0), rows_ready)

    def swap(src, dst, i):
        return remote(
            src_ref=src,
            dst_ref=dst.at[seg],
            send_sem=w_send_sem.at[i],
            recv_sem=w_recv_sem.at[i],
            device_id=peer,
            device_id_type=MESH,
        )

    swaps = [
        swap(w_reduce.at[0], wr, 0),
        swap(gb.at[seg], gb, 1),
        swap(w_spatial.at[0], ws, 2),
        swap(w_expand.at[0], we, 3),
    ]
    for copy in swaps:
        copy.start()

    def row_sends(e):
        for n, (i, j, there) in enumerate(around[:2]):
            yield there, remote(
                src_ref=row_send.at[e, n],
                dst_ref=row_recv.at[e, 1 - n],
                send_sem=send_sem.at[e, n],
                recv_sem=recv_sem.at[e, 1 - n],
                device_id=at(i, j),
                device_id_type=MESH,
            )

    def edge_sends():
        for n, (i, j, there) in enumerate(around):
            a, b = (1 + i) // 2, (1 + j) // 2
            if j == 0:
                src, dst, here = lines_send.at[a], lines_recv.at[1 - a], lines_recv.at[a]
            elif i == 0:
                src, dst, here = col_send.at[b], col_recv.at[1 - b], col_recv.at[b]
            else:
                src, dst = diag_send.at[a, b], diag_recv.at[1 - a, 1 - b]
                here = diag_recv.at[a, b]
            copy = remote(
                src_ref=src,
                dst_ref=dst,
                send_sem=edge_send_sem.at[n],
                recv_sem=edge_recv_sem.at[mirror(n)],
                device_id=at(i, j),
                device_id_type=MESH,
            )
            yield there, copy, here

    def mirror(n):
        i, j, _ = around[n]
        return [(a, b) for a, b, _ in around].index((-i, -j))

    def place_row(e, r, red):
        lane = (r + 1) % 2 * 3 * inner
        rb[e, :, (r + 1) // 2, :, lane : lane + 3 * inner] = jnp.concatenate(
            [
                pltpu.roll(red, 1, 1).astype(BF16),
                red.astype(BF16),
                pltpu.roll(red, last, 1).astype(BF16),
            ],
            axis=2,
        )

    def reduce_pair(e, x, p):
        v = jnp.dot(x.reshape(-1, chans), wr[e], preferred_element_type=F32)
        v = v.reshape(slides, 2, cols // TW, TW, inner)
        mask = mk[:, 1 : 1 + cols // TW, 0:1][:, None]
        red = jnp.maximum(v * (gb[e, 0:1] * mask) + gb[e, 2:3] * mask, 0.0)
        return red.reshape(slides, 2, cols, inner)

    def send_row(e, way, red):
        row_send[e, way] = red[:, way].astype(BF16)
        there, copy = list(row_sends(e))[way]
        pl.when(there)(copy.start)

    def halo(e):
        copies = list(row_sends(e))
        for n, (there, _) in enumerate(copies):
            pl.when(there)(copies[1 - n][1].wait_recv)
        for way, there, r in ((0, row > 0, -1), (1, row < n_row - 1, 2 * pairs)):
            place_row(e, r, jnp.where(there, row_recv[e, way].astype(F32), 0.0))

    def spatial(e, p):
        total = jnp.dot(rb[e, :, p].reshape(-1, 6 * inner), wa[e], preferred_element_type=F32)
        total += jnp.dot(rb[e, :, p + 1].reshape(-1, 6 * inner), wb[e], preferred_element_type=F32)
        gain, bias = widen(gb[e, 1:2], 2), widen(gb[e, 3:4], 2)
        return jnp.maximum(total * gain + bias, 0.0).astype(BF16)

    def expand(e, sp, p, before, after):
        gain, bias = outer(e)
        mask = mk[:, 1 : 1 + cols // TW, 0:1]
        mask = jnp.concatenate([mask] * (chans // inner), axis=3)
        for half in range(2):
            z = jnp.dot(
                sp[:, half * inner : (half + 1) * inner], we[e], preferred_element_type=F32
            ).reshape(slides, cols, chans)
            y = jnp.maximum(z * gain + bias + before[:, p, half].astype(F32), 0.0)
            y = y.reshape(slides, cols // TW, TW, chans) * mask
            after[:, p, half] = y.reshape(slides, cols, chans).astype(BF16)

    def spread(b):
        depth = 3 * inner
        zero = jnp.zeros((depth, inner), BF16)
        for w, first, second in (
            ([ws[b, i].reshape(depth, inner) for i in range(3)], wa, wb),
            ([ws[b, :, i].reshape(depth, inner) for i in range(3)], wat, wbt),
        ):
            first[b] = jnp.concatenate(
                [jnp.concatenate([w[0], zero], axis=1), jnp.concatenate([w[1], w[0]], axis=1)],
                axis=0,
            )
            second[b] = jnp.concatenate(
                [jnp.concatenate([w[2], w[1]], axis=1), jnp.concatenate([zero, w[2]], axis=1)],
                axis=0,
            )

    def outer(b):
        n = chans // inner
        gain = jnp.concatenate([gb[b, 4 + i : 5 + i] for i in range(n)], axis=1)
        bias = jnp.concatenate([gb[b, 4 + n + i : 5 + n + i] for i in range(n)], axis=1)
        return gain, bias

    def edge_pixels(s, side):
        cells = img[s, :, :, side * (cols - 16) : side * (cols - 16) + 16]
        return cells.reshape(2 * pairs * 16, chans)

    def send_edges():
        meet(0, 2 * number(lambda j: j != 0), cols_ready)
        parts = []
        for s in range(slides):
            parts.append(
                [
                    jnp.dot(gather[side], edge_pixels(s, side), preferred_element_type=F32)
                    for side in range(2)
                ]
            )
            for side in range(2):
                col_send[side, s] = parts[s][side][0:16].astype(BF16)
            for way in range(2):
                cut = slice(16 + 8 * way, 24 + 8 * way)
                lines_send[way, s] = jnp.concatenate(
                    [parts[s][0][cut], parts[s][1][cut]], axis=0
                ).astype(BF16)
        for way in range(2):
            cut = slice(32 + 8 * way, 40 + 8 * way)
            for side in range(2):
                for t in range(2):
                    two = [parts[min(2 * t + i, slides - 1)][side][cut] for i in range(2)]
                    diag_send[way, side, t] = jnp.concatenate(two, axis=0).astype(BF16)
        for there, copy, _ in edge_sends():
            pl.when(there)(copy.start)

    def edge_wait():
        copies = list(edge_sends())
        for n, (there, _, here) in enumerate(copies):
            pl.when(there)(copies[mirror(n)][1].wait_recv)

            @pl.when(jnp.logical_not(there))
            def _():
                here[...] = jnp.zeros_like(here)

    def edge_strips():
        strips = 2 * slides
        own_row = lax.broadcasted_iota(jnp.int32, (16, inner), 0)
        valid = jnp.where(
            own_row < 8,
            1.0,
            jnp.where(
                own_row < 14,
                jnp.where(row < n_row - 1, 1.0, 0.0),
                jnp.where(row > 0, 1.0, 0.0),
            ),
        )
        cells, masks = [], []
        for s in range(slides):
            for side in range(2):
                mine = edge_pixels(s, side)
                source = jnp.concatenate(
                    [
                        mine,
                        col_recv[side, s],
                        lines_recv[0, s],
                        lines_recv[1, s],
                        diag_recv[0, side, s // 2],
                        diag_recv[1, side, s // 2],
                        mine[0:48],
                    ],
                    axis=0,
                )
                k = 4 * side + 2 * (s % 2)
                pick = jnp.concatenate([window[k], window[k + 1]], axis=1)
                got = jnp.dot(pick, source, preferred_element_type=F32)
                cells.append(got.astype(BF16).reshape(1, 6, 16, chans))
                tiles = (2, 2, 2, 2, 3, 3) if side else (0, 0, 1, 1, 1, 1)
                masks.append([mk[s, t, 0:1] for t in tiles])
        x = jnp.concatenate(cells, axis=0)

        def mask_of(columns):
            return jnp.concatenate(
                [jnp.stack([m[w] * valid for w in columns])[None] for m in masks], axis=0
            )

        def reduced(e, x, columns):
            n = len(columns)
            v = jnp.dot(x.reshape(-1, chans), wr[e], preferred_element_type=F32)
            v = jnp.maximum(v * gb[e, 0:1] + gb[e, 2:3], 0.0)
            v = v.reshape(strips, n, 16, inner) * mask_of(columns)
            flat = v.reshape(strips * n, 16, inner)
            return jnp.concatenate(
                [
                    pltpu.roll(flat, 1, 1).astype(BF16),
                    flat.astype(BF16),
                    pltpu.roll(flat, 15, 1).astype(BF16),
                ],
                axis=2,
            ).reshape(strips, n, 16, 3 * inner)

        def conv(e, first, second):
            total = jnp.dot(first, wat[e], preferred_element_type=F32)
            total += jnp.dot(second, wbt[e], preferred_element_type=F32)
            gain, bias = widen(gb[e, 1:2], 2), widen(gb[e, 3:4], 2)
            return jnp.maximum(total * gain + bias, 0.0)

        def expanded(e, sp, h, mask):
            gain, bias = outer(e)
            z = jnp.dot(sp, we[e], preferred_element_type=F32).reshape(h.shape)
            z = jnp.maximum(z * gain + bias + h.astype(F32), 0.0)
            return z * mask

        r = reduced(0, x, range(6))
        two = [jnp.concatenate([r[:, 2 * i], r[:, 2 * i + 1]], axis=2)[:, None] for i in range(3)]
        sp = conv(
            0,
            jnp.concatenate(two[0:2], axis=1).reshape(-1, 6 * inner),
            jnp.concatenate(two[1:3], axis=1).reshape(-1, 6 * inner),
        ).astype(BF16)
        h, red = [], []
        for half in range(2):
            columns = (1 + half, 3 + half)
            before = jnp.concatenate([x[:, w][:, None] for w in columns], axis=1)
            mask = jnp.concatenate(
                [
                    jnp.stack([jnp.broadcast_to(widen(m[w], chans // inner), (16, chans)) for w in columns])[None]
                    for m in masks
                ],
                axis=0,
            )
            now = expanded(0, sp[:, half * inner : (half + 1) * inner], before, mask)
            h.append(now)
            red.append(reduced(1, now.astype(BF16), columns))
        first, second = (
            jnp.concatenate([red[0][:, i], red[1][:, i]], axis=2).reshape(-1, 6 * inner)
            for i in range(2)
        )
        sp = conv(1, first, second).reshape(strips, 16, 2 * inner)[:, 0:8]
        done = []
        for half in range(2):
            now = h[1 - half][:, half, 0:8].astype(BF16)
            mask = jnp.concatenate([widen(m[2 + half], chans // inner)[None] for m in masks], axis=0)
            z = sp[:, :, half * inner : (half + 1) * inner].reshape(strips * 8, inner)
            done.append(expanded(1, z.astype(BF16), now, mask)[:, None])
        done = jnp.concatenate(done, axis=1).reshape(strips * 16, chans).astype(BF16)
        done = jnp.concatenate([done, jnp.zeros((128 - strips * 16, chans), BF16)], axis=0)
        for i in range(strips):
            put = jnp.dot(scatter[i], done, preferred_element_type=F32).reshape(pairs, 2, 16, chans)
            fixed[i] = put.astype(BF16)

    turn = lax.rem(col, RUN)
    late, soon = turn == 0, turn == RUN - 1
    for load in own[9:]:
        load.wait()
    for s in range(slides):
        image_load(s).wait()

    own[0].wait()
    for copy in swaps[:2]:
        copy.wait()
    ends = (0, pairs - 1)
    between = tuple(range(1, pairs - 1))

    def place_pairs(e, group, reds):
        for p, red in zip(group, reds):
            for half in range(2):
                place_row(e, 2 * p + half, red[:, half])

    def reduce_ends(e, x):
        reds = [reduce_pair(e, x[:, p], p) for p in ends]
        for way in range(2):
            send_row(e, way, reds[way])
        place_pairs(e, ends, reds)

    def reduce_between(e, x):
        place_pairs(e, between, [reduce_pair(e, x[:, p], p) for p in between])

    reduce_ends(0, img)
    reduce_between(0, img)
    pl.when(soon)(send_edges)

    for load in own[1:3]:
        load.wait()
    for copy in swaps[2:]:
        copy.wait()
    spread(0)
    spread(1)

    def expand_pairs(e, group, before, after):
        parts = [spatial(e, p) for p in group]
        for p, sp in zip(group, parts):
            expand(e, sp, p, before, after)

    expand_pairs(0, between, img, mid)
    pl.when((turn > 0) & (turn < RUN - 1))(send_edges)
    reduce_between(1, mid)
    halo(0)
    expand_pairs(0, ends, img, mid)
    reduce_ends(1, mid)
    pl.when(late)(send_edges)
    expand_pairs(1, between, mid, out)

    @pl.when(jnp.logical_not(late))
    def _():
        edge_wait()
        edge_strips()

    halo(1)
    expand_pairs(1, ends, mid, out)

    @pl.when(late)
    def _():
        edge_wait()
        edge_strips()

    for i in range(2 * slides):
        place = lax.broadcasted_iota(jnp.int32, (pairs, 2, 16, chans), 2)
        here = out.at[i // 2, :, :, i % 2 * (cols - 16) : i % 2 * (cols - 16) + 16]
        edges = place >= 14 if i % 2 else place < 2
        here[...] = jnp.where(edges, fixed[i].astype(F32), here[...].astype(F32)).astype(BF16)
    for there, copy, _ in edge_sends():
        pl.when(there)(copy.wait_send)

    for e in range(2):
        for there, copy in row_sends(e):
            pl.when(there)(copy.wait_send)


def write_kernel(held, out, sem):
    copies = [pltpu.make_async_copy(held.at[s], out.at[s], sem.at[s]) for s in range(held.shape[0])]
    for copy in copies:
        copy.start()
    for copy in copies:
        copy.wait()


def shards(grid, images, tissue_list, tissue_count, *weights):
    total, rows, cols, chans = images.shape
    slides, pairs = total // 2, rows // 2
    inner = weights[0].shape[2]
    w_reduce, w_spatial, w_expand, inner_gain, inner_bias, outer_gain, outer_bias = weights
    w_spatial = w_spatial.reshape(1, 3, 3, inner, inner)
    picks = [jnp.asarray(x) for x in selections(rows)]
    hbm = pl.BlockSpec(memory_space=pltpu.HBM)
    vmem = pl.BlockSpec(memory_space=pltpu.VMEM)
    dma = pltpu.SemaphoreType.DMA
    held = pl.pallas_call(
        functools.partial(blocks_kernel, grid),
        out_shape=pltpu.VMEM((slides, pairs, 2, cols, chans), BF16),
        in_specs=[hbm] * 13,
        out_specs=vmem,
        scratch_shapes=[
            *[pltpu.VMEM((slides, pairs, 2, cols, chans), BF16)] * 2,
            pltpu.VMEM(tissue_list.shape, jnp.int32),
            pltpu.SMEM(tissue_count.shape, jnp.int32),
            pltpu.VMEM(inner_gain.shape, BF16),
            pltpu.VMEM(inner_bias.shape, BF16),
            pltpu.VMEM(outer_gain.shape, BF16),
            pltpu.VMEM(outer_bias.shape, BF16),
            pltpu.VMEM((2, chans, inner), BF16),
            pltpu.VMEM((2, 3, 3, inner, inner), BF16),
            *[pltpu.VMEM((2, 6 * inner, 2 * inner), BF16)] * 4,
            pltpu.VMEM((2, inner, chans), BF16),
            pltpu.VMEM((2, 16, inner), F32),
            pltpu.VMEM((slides, cols // TW + 2, 8, inner), F32),
            pltpu.VMEM((2, slides, pairs + 1, cols, 6 * inner), BF16),
            *[pltpu.VMEM((2, 2, slides, cols, inner), BF16)] * 2,
            *[pltpu.VMEM(x.shape, BF16) for x in picks],
            *[pltpu.VMEM((2, slides, 16, chans), BF16)] * 4,
            *[pltpu.VMEM((2, 2, 2, 16, chans), BF16)] * 2,
            pltpu.VMEM((2 * slides, pairs, 2, 16, chans), BF16),
            pltpu.SemaphoreType.REGULAR,
            pltpu.SemaphoreType.REGULAR,
            dma((slides,)),
            dma((12,)),
            dma((8,)),
            dma((8,)),
            dma((4,)),
            dma((4,)),
            dma((2, 2)),
            dma((2, 2)),
        ],
        compiler_params=pltpu.CompilerParams(
            collective_id=0, has_side_effects=True, vmem_limit_bytes=40 * 2**20
        ),
        name="blocks",
    )(
        *(
            pltpu.with_memory_space_constraint(x, pltpu.HBM)
            for x in (
                images.reshape(total, pairs, 2, cols, chans),
                tissue_list,
                tissue_count,
                w_reduce,
                w_spatial,
                w_expand,
                inner_gain,
                inner_bias,
                outer_gain,
                outer_bias,
                *picks,
            )
        )
    )
    out = pl.pallas_call(
        write_kernel,
        out_shape=jax.ShapeDtypeStruct((slides, pairs, 2, cols, chans), BF16),
        in_specs=[vmem],
        out_specs=hbm,
        scratch_shapes=[dma((slides,))],
        compiler_params=pltpu.CompilerParams(vmem_limit_bytes=16 * 2**20),
        name="write",
    )(held)
    return out.reshape(slides, rows, cols, chans)


def solution(mesh):
    placed = (
        P(None, "row", "col", None),
        P(),
        P(),
        P("segment", None, None),
        P("segment", None, None, None, None),
        P("segment", None, None),
        P("segment", None, None),
        P("segment", None, None),
        P("segment", None),
        P("segment", None),
    )
    return jax.shard_map(
        functools.partial(shards, (mesh.shape["row"], mesh.shape["col"])),
        mesh=mesh,
        in_specs=placed,
        out_specs=P("segment", "row", "col", None),
        check_vma=False,
    )
```

```python
import functools

import jax
import jax.numpy as jnp
import ml_dtypes
import numpy as np
from jax import lax
from jax.experimental import pallas as pl
from jax.experimental.pallas import tpu as pltpu
from jax.sharding import PartitionSpec as P

MESH = pl.DeviceIdType.MESH
TW = 64
F32 = jnp.float32
BF16 = jnp.bfloat16
remote = pltpu.make_async_remote_copy


RUN = 8


def selections(rows):
    gather = np.zeros((2, 48, 128), np.float32)
    window = np.zeros((2, 2, 96, 256), np.float32)
    scatter = np.zeros((6, 128, 128), np.float32)
    for side in range(2):
        own = [12 * side + q for q in range(4)]
        outer = own[2:] if side else own[:2]
        for q in range(2):
            for r in range(rows):
                gather[side, q * 8 + r, r * 16 + outer[q]] = 1
            for t in range(2):
                gather[side, 32 + q * 2 + t, t * 16 + outer[q]] = 1
                gather[side, 40 + q * 2 + t, (rows - 2 + t) * 16 + outer[q]] = 1
        for q in range(4):
            for t in range(2):
                gather[side, 16 + q * 2 + t, t * 16 + own[q]] = 1
                gather[side, 24 + q * 2 + t, (rows - 2 + t) * 16 + own[q]] = 1
        for half in range(2):
            to = window[side, half]
            for q in range(4):
                w = (q if side else q + 2) * 16
                for r in range(rows):
                    to[w + r, r * 16 + own[q]] = 1
                for t in range(2):
                    to[w + 8 + t, 160 + side * 8 + q * 2 + t] = 1
                    to[w + 14 + t, 144 + side * 8 + q * 2 + t] = 1
            for q in range(2):
                w = (q + 4 if side else q) * 16
                for r in range(rows):
                    to[w + r, 128 + q * 8 + r] = 1
                for t in range(2):
                    to[w + 8 + t, 192 + half * 8 + q * 2 + t] = 1
                    to[w + 14 + t, 176 + half * 8 + q * 2 + t] = 1
        for s in range(3):
            strip = s * 2 + side
            for q in range(2):
                for r in range(rows):
                    scatter[strip, r * 16 + 14 * side + q, strip * 16 + q * 8 + r] = 1
    window = window.reshape(4, 96, 2, 128).swapaxes(1, 2)
    window = window.reshape(8, 96, 128)
    return [x.astype(ml_dtypes.bfloat16) for x in (gather, window, scatter)]


def widen(row, times):
    return jnp.concatenate([row] * times, axis=1)


def inside(i, n):
    return (i >= 0) & (i < n)


def blocks_kernel(
    grid,
    images,
    tissue_list,
    tissue_count,
    w_reduce,
    w_spatial,
    w_expand,
    inner_gain,
    inner_bias,
    outer_gain,
    outer_bias,
    gather_in,
    window_in,
    scatter_in,
    out,
    img,
    mid,
    listed,
    counts,
    ig,
    ib,
    og,
    ob,
    wr,
    ws,
    wa,
    wb,
    wat,
    wbt,
    we,
    gb,
    mk,
    rb,
    row_send,
    row_recv,
    gather,
    window,
    scatter,
    col_send,
    col_recv,
    lines_send,
    lines_recv,
    diag_send,
    diag_recv,
    fixed,
    rows_ready,
    cols_ready,
    img_sem,
    w_sem,
    edge_send_sem,
    edge_recv_sem,
    w_send_sem,
    w_recv_sem,
    send_sem,
    recv_sem,
):
    n_row, n_col = grid
    slides, pairs, _, cols, chans = img.shape
    inner = wr.shape[2]
    last = cols - 1
    seg = lax.axis_index("segment")
    row = lax.axis_index("row")
    col = lax.axis_index("col")
    peer = {"segment": 1 - seg}
    around = [
        (i, j, inside(row + i, n_row) & inside(col + j, n_col))
        for j in (0, -1, 1)
        for i in (-1, 1, 0)
        if i or j
    ]

    def at(i, j):
        return {"row": row + i, "col": col + j}

    barrier = pltpu.get_barrier_semaphore()

    def greet(other):
        pl.semaphore_signal(barrier, inc=1, device_id=other, device_id_type=MESH)

    pl.when(seg == 0)(functools.partial(greet, peer))
    for i, j, there in around:
        core = 1 if j == 0 else 0
        pl.when(there)(functools.partial(greet, {"segment": core, **at(i, j)}))

    def meet(core, count, ready):
        @pl.when(seg == core)
        def _():
            pl.semaphore_wait(barrier, count)
            pl.semaphore_signal(ready, inc=1, device_id=peer, device_id_type=MESH)

        @pl.when(seg != core)
        def _():
            pl.semaphore_wait(ready, 1)

    def number(pick):
        return sum((there.astype(jnp.int32) for _, j, there in around if pick(j)), 0)

    def image_load(s):
        return pltpu.make_async_copy(images.at[seg * slides + s], img.at[s], img_sem.at[s])

    own = [
        pltpu.make_async_copy(src, dst, w_sem.at[i])
        for i, (src, dst) in enumerate(
            (
                (w_reduce.at[0], wr.at[seg]),
                (w_spatial.at[0], ws.at[seg]),
                (w_expand.at[0], we.at[seg]),
                (inner_gain, ig),
                (inner_bias, ib),
                (outer_gain, og),
                (outer_bias, ob),
                (tissue_count, counts),
                (tissue_list, listed),
                (gather_in, gather),
                (window_in, window),
                (scatter_in, scatter),
            )
        )
    ]
    for load in own[3:9] + own[:1]:
        load.start()
    for s in range(slides):
        image_load(s).start()
    for load in own[1:3] + own[9:]:
        load.start()
    for load in own[3:9]:
        load.wait()

    lines = [ig[0].astype(F32), ib[0].astype(F32)]
    for whole in (og[...].astype(F32), ob[...].astype(F32)):
        lines += [whole[:, i * inner : (i + 1) * inner] for i in range(chans // inner)]
    lines.append(jnp.zeros((4, inner), F32))
    gb[seg] = jnp.concatenate(lines, axis=0)

    position = lax.broadcasted_iota(jnp.int32, (1, listed.shape[1]), 1)
    for s in range(slides):
        slide = seg * slides + s
        here = listed[pl.ds(slide, 1), :]
        for t in range(cols // TW + 2):
            tile = col * (cols // TW) + t - 1
            hit = (here == tile) & (position < counts[slide])
            one = jnp.max(jnp.where(hit, 1.0, 0.0), axis=1, keepdims=True)
            mk[s, t] = jnp.broadcast_to(one, mk.shape[2:])

    meet(1, 1 + 2 * number(lambda j: j == 0), rows_ready)

    def swap(src, dst, i):
        return remote(
            src_ref=src,
            dst_ref=dst.at[seg],
            send_sem=w_send_sem.at[i],
            recv_sem=w_recv_sem.at[i],
            device_id=peer,
            device_id_type=MESH,
        )

    swaps = [
        swap(w_reduce.at[0], wr, 0),
        swap(gb.at[seg], gb, 1),
        swap(w_spatial.at[0], ws, 2),
        swap(w_expand.at[0], we, 3),
    ]
    for copy in swaps:
        copy.start()

    def row_sends(e):
        for n, (i, j, there) in enumerate(around[:2]):
            yield there, remote(
                src_ref=row_send.at[e, n],
                dst_ref=row_recv.at[e, 1 - n],
                send_sem=send_sem.at[e, n],
                recv_sem=recv_sem.at[e, 1 - n],
                device_id=at(i, j),
                device_id_type=MESH,
            )

    def edge_sends():
        for n, (i, j, there) in enumerate(around):
            a, b = (1 + i) // 2, (1 + j) // 2
            if j == 0:
                src, dst, here = lines_send.at[a], lines_recv.at[1 - a], lines_recv.at[a]
            elif i == 0:
                src, dst, here = col_send.at[b], col_recv.at[1 - b], col_recv.at[b]
            else:
                src, dst = diag_send.at[a, b], diag_recv.at[1 - a, 1 - b]
                here = diag_recv.at[a, b]
            copy = remote(
                src_ref=src,
                dst_ref=dst,
                send_sem=edge_send_sem.at[n],
                recv_sem=edge_recv_sem.at[mirror(n)],
                device_id=at(i, j),
                device_id_type=MESH,
            )
            yield there, copy, here

    def mirror(n):
        i, j, _ = around[n]
        return [(a, b) for a, b, _ in around].index((-i, -j))

    def place_row(e, r, red):
        lane = (r + 1) % 2 * 3 * inner
        rb[e, :, (r + 1) // 2, :, lane : lane + 3 * inner] = jnp.concatenate(
            [
                pltpu.roll(red, 1, 1).astype(BF16),
                red.astype(BF16),
                pltpu.roll(red, last, 1).astype(BF16),
            ],
            axis=2,
        )

    def reduce_pair(e, x, p):
        v = jnp.dot(x.reshape(-1, chans), wr[e], preferred_element_type=F32)
        v = v.reshape(slides, 2, cols // TW, TW, inner)
        mask = mk[:, 1 : 1 + cols // TW, 0:1][:, None]
        red = jnp.maximum(v * (gb[e, 0:1] * mask) + gb[e, 2:3] * mask, 0.0)
        return red.reshape(slides, 2, cols, inner)

    def send_row(e, way, red):
        row_send[e, way] = red[:, way].astype(BF16)
        there, copy = list(row_sends(e))[way]
        pl.when(there)(copy.start)

    def halo(e):
        copies = list(row_sends(e))
        for n, (there, _) in enumerate(copies):
            pl.when(there)(copies[1 - n][1].wait_recv)
        for way, there, r in ((0, row > 0, -1), (1, row < n_row - 1, 2 * pairs)):
            place_row(e, r, jnp.where(there, row_recv[e, way].astype(F32), 0.0))

    def spatial_part(e, p, w, i):
        return jnp.dot(rb[e, :, p + i].reshape(-1, 6 * inner), w[e], preferred_element_type=F32)

    def spatial(e, p, first=None, second=None):
        first = spatial_part(e, p, wa, 0) if first is None else first
        second = spatial_part(e, p, wb, 1) if second is None else second
        gain, bias = widen(gb[e, 1:2], 2), widen(gb[e, 3:4], 2)
        return jnp.maximum((first + second) * gain + bias, 0.0).astype(BF16)

    def expand(e, sp, p, before, after):
        gain, bias = outer(e)
        mask = mk[:, 1 : 1 + cols // TW, 0:1]
        mask = jnp.concatenate([mask] * (chans // inner), axis=3)
        for half in range(2):
            z = jnp.dot(
                sp[:, half * inner : (half + 1) * inner], we[e], preferred_element_type=F32
            ).reshape(slides, cols, chans)
            y = jnp.maximum(z * gain + bias + before[:, p, half].astype(F32), 0.0)
            y = y.reshape(slides, cols // TW, TW, chans) * mask
            after[:, p, half] = y.reshape(slides, cols, chans).astype(BF16)

    def spread(b):
        depth = 3 * inner
        zero = jnp.zeros((depth, inner), BF16)
        for w, first, second in (
            ([ws[b, i].reshape(depth, inner) for i in range(3)], wa, wb),
            ([ws[b, :, i].reshape(depth, inner) for i in range(3)], wat, wbt),
        ):
            first[b] = jnp.concatenate(
                [jnp.concatenate([w[0], zero], axis=1), jnp.concatenate([w[1], w[0]], axis=1)],
                axis=0,
            )
            second[b] = jnp.concatenate(
                [jnp.concatenate([w[2], w[1]], axis=1), jnp.concatenate([zero, w[2]], axis=1)],
                axis=0,
            )

    def outer(b):
        n = chans // inner
        gain = jnp.concatenate([gb[b, 4 + i : 5 + i] for i in range(n)], axis=1)
        bias = jnp.concatenate([gb[b, 4 + n + i : 5 + n + i] for i in range(n)], axis=1)
        return gain, bias

    def edge_pixels(s, side):
        cells = img[s, :, :, side * (cols - 16) : side * (cols - 16) + 16]
        return cells.reshape(2 * pairs * 16, chans)

    def send_edges():
        meet(0, 2 * number(lambda j: j != 0), cols_ready)
        parts = []
        for s in range(slides):
            parts.append(
                [
                    jnp.dot(gather[side], edge_pixels(s, side), preferred_element_type=F32)
                    for side in range(2)
                ]
            )
            for side in range(2):
                col_send[side, s] = parts[s][side][0:16].astype(BF16)
            for way in range(2):
                cut = slice(16 + 8 * way, 24 + 8 * way)
                lines_send[way, s] = jnp.concatenate(
                    [parts[s][0][cut], parts[s][1][cut]], axis=0
                ).astype(BF16)
        for way in range(2):
            cut = slice(32 + 8 * way, 40 + 8 * way)
            for side in range(2):
                for t in range(2):
                    two = [parts[min(2 * t + i, slides - 1)][side][cut] for i in range(2)]
                    diag_send[way, side, t] = jnp.concatenate(two, axis=0).astype(BF16)
        for there, copy, _ in edge_sends():
            pl.when(there)(copy.start)

    def edge_wait():
        copies = list(edge_sends())
        for n, (there, _, here) in enumerate(copies):
            pl.when(there)(copies[mirror(n)][1].wait_recv)

            @pl.when(jnp.logical_not(there))
            def _():
                here[...] = jnp.zeros_like(here)

    def edge_strips():
        strips = 2 * slides
        own_row = lax.broadcasted_iota(jnp.int32, (16, inner), 0)
        valid = jnp.where(
            own_row < 8,
            1.0,
            jnp.where(
                own_row < 14,
                jnp.where(row < n_row - 1, 1.0, 0.0),
                jnp.where(row > 0, 1.0, 0.0),
            ),
        )
        cells, masks = [], []
        for s in range(slides):
            for side in range(2):
                mine = edge_pixels(s, side)
                source = jnp.concatenate(
                    [
                        mine,
                        col_recv[side, s],
                        lines_recv[0, s],
                        lines_recv[1, s],
                        diag_recv[0, side, s // 2],
                        diag_recv[1, side, s // 2],
                        mine[0:48],
                    ],
                    axis=0,
                )
                k = 4 * side + 2 * (s % 2)
                pick = jnp.concatenate([window[k], window[k + 1]], axis=1)
                got = jnp.dot(pick, source, preferred_element_type=F32)
                cells.append(got.astype(BF16).reshape(1, 6, 16, chans))
                tiles = (2, 2, 2, 2, 3, 3) if side else (0, 0, 1, 1, 1, 1)
                masks.append([mk[s, t, 0:1] for t in tiles])
        x = jnp.concatenate(cells, axis=0)

        def mask_of(columns):
            return jnp.concatenate(
                [jnp.stack([m[w] * valid for w in columns])[None] for m in masks], axis=0
            )

        def reduced(e, x, columns):
            n = len(columns)
            v = jnp.dot(x.reshape(-1, chans), wr[e], preferred_element_type=F32)
            v = jnp.maximum(v * gb[e, 0:1] + gb[e, 2:3], 0.0)
            v = v.reshape(strips, n, 16, inner) * mask_of(columns)
            flat = v.reshape(strips * n, 16, inner)
            return jnp.concatenate(
                [
                    pltpu.roll(flat, 1, 1).astype(BF16),
                    flat.astype(BF16),
                    pltpu.roll(flat, 15, 1).astype(BF16),
                ],
                axis=2,
            ).reshape(strips, n, 16, 3 * inner)

        def conv(e, first, second):
            total = jnp.dot(first, wat[e], preferred_element_type=F32)
            total += jnp.dot(second, wbt[e], preferred_element_type=F32)
            gain, bias = widen(gb[e, 1:2], 2), widen(gb[e, 3:4], 2)
            return jnp.maximum(total * gain + bias, 0.0)

        def expanded(e, sp, h, mask):
            gain, bias = outer(e)
            z = jnp.dot(sp, we[e], preferred_element_type=F32).reshape(h.shape)
            z = jnp.maximum(z * gain + bias + h.astype(F32), 0.0)
            return z * mask

        r = reduced(0, x, range(6))
        two = [jnp.concatenate([r[:, 2 * i], r[:, 2 * i + 1]], axis=2)[:, None] for i in range(3)]
        sp = conv(
            0,
            jnp.concatenate(two[0:2], axis=1).reshape(-1, 6 * inner),
            jnp.concatenate(two[1:3], axis=1).reshape(-1, 6 * inner),
        ).astype(BF16)
        h, red = [], []
        for half in range(2):
            columns = (1 + half, 3 + half)
            before = jnp.concatenate([x[:, w][:, None] for w in columns], axis=1)
            mask = jnp.concatenate(
                [
                    jnp.stack([jnp.broadcast_to(widen(m[w], chans // inner), (16, chans)) for w in columns])[None]
                    for m in masks
                ],
                axis=0,
            )
            now = expanded(0, sp[:, half * inner : (half + 1) * inner], before, mask)
            h.append(now)
            red.append(reduced(1, now.astype(BF16), columns))
        first, second = (
            jnp.concatenate([red[0][:, i], red[1][:, i]], axis=2).reshape(-1, 6 * inner)
            for i in range(2)
        )
        sp = conv(1, first, second).reshape(strips, 16, 2 * inner)[:, 0:8]
        done = []
        for half in range(2):
            now = h[1 - half][:, half, 0:8].astype(BF16)
            mask = jnp.concatenate([widen(m[2 + half], chans // inner)[None] for m in masks], axis=0)
            z = sp[:, :, half * inner : (half + 1) * inner].reshape(strips * 8, inner)
            done.append(expanded(1, z.astype(BF16), now, mask)[:, None])
        done = jnp.concatenate(done, axis=1).reshape(strips * 16, chans).astype(BF16)
        done = jnp.concatenate([done, jnp.zeros((128 - strips * 16, chans), BF16)], axis=0)
        for i in range(strips):
            put = jnp.dot(scatter[i], done, preferred_element_type=F32).reshape(pairs, 2, 16, chans)
            fixed[i] = put.astype(BF16)

    turn = lax.rem(col, RUN)
    late, soon = turn == 0, turn == RUN - 1
    for load in own[9:]:
        load.wait()
    for s in range(slides):
        image_load(s).wait()
    pl.when(soon)(send_edges)

    own[0].wait()
    for copy in swaps[:2]:
        copy.wait()
    ends = (0, pairs - 1)
    between = tuple(range(1, pairs - 1))

    def place_pairs(e, group, reds):
        for p, red in zip(group, reds):
            for half in range(2):
                place_row(e, 2 * p + half, red[:, half])

    def reduce_ends(e, x):
        reds = [reduce_pair(e, x[:, p], p) for p in ends]
        for way in range(2):
            send_row(e, way, reds[way])
        place_pairs(e, ends, reds)

    def reduce_between(e, x):
        place_pairs(e, between, [reduce_pair(e, x[:, p], p) for p in between])

    reduce_ends(0, img)
    reduce_between(0, img)

    for load in own[1:3]:
        load.wait()
    for copy in swaps[2:]:
        copy.wait()
    spread(0)
    spread(1)

    def expand_pairs(e, group, before, after):
        parts = [spatial(e, p) for p in group]
        for p, sp in zip(group, parts):
            expand(e, sp, p, before, after)

    def expand_ends(e, before, after):
        top, bottom = ends
        below = spatial_part(e, top, wb, 1)
        above = spatial_part(e, bottom, wa, 0)
        halo(e)
        parts = [spatial(e, top, second=below), spatial(e, bottom, first=above)]
        for p, sp in zip(ends, parts):
            expand(e, sp, p, before, after)

    expand_pairs(0, between, img, mid)
    pl.when((turn > 0) & (turn < RUN - 1))(send_edges)
    reduce_between(1, mid)
    expand_ends(0, img, mid)
    reduce_ends(1, mid)
    pl.when(late)(send_edges)
    expand_pairs(1, between, mid, out)

    @pl.when(turn > 1)
    def _():
        edge_wait()
        edge_strips()

    expand_ends(1, mid, out)

    @pl.when(turn <= 1)
    def _():
        edge_wait()
        edge_strips()

    for i in range(2 * slides):
        place = lax.broadcasted_iota(jnp.int32, (pairs, 2, 16, chans), 2)
        here = out.at[i // 2, :, :, i % 2 * (cols - 16) : i % 2 * (cols - 16) + 16]
        edges = place >= 14 if i % 2 else place < 2
        here[...] = jnp.where(edges, fixed[i].astype(F32), here[...].astype(F32)).astype(BF16)
    for there, copy, _ in edge_sends():
        pl.when(there)(copy.wait_send)

    for e in range(2):
        for there, copy in row_sends(e):
            pl.when(there)(copy.wait_send)


def write_kernel(held, out, sem):
    copies = [pltpu.make_async_copy(held.at[s], out.at[s], sem.at[s]) for s in range(held.shape[0])]
    for copy in copies:
        copy.start()
    for copy in copies:
        copy.wait()


def shards(grid, images, tissue_list, tissue_count, *weights):
    total, rows, cols, chans = images.shape
    slides, pairs = total // 2, rows // 2
    inner = weights[0].shape[2]
    w_reduce, w_spatial, w_expand, inner_gain, inner_bias, outer_gain, outer_bias = weights
    w_spatial = w_spatial.reshape(1, 3, 3, inner, inner)
    picks = [jnp.asarray(x) for x in selections(rows)]
    hbm = pl.BlockSpec(memory_space=pltpu.HBM)
    vmem = pl.BlockSpec(memory_space=pltpu.VMEM)
    dma = pltpu.SemaphoreType.DMA
    held = pl.pallas_call(
        functools.partial(blocks_kernel, grid),
        out_shape=pltpu.VMEM((slides, pairs, 2, cols, chans), BF16),
        in_specs=[hbm] * 13,
        out_specs=vmem,
        scratch_shapes=[
            *[pltpu.VMEM((slides, pairs, 2, cols, chans), BF16)] * 2,
            pltpu.VMEM(tissue_list.shape, jnp.int32),
            pltpu.SMEM(tissue_count.shape, jnp.int32),
            pltpu.VMEM(inner_gain.shape, BF16),
            pltpu.VMEM(inner_bias.shape, BF16),
            pltpu.VMEM(outer_gain.shape, BF16),
            pltpu.VMEM(outer_bias.shape, BF16),
            pltpu.VMEM((2, chans, inner), BF16),
            pltpu.VMEM((2, 3, 3, inner, inner), BF16),
            *[pltpu.VMEM((2, 6 * inner, 2 * inner), BF16)] * 4,
            pltpu.VMEM((2, inner, chans), BF16),
            pltpu.VMEM((2, 16, inner), F32),
            pltpu.VMEM((slides, cols // TW + 2, 8, inner), F32),
            pltpu.VMEM((2, slides, pairs + 1, cols, 6 * inner), BF16),
            *[pltpu.VMEM((2, 2, slides, cols, inner), BF16)] * 2,
            *[pltpu.VMEM(x.shape, BF16) for x in picks],
            *[pltpu.VMEM((2, slides, 16, chans), BF16)] * 4,
            *[pltpu.VMEM((2, 2, 2, 16, chans), BF16)] * 2,
            pltpu.VMEM((2 * slides, pairs, 2, 16, chans), BF16),
            pltpu.SemaphoreType.REGULAR,
            pltpu.SemaphoreType.REGULAR,
            dma((slides,)),
            dma((12,)),
            dma((8,)),
            dma((8,)),
            dma((4,)),
            dma((4,)),
            dma((2, 2)),
            dma((2, 2)),
        ],
        compiler_params=pltpu.CompilerParams(
            collective_id=0, has_side_effects=True, vmem_limit_bytes=40 * 2**20
        ),
        name="blocks",
    )(
        *(
            pltpu.with_memory_space_constraint(x, pltpu.HBM)
            for x in (
                images.reshape(total, pairs, 2, cols, chans),
                tissue_list,
                tissue_count,
                w_reduce,
                w_spatial,
                w_expand,
                inner_gain,
                inner_bias,
                outer_gain,
                outer_bias,
                *picks,
            )
        )
    )
    out = pl.pallas_call(
        write_kernel,
        out_shape=jax.ShapeDtypeStruct((slides, pairs, 2, cols, chans), BF16),
        in_specs=[vmem],
        out_specs=hbm,
        scratch_shapes=[dma((slides,))],
        compiler_params=pltpu.CompilerParams(vmem_limit_bytes=16 * 2**20),
        name="write",
    )(held)
    return out.reshape(slides, rows, cols, chans)


def solution(mesh):
    placed = (
        P(None, "row", "col", None),
        P(),
        P(),
        P("segment", None, None),
        P("segment", None, None, None, None),
        P("segment", None, None),
        P("segment", None, None),
        P("segment", None, None),
        P("segment", None),
        P("segment", None),
    )
    return jax.shard_map(
        functools.partial(shards, (mesh.shape["row"], mesh.shape["col"])),
        mesh=mesh,
        in_specs=placed,
        out_specs=P("segment", "row", "col", None),
        check_vma=False,
    )
```

```python
import functools

import jax
import jax.numpy as jnp
import ml_dtypes
import numpy as np
from jax import lax
from jax.experimental import pallas as pl
from jax.experimental.pallas import tpu as pltpu
from jax.sharding import PartitionSpec as P

MESH = pl.DeviceIdType.MESH
TW = 64
F32 = jnp.float32
BF16 = jnp.bfloat16
remote = pltpu.make_async_remote_copy


RUN = 8


def selections(rows):
    gather = np.zeros((2, 48, 128), np.float32)
    window = np.zeros((2, 2, 96, 256), np.float32)
    scatter = np.zeros((6, 128, 128), np.float32)
    for side in range(2):
        own = [12 * side + q for q in range(4)]
        outer = own[2:] if side else own[:2]
        for q in range(2):
            for r in range(rows):
                gather[side, q * 8 + r, r * 16 + outer[q]] = 1
            for t in range(2):
                gather[side, 32 + q * 2 + t, t * 16 + outer[q]] = 1
                gather[side, 40 + q * 2 + t, (rows - 2 + t) * 16 + outer[q]] = 1
        for q in range(4):
            for t in range(2):
                gather[side, 16 + q * 2 + t, t * 16 + own[q]] = 1
                gather[side, 24 + q * 2 + t, (rows - 2 + t) * 16 + own[q]] = 1
        for half in range(2):
            to = window[side, half]
            for q in range(4):
                w = (q if side else q + 2) * 16
                for r in range(rows):
                    to[w + r, r * 16 + own[q]] = 1
                for t in range(2):
                    to[w + 8 + t, 160 + side * 8 + q * 2 + t] = 1
                    to[w + 14 + t, 144 + side * 8 + q * 2 + t] = 1
            for q in range(2):
                w = (q + 4 if side else q) * 16
                for r in range(rows):
                    to[w + r, 128 + q * 8 + r] = 1
                for t in range(2):
                    to[w + 8 + t, 192 + half * 8 + q * 2 + t] = 1
                    to[w + 14 + t, 176 + half * 8 + q * 2 + t] = 1
        for s in range(3):
            strip = s * 2 + side
            for q in range(2):
                for r in range(rows):
                    scatter[strip, r * 16 + 14 * side + q, strip * 16 + q * 8 + r] = 1
    window = window.reshape(4, 96, 2, 128).swapaxes(1, 2)
    window = window.reshape(8, 96, 128)
    return [x.astype(ml_dtypes.bfloat16) for x in (gather, window, scatter)]


def widen(row, times):
    return jnp.concatenate([row] * times, axis=1)


def inside(i, n):
    return (i >= 0) & (i < n)


def blocks_kernel(
    grid,
    images,
    tissue_list,
    tissue_count,
    w_reduce,
    w_spatial,
    w_expand,
    inner_gain,
    inner_bias,
    outer_gain,
    outer_bias,
    gather_in,
    window_in,
    scatter_in,
    out,
    img,
    mid,
    listed,
    counts,
    ig,
    ib,
    og,
    ob,
    wr,
    ws,
    wa,
    wb,
    wat,
    wbt,
    we,
    gb,
    mk,
    rb,
    row_send,
    row_recv,
    gather,
    window,
    scatter,
    col_send,
    col_recv,
    lines_send,
    lines_recv,
    diag_send,
    diag_recv,
    fixed,
    rows_ready,
    cols_ready,
    img_sem,
    w_sem,
    edge_send_sem,
    edge_recv_sem,
    w_send_sem,
    w_recv_sem,
    send_sem,
    recv_sem,
):
    n_row, n_col = grid
    slides, pairs, _, cols, chans = img.shape
    inner = wr.shape[2]
    last = cols - 1
    seg = lax.axis_index("segment")
    row = lax.axis_index("row")
    col = lax.axis_index("col")
    peer = {"segment": 1 - seg}
    around = [
        (i, j, inside(row + i, n_row) & inside(col + j, n_col))
        for j in (0, -1, 1)
        for i in (-1, 1, 0)
        if i or j
    ]

    def at(i, j):
        return {"row": row + i, "col": col + j}

    barrier = pltpu.get_barrier_semaphore()

    def greet(other):
        pl.semaphore_signal(barrier, inc=1, device_id=other, device_id_type=MESH)

    pl.when(seg == 0)(functools.partial(greet, peer))
    for i, j, there in around:
        core = 1 if j == 0 else 0
        pl.when(there)(functools.partial(greet, {"segment": core, **at(i, j)}))

    def meet(core, count, ready):
        @pl.when(seg == core)
        def _():
            pl.semaphore_wait(barrier, count)
            pl.semaphore_signal(ready, inc=1, device_id=peer, device_id_type=MESH)

        @pl.when(seg != core)
        def _():
            pl.semaphore_wait(ready, 1)

    def number(pick):
        return sum((there.astype(jnp.int32) for _, j, there in around if pick(j)), 0)

    def image_load(s):
        return pltpu.make_async_copy(images.at[seg * slides + s], img.at[s], img_sem.at[s])

    own = [
        pltpu.make_async_copy(src, dst, w_sem.at[i])
        for i, (src, dst) in enumerate(
            (
                (w_reduce.at[0], wr.at[seg]),
                (w_spatial.at[0], ws.at[seg]),
                (w_expand.at[0], we.at[seg]),
                (inner_gain, ig),
                (inner_bias, ib),
                (outer_gain, og),
                (outer_bias, ob),
                (tissue_count, counts),
                (tissue_list, listed),
                (gather_in, gather),
                (window_in, window),
                (scatter_in, scatter),
            )
        )
    ]
    for load in own[3:9] + own[:1]:
        load.start()
    for s in range(slides):
        image_load(s).start()
    for load in own[1:3] + own[9:]:
        load.start()
    for load in own[3:9]:
        load.wait()

    lines = [ig[0].astype(F32), ib[0].astype(F32)]
    for whole in (og[...].astype(F32), ob[...].astype(F32)):
        lines += [whole[:, i * inner : (i + 1) * inner] for i in range(chans // inner)]
    lines.append(jnp.zeros((4, inner), F32))
    gb[seg] = jnp.concatenate(lines, axis=0)

    position = lax.broadcasted_iota(jnp.int32, (1, listed.shape[1]), 1)
    for s in range(slides):
        slide = seg * slides + s
        here = listed[pl.ds(slide, 1), :]
        for t in range(cols // TW + 2):
            tile = col * (cols // TW) + t - 1
            hit = (here == tile) & (position < counts[slide])
            one = jnp.max(jnp.where(hit, 1.0, 0.0), axis=1, keepdims=True)
            mk[s, t] = jnp.broadcast_to(one, mk.shape[2:])

    meet(1, 1 + 2 * number(lambda j: j == 0), rows_ready)

    def swap(src, dst, i):
        return remote(
            src_ref=src,
            dst_ref=dst.at[seg],
            send_sem=w_send_sem.at[i],
            recv_sem=w_recv_sem.at[i],
            device_id=peer,
            device_id_type=MESH,
        )

    swaps = [
        swap(w_reduce.at[0], wr, 0),
        swap(gb.at[seg], gb, 1),
        swap(w_spatial.at[0], ws, 2),
        swap(w_expand.at[0], we, 3),
    ]
    for copy in swaps:
        copy.start()

    def row_sends(e):
        for n, (i, j, there) in enumerate(around[:2]):
            yield there, remote(
                src_ref=row_send.at[e, n],
                dst_ref=row_recv.at[e, 1 - n],
                send_sem=send_sem.at[e, n],
                recv_sem=recv_sem.at[e, 1 - n],
                device_id=at(i, j),
                device_id_type=MESH,
            )

    def edge_sends():
        for n, (i, j, there) in enumerate(around):
            a, b = (1 + i) // 2, (1 + j) // 2
            if j == 0:
                src, dst, here = lines_send.at[a], lines_recv.at[1 - a], lines_recv.at[a]
            elif i == 0:
                src, dst, here = col_send.at[b], col_recv.at[1 - b], col_recv.at[b]
            else:
                src, dst = diag_send.at[a, b], diag_recv.at[1 - a, 1 - b]
                here = diag_recv.at[a, b]
            copy = remote(
                src_ref=src,
                dst_ref=dst,
                send_sem=edge_send_sem.at[n],
                recv_sem=edge_recv_sem.at[mirror(n)],
                device_id=at(i, j),
                device_id_type=MESH,
            )
            yield there, copy, here

    def mirror(n):
        i, j, _ = around[n]
        return [(a, b) for a, b, _ in around].index((-i, -j))

    def place_row(e, r, red):
        lane = (r + 1) % 2 * 3 * inner
        rb[e, :, (r + 1) // 2, :, lane : lane + 3 * inner] = jnp.concatenate(
            [
                pltpu.roll(red, 1, 1).astype(BF16),
                red.astype(BF16),
                pltpu.roll(red, last, 1).astype(BF16),
            ],
            axis=2,
        )

    def reduce_pair(e, x, p):
        v = jnp.dot(x.reshape(-1, chans), wr[e], preferred_element_type=F32)
        v = v.reshape(slides, 2, cols // TW, TW, inner)
        mask = mk[:, 1 : 1 + cols // TW, 0:1][:, None]
        red = jnp.maximum(v * (gb[e, 0:1] * mask) + gb[e, 2:3] * mask, 0.0)
        return red.reshape(slides, 2, cols, inner)

    def send_row(e, way, red):
        row_send[e, way] = red[:, way].astype(BF16)
        there, copy = list(row_sends(e))[way]
        pl.when(there)(copy.start)

    def halo(e):
        copies = list(row_sends(e))
        for n, (there, _) in enumerate(copies):
            pl.when(there)(copies[1 - n][1].wait_recv)
        for way, there, r in ((0, row > 0, -1), (1, row < n_row - 1, 2 * pairs)):
            place_row(e, r, jnp.where(there, row_recv[e, way].astype(F32), 0.0))

    def spatial_part(e, p, w, i):
        return jnp.dot(rb[e, :, p + i].reshape(-1, 6 * inner), w[e], preferred_element_type=F32)

    def spatial(e, p, first=None, second=None):
        first = spatial_part(e, p, wa, 0) if first is None else first
        second = spatial_part(e, p, wb, 1) if second is None else second
        gain, bias = widen(gb[e, 1:2], 2), widen(gb[e, 3:4], 2)
        return jnp.maximum((first + second) * gain + bias, 0.0).astype(BF16)

    def expand(e, sp, p, before, after):
        gain, bias = outer(e)
        mask = mk[:, 1 : 1 + cols // TW, 0:1]
        mask = jnp.concatenate([mask] * (chans // inner), axis=3)
        for half in range(2):
            z = jnp.dot(
                sp[:, half * inner : (half + 1) * inner], we[e], preferred_element_type=F32
            ).reshape(slides, cols, chans)
            y = jnp.maximum(z * gain + bias + before[:, p, half].astype(F32), 0.0)
            y = y.reshape(slides, cols // TW, TW, chans) * mask
            after[:, p, half] = y.reshape(slides, cols, chans).astype(BF16)

    def spread(b):
        depth = 3 * inner
        zero = jnp.zeros((depth, inner), BF16)
        for w, first, second in (
            ([ws[b, i].reshape(depth, inner) for i in range(3)], wa, wb),
            ([ws[b, :, i].reshape(depth, inner) for i in range(3)], wat, wbt),
        ):
            first[b] = jnp.concatenate(
                [jnp.concatenate([w[0], zero], axis=1), jnp.concatenate([w[1], w[0]], axis=1)],
                axis=0,
            )
            second[b] = jnp.concatenate(
                [jnp.concatenate([w[2], w[1]], axis=1), jnp.concatenate([zero, w[2]], axis=1)],
                axis=0,
            )

    def outer(b):
        n = chans // inner
        gain = jnp.concatenate([gb[b, 4 + i : 5 + i] for i in range(n)], axis=1)
        bias = jnp.concatenate([gb[b, 4 + n + i : 5 + n + i] for i in range(n)], axis=1)
        return gain, bias

    def edge_pixels(s, side):
        cells = img[s, :, :, side * (cols - 16) : side * (cols - 16) + 16]
        return cells.reshape(2 * pairs * 16, chans)

    def gather_edges():
        parts = []
        for s in range(slides):
            parts.append(
                [
                    jnp.dot(gather[side], edge_pixels(s, side), preferred_element_type=F32)
                    for side in range(2)
                ]
            )
            for side in range(2):
                col_send[side, s] = parts[s][side][0:16].astype(BF16)
            for way in range(2):
                cut = slice(16 + 8 * way, 24 + 8 * way)
                lines_send[way, s] = jnp.concatenate(
                    [parts[s][0][cut], parts[s][1][cut]], axis=0
                ).astype(BF16)
        for way in range(2):
            cut = slice(32 + 8 * way, 40 + 8 * way)
            for side in range(2):
                for t in range(2):
                    two = [parts[min(2 * t + i, slides - 1)][side][cut] for i in range(2)]
                    diag_send[way, side, t] = jnp.concatenate(two, axis=0).astype(BF16)

    def send_edges():
        meet(0, 2 * number(lambda j: j != 0), cols_ready)
        for there, copy, _ in edge_sends():
            pl.when(there)(copy.start)

    def edge_wait():
        copies = list(edge_sends())
        for n, (there, _, here) in enumerate(copies):
            pl.when(there)(copies[mirror(n)][1].wait_recv)

            @pl.when(jnp.logical_not(there))
            def _():
                here[...] = jnp.zeros_like(here)

    def edge_strips():
        strips = 2 * slides
        own_row = lax.broadcasted_iota(jnp.int32, (16, inner), 0)
        valid = jnp.where(
            own_row < 8,
            1.0,
            jnp.where(
                own_row < 14,
                jnp.where(row < n_row - 1, 1.0, 0.0),
                jnp.where(row > 0, 1.0, 0.0),
            ),
        )
        cells, masks = [], []
        for s in range(slides):
            for side in range(2):
                mine = edge_pixels(s, side)
                source = jnp.concatenate(
                    [
                        mine,
                        col_recv[side, s],
                        lines_recv[0, s],
                        lines_recv[1, s],
                        diag_recv[0, side, s // 2],
                        diag_recv[1, side, s // 2],
                        mine[0:48],
                    ],
                    axis=0,
                )
                k = 4 * side + 2 * (s % 2)
                pick = jnp.concatenate([window[k], window[k + 1]], axis=1)
                got = jnp.dot(pick, source, preferred_element_type=F32)
                cells.append(got.astype(BF16).reshape(1, 6, 16, chans))
                tiles = (2, 2, 2, 2, 3, 3) if side else (0, 0, 1, 1, 1, 1)
                masks.append([mk[s, t, 0:1] for t in tiles])
        x = jnp.concatenate(cells, axis=0)

        def mask_of(columns):
            return jnp.concatenate(
                [jnp.stack([m[w] * valid for w in columns])[None] for m in masks], axis=0
            )

        def reduced(e, x, columns):
            n = len(columns)
            v = jnp.dot(x.reshape(-1, chans), wr[e], preferred_element_type=F32)
            v = jnp.maximum(v * gb[e, 0:1] + gb[e, 2:3], 0.0)
            v = v.reshape(strips, n, 16, inner) * mask_of(columns)
            flat = v.reshape(strips * n, 16, inner)
            return jnp.concatenate(
                [
                    pltpu.roll(flat, 1, 1).astype(BF16),
                    flat.astype(BF16),
                    pltpu.roll(flat, 15, 1).astype(BF16),
                ],
                axis=2,
            ).reshape(strips, n, 16, 3 * inner)

        def conv(e, first, second):
            total = jnp.dot(first, wat[e], preferred_element_type=F32)
            total += jnp.dot(second, wbt[e], preferred_element_type=F32)
            gain, bias = widen(gb[e, 1:2], 2), widen(gb[e, 3:4], 2)
            return jnp.maximum(total * gain + bias, 0.0)

        def expanded(e, sp, h, mask):
            gain, bias = outer(e)
            z = jnp.dot(sp, we[e], preferred_element_type=F32).reshape(h.shape)
            z = jnp.maximum(z * gain + bias + h.astype(F32), 0.0)
            return z * mask

        r = reduced(0, x, range(6))
        two = [jnp.concatenate([r[:, 2 * i], r[:, 2 * i + 1]], axis=2)[:, None] for i in range(3)]
        sp = conv(
            0,
            jnp.concatenate(two[0:2], axis=1).reshape(-1, 6 * inner),
            jnp.concatenate(two[1:3], axis=1).reshape(-1, 6 * inner),
        ).astype(BF16)
        h, red = [], []
        for half in range(2):
            columns = (1 + half, 3 + half)
            before = jnp.concatenate([x[:, w][:, None] for w in columns], axis=1)
            mask = jnp.concatenate(
                [
                    jnp.stack([jnp.broadcast_to(widen(m[w], chans // inner), (16, chans)) for w in columns])[None]
                    for m in masks
                ],
                axis=0,
            )
            now = expanded(0, sp[:, half * inner : (half + 1) * inner], before, mask)
            h.append(now)
            red.append(reduced(1, now.astype(BF16), columns))
        first, second = (
            jnp.concatenate([red[0][:, i], red[1][:, i]], axis=2).reshape(-1, 6 * inner)
            for i in range(2)
        )
        sp = conv(1, first, second).reshape(strips, 16, 2 * inner)[:, 0:8]
        done = []
        for half in range(2):
            now = h[1 - half][:, half, 0:8].astype(BF16)
            mask = jnp.concatenate([widen(m[2 + half], chans // inner)[None] for m in masks], axis=0)
            z = sp[:, :, half * inner : (half + 1) * inner].reshape(strips * 8, inner)
            done.append(expanded(1, z.astype(BF16), now, mask)[:, None])
        done = jnp.concatenate(done, axis=1).reshape(strips * 16, chans).astype(BF16)
        done = jnp.concatenate([done, jnp.zeros((128 - strips * 16, chans), BF16)], axis=0)
        for i in range(strips):
            put = jnp.dot(scatter[i], done, preferred_element_type=F32).reshape(pairs, 2, 16, chans)
            fixed[i] = put.astype(BF16)

    turn = lax.rem(col, RUN)
    late, soon = turn == 0, turn == RUN - 1
    for load in own[9:]:
        load.wait()
    for s in range(slides):
        image_load(s).wait()
    gather_edges()
    pl.when(soon)(send_edges)

    own[0].wait()
    for copy in swaps[:2]:
        copy.wait()
    ends = (0, pairs - 1)
    between = tuple(range(1, pairs - 1))

    def place_pairs(e, group, reds):
        for p, red in zip(group, reds):
            for half in range(2):
                place_row(e, 2 * p + half, red[:, half])

    def reduce_ends(e, x):
        reds = [reduce_pair(e, x[:, p], p) for p in ends]
        for way in range(2):
            send_row(e, way, reds[way])
        place_pairs(e, ends, reds)

    def reduce_between(e, x):
        place_pairs(e, between, [reduce_pair(e, x[:, p], p) for p in between])

    reduce_ends(0, img)
    reduce_between(0, img)

    for load in own[1:3]:
        load.wait()
    for copy in swaps[2:]:
        copy.wait()
    spread(0)
    spread(1)

    def expand_pairs(e, group, before, after):
        parts = [spatial(e, p) for p in group]
        for p, sp in zip(group, parts):
            expand(e, sp, p, before, after)

    def expand_ends(e, before, after):
        top, bottom = ends
        below = spatial_part(e, top, wb, 1)
        above = spatial_part(e, bottom, wa, 0)
        halo(e)
        parts = [spatial(e, top, second=below), spatial(e, bottom, first=above)]
        for p, sp in zip(ends, parts):
            expand(e, sp, p, before, after)

    expand_pairs(0, between, img, mid)
    pl.when((turn > 0) & (turn < RUN - 1))(send_edges)
    reduce_between(1, mid)
    expand_ends(0, img, mid)
    reduce_ends(1, mid)
    pl.when(late)(send_edges)
    expand_pairs(1, between, mid, out)

    @pl.when(turn > 1)
    def _():
        edge_wait()
        edge_strips()

    expand_ends(1, mid, out)

    @pl.when(turn <= 1)
    def _():
        edge_wait()
        edge_strips()

    for i in range(2 * slides):
        place = lax.broadcasted_iota(jnp.int32, (pairs, 2, 16, chans), 2)
        here = out.at[i // 2, :, :, i % 2 * (cols - 16) : i % 2 * (cols - 16) + 16]
        edges = place >= 14 if i % 2 else place < 2
        here[...] = jnp.where(edges, fixed[i].astype(F32), here[...].astype(F32)).astype(BF16)
    for there, copy, _ in edge_sends():
        pl.when(there)(copy.wait_send)

    for e in range(2):
        for there, copy in row_sends(e):
            pl.when(there)(copy.wait_send)


def write_kernel(held, out, sem):
    copies = [pltpu.make_async_copy(held.at[s], out.at[s], sem.at[s]) for s in range(held.shape[0])]
    for copy in copies:
        copy.start()
    for copy in copies:
        copy.wait()


def shards(grid, images, tissue_list, tissue_count, *weights):
    total, rows, cols, chans = images.shape
    slides, pairs = total // 2, rows // 2
    inner = weights[0].shape[2]
    w_reduce, w_spatial, w_expand, inner_gain, inner_bias, outer_gain, outer_bias = weights
    w_spatial = w_spatial.reshape(1, 3, 3, inner, inner)
    picks = [jnp.asarray(x) for x in selections(rows)]
    hbm = pl.BlockSpec(memory_space=pltpu.HBM)
    vmem = pl.BlockSpec(memory_space=pltpu.VMEM)
    dma = pltpu.SemaphoreType.DMA
    held = pl.pallas_call(
        functools.partial(blocks_kernel, grid),
        out_shape=pltpu.VMEM((slides, pairs, 2, cols, chans), BF16),
        in_specs=[hbm] * 13,
        out_specs=vmem,
        scratch_shapes=[
            *[pltpu.VMEM((slides, pairs, 2, cols, chans), BF16)] * 2,
            pltpu.VMEM(tissue_list.shape, jnp.int32),
            pltpu.SMEM(tissue_count.shape, jnp.int32),
            pltpu.VMEM(inner_gain.shape, BF16),
            pltpu.VMEM(inner_bias.shape, BF16),
            pltpu.VMEM(outer_gain.shape, BF16),
            pltpu.VMEM(outer_bias.shape, BF16),
            pltpu.VMEM((2, chans, inner), BF16),
            pltpu.VMEM((2, 3, 3, inner, inner), BF16),
            *[pltpu.VMEM((2, 6 * inner, 2 * inner), BF16)] * 4,
            pltpu.VMEM((2, inner, chans), BF16),
            pltpu.VMEM((2, 16, inner), F32),
            pltpu.VMEM((slides, cols // TW + 2, 8, inner), F32),
            pltpu.VMEM((2, slides, pairs + 1, cols, 6 * inner), BF16),
            *[pltpu.VMEM((2, 2, slides, cols, inner), BF16)] * 2,
            *[pltpu.VMEM(x.shape, BF16) for x in picks],
            *[pltpu.VMEM((2, slides, 16, chans), BF16)] * 4,
            *[pltpu.VMEM((2, 2, 2, 16, chans), BF16)] * 2,
            pltpu.VMEM((2 * slides, pairs, 2, 16, chans), BF16),
            pltpu.SemaphoreType.REGULAR,
            pltpu.SemaphoreType.REGULAR,
            dma((slides,)),
            dma((12,)),
            dma((8,)),
            dma((8,)),
            dma((4,)),
            dma((4,)),
            dma((2, 2)),
            dma((2, 2)),
        ],
        compiler_params=pltpu.CompilerParams(
            collective_id=0, has_side_effects=True, vmem_limit_bytes=40 * 2**20
        ),
        name="blocks",
    )(
        *(
            pltpu.with_memory_space_constraint(x, pltpu.HBM)
            for x in (
                images.reshape(total, pairs, 2, cols, chans),
                tissue_list,
                tissue_count,
                w_reduce,
                w_spatial,
                w_expand,
                inner_gain,
                inner_bias,
                outer_gain,
                outer_bias,
                *picks,
            )
        )
    )
    out = pl.pallas_call(
        write_kernel,
        out_shape=jax.ShapeDtypeStruct((slides, pairs, 2, cols, chans), BF16),
        in_specs=[vmem],
        out_specs=hbm,
        scratch_shapes=[dma((slides,))],
        compiler_params=pltpu.CompilerParams(vmem_limit_bytes=16 * 2**20),
        name="write",
    )(held)
    return out.reshape(slides, rows, cols, chans)


def solution(mesh):
    placed = (
        P(None, "row", "col", None),
        P(),
        P(),
        P("segment", None, None),
        P("segment", None, None, None, None),
        P("segment", None, None),
        P("segment", None, None),
        P("segment", None, None),
        P("segment", None),
        P("segment", None),
    )
    return jax.shard_map(
        functools.partial(shards, (mesh.shape["row"], mesh.shape["col"])),
        mesh=mesh,
        in_specs=placed,
        out_specs=P("segment", "row", "col", None),
        check_vma=False,
    )
```
